128 devices in a mesh: tp: 8 (over x, core), ep: 16 (over z, y).
Axes of the slice: x: 4, y: 4, z: 4, core: 2. Of those that a mesh axis runs over, the one named last changes fastest.
Arguments:
- hidden: bfloat16 [256, 7168], P(('tp', 'ep')), may hold values from -6 to 6
- queries: bfloat16 [256, 128, 576], P(('tp', 'ep')), may hold values from -1024 to 1024
- cache: bfloat16 [256, 1024, 576], P(('tp', 'ep')), may hold values from -6 to 6
- new_latent: bfloat16 [256, 576], P(('tp', 'ep')), may hold values from -6 to 6
- lengths: int32 [256], P(('tp', 'ep')), may hold values from 1 to 1024, 131072 in all
- w_values: bfloat16 [128, 512, 128], P('tp'), may hold values from -0.25 to 0.25
- w_out: bfloat16 [128, 128, 7168], P('tp', None, 'ep'), may hold values from -0.1875 to 0.1875
- gain_attn: float32 [7168], replicated, may hold values from 0.1 to 1.9
- w_dense_gate: bfloat16 [7168, 18432], P(None, ('tp', 'ep')), may hold values from -0.0625 to 0.0625
- w_dense_up: bfloat16 [7168, 18432], P(None, ('tp', 'ep')), may hold values from -0.0625 to 0.0625
- w_dense_down: bfloat16 [18432, 7168], P(('tp', 'ep')), may hold values from -0.046875 to 0.046875
- gain_moe: float32 [7168], replicated, may hold values from 0.1 to 1.9
- w_router: bfloat16 [7168, 16], replicated, may hold values from -0.0625 to 0.0625
- expert_ids: int32 [256, 8], P(('tp', 'ep')), may hold values from 0 to 15, all different within a row; in each aligned block of 2 rows (0 to 1, 2 to 3, ...) at most 2 rows name the same one
- w_expert_gate: bfloat16 [16, 7168, 2048], P('ep', None, 'tp'), may hold values from -0.0625 to 0.0625
- w_expert_up: bfloat16 [16, 7168, 2048], P('ep', None, 'tp'), may hold values from -0.0625 to 0.0625
- w_expert_down: bfloat16 [16, 2048, 7168], P('ep', 'tp'), may hold values from -0.125 to 0.125
Outputs:
- layer_out: bfloat16 [256, 7168], P(('tp', 'ep'))
The draws below stay inside these ranges and needn't reach their ends.
Inputs may be any that keep to these rules, and one draw needn't show every extreme that they name: Request t attends to its first lengths[t] cached positions and to its new position. `expert_ids`: each row names 8 different experts; in the rows of one device no expert is named by more than 2 rows.
All inputs are finite; a program needn't handle non-finite values. No bound on the sum of `lengths` on one device may be relied on, other than what follows from the above.
Results may differ from the reference program's by a relative error of at most 0.022.
Values may be sent and summed in bfloat16 or wider, within the bound.
A program may use at most 128 MiB of HBM per device.

```python
import math
import jax
import jax.numpy as jnp
import numpy as np
from jax import lax

D = 7168
H = 128
LAT = 512
ROPE = 64
VD = 128
FF = 18432
EH = 2048
TOP = 8
EXPERTS = 16
TOK_DEV = 2
CACHE = 1024
TOKENS = 256
CAP = 2
N_TP = 8


def anchor_rows(key):
    return jnp.clip(jax.random.normal(jax.random.fold_in(key, 101), (TOKENS, ROPE), jnp.float32), -4.0, 4.0)


def draw_cache(key, part):
    anchor = anchor_rows(key)
    key = jax.random.fold_in(key, 1)
    fresh_draw = jnp.clip(jax.random.normal(key, (TOKENS, CACHE, LAT + ROPE), jnp.float32), -6.0, 6.0)
    first_row = jnp.concatenate([fresh_draw[:, 0, :LAT], anchor], axis=1)
    return fresh_draw.at[:, 0, :].set(first_row).astype(jnp.bfloat16)


def draw_new_latent(key, part):
    key = jax.random.fold_in(key, 2)
    key_fresh = jax.random.fold_in(key, 0)
    fresh_draw = jnp.clip(jax.random.normal(key_fresh, (TOKENS, LAT + ROPE), jnp.float32), -6.0, 6.0)
    rope_part = fresh_draw[:, LAT:]
    return jnp.concatenate([fresh_draw[:, :LAT], rope_part], axis=1).astype(jnp.bfloat16)


def draw_queries(key, part):
    key = jax.random.fold_in(key, 3)
    fresh_draw = jnp.clip(jax.random.normal(key, (TOKENS, H, LAT + ROPE), jnp.float32), -6.0, 6.0)
    mixing = 0.0
    token_index = jnp.arange(TOKENS)
    head_index = jnp.arange(H)
    chosen = ((token_index % 5 == 0)[:, None] & (head_index % 16 == 0)[None, :]).astype(jnp.float32) * mixing
    rope_part = fresh_draw[:, :, LAT:] * (1.0 - chosen[:, :, None])
    return jnp.concatenate([fresh_draw[:, :, :LAT], rope_part], axis=2).astype(jnp.bfloat16)


def block_levels(stream_key, shape, cuts, least, top_value):
    level, own = 1.0, jax.random.fold_in(stream_key, 6)
    for position, parts in cuts:
        steps = jnp.exp(jax.random.uniform(jax.random.fold_in(own, position), (parts,), jnp.float32, least / len(cuts), top_value / len(cuts)))
        level = level * jnp.repeat(steps, shape[position] // parts).reshape([-1 if axis == position else 1 for axis in range(len(shape))])
    return level


def profile(amount, total, most, lean):
    portions = [(1 << 20) // math.isqrt(rank ** lean) + 1 for rank in range(2, amount + 1)]
    surplus, holding = total - most - (amount - 1), [1] * (amount - 1)
    while surplus > 0:
        free = [i for i in range(amount - 1) if holding[i] < most]
        mass, remaining = sum([portions[i] for i in free]), surplus
        for i in free:
            addition = min(most - holding[i], max(1, remaining * portions[i] // mass), surplus)
            holding[i] = holding[i] + addition
            surplus = surplus - addition
    return np.array([most] + holding)


def ragged(stream_key, amount, total, bound, skew):
    if amount == 2:
        one = jax.random.randint(stream_key, (), max(1, total - bound), min(bound, total - 1) + 1)
        return jnp.stack([one, total - one])
    tallies = jnp.asarray(profile(amount, total, bound, skew), jnp.int32)
    couples = (amount - 1) // 2
    giver, sink = tallies[1:1 + 2 * couples:2], tallies[2:2 + 2 * couples:2]
    room = jnp.minimum(giver - 1, bound - sink)
    moved = jax.random.randint(jax.random.fold_in(stream_key, 1), (couples,), 0, 1 << 20) % (room + 1)
    tallies = tallies.at[1:1 + 2 * couples:2].set(giver - moved).at[2:2 + 2 * couples:2].set(sink + moved)
    return tallies[jax.random.permutation(jax.random.fold_in(stream_key, 2), amount)]


def routed_block(rng, own, number, rows, count, top, reach, lean):
    sequence = jax.random.permutation(rng, count)
    crowded, usual = shares(count, rows * top, reach, lean, True), shares(count, rows * top, reach, lean, False)
    places = jnp.arange(count)

    def named(tallies, turn):
        used = int((tallies > 0).sum())
        fixed = max(1, used // 4)
        moved = fixed + (places - fixed + turn * (used - fixed)) % max(1, count - fixed)
        return jnp.zeros((count,), jnp.int32).at[sequence[jnp.where(places < fixed, places, moved)]].set(jnp.asarray(tallies, jnp.int32))

    tallies = jnp.where(number % 4 == 0, named(crowded, number // 4), named(usual, number - number // 4 - 1))
    mixed = jax.random.permutation(jax.random.fold_in(own, 3), count)
    source_of, taker = mixed[0:count // 2 * 2:2], mixed[1:count // 2 * 2:2]
    slack = jnp.minimum(tallies[source_of] - 1, reach - tallies[taker]) // 2
    slack = jnp.where((source_of == sequence[0]) | (taker == sequence[0]) | (tallies[taker] == 0), 0, jnp.maximum(slack, 0))
    moved = jax.random.randint(jax.random.fold_in(own, 4), (count // 2,), 0, 1 << 20) % (slack + 1)
    tallies = tallies.at[source_of].add(-moved).at[taker].add(moved)
    members = jnp.searchsorted(jnp.cumsum(tallies), jnp.arange(rows * top), side="right").astype(jnp.int32)
    grid = members.reshape(top, rows).T
    grid = grid[jax.random.permutation(jax.random.fold_in(own, 1), rows)]
    turn = jax.random.randint(jax.random.fold_in(own, 2), (rows, 1), 0, top)
    return jnp.take_along_axis(grid, (jnp.arange(top)[None, :] + turn) % top, axis=1)


def shares(count, total, most, lean, full):
    portions = [(1 << 20) // math.isqrt(rank ** lean) + 1 for rank in range(1, count + 1)]
    largest = most if full else min(most, max(-(-total // count), total * portions[0] // sum(portions)))
    least = 1 if total - largest >= count - 1 else 0
    counts, spare = [largest] + [least] * (count - 1), total - largest - least * (count - 1)
    while spare > 0:
        free = [i for i in range(1, count) if counts[i] < largest] or [i for i in range(1, count) if counts[i] < most]
        mass, remaining = sum([portions[i] for i in free]), spare
        for i in free:
            addition = min(most - counts[i], max(1, remaining * portions[i] // mass), spare)
            counts[i] = counts[i] + addition
            spare = spare - addition
    return np.array(counts)


def scatter_about(own_key, shape, deviation, most, cuts=(), kind=jnp.bfloat16):
    values = jax.random.normal(own_key, shape, jnp.float32) * deviation
    if len(cuts) > 0:
        values = block_levels(own_key, shape, cuts, -0.22, 0.18) * values
    return jnp.clip(values, min=-most, max=most).astype(kind)


def setup_inputs(seed: int = 0) -> dict:
    key_list = jax.random.split(jax.random.key(seed), 18)
    hidden = scatter_about(key_list[0], (TOKENS, D), 1.0, 6.0, ((0, 128),))
    queries = draw_queries(jax.random.fold_in(key_list[17], 71), 0)
    cache = draw_cache(jax.random.fold_in(key_list[17], 71), 0)
    new_latent = draw_new_latent(jax.random.fold_in(key_list[17], 71), 0)
    lengths = ragged(key_list[4], TOKENS, TOKENS * CACHE // 2, CACHE, 2).astype(jnp.int32)
    w_values = scatter_about(key_list[5], (H, LAT, VD), LAT ** -0.5, 0.25, ((0, 8),))
    w_out = scatter_about(key_list[6], (H, VD, D), (H * VD // 16) ** -0.5, 0.1875, ((0, 8), (2, 16)))
    gain_attn = jnp.clip(1.0 + 0.18 * jax.random.normal(key_list[7], (D,), jnp.float32), 0.1, 1.9)
    w_dense_gate = scatter_about(key_list[8], (D, FF), D ** -0.5, 0.0625, ((1, 128),))
    w_dense_up = scatter_about(key_list[9], (D, FF), D ** -0.5, 0.0625, ((1, 128),))
    w_dense_down = scatter_about(key_list[10], (FF, D), FF ** -0.5, 0.046875, ((0, 128),))
    gain_moe = jnp.clip(1.0 + 0.18 * jax.random.normal(key_list[11], (D,), jnp.float32), 0.1, 1.9)
    w_router = scatter_about(key_list[12], (D, EXPERTS), D ** -0.5, 0.0625)
    expert_ids_keys = jax.random.split(jax.random.fold_in(key_list[13], 1), TOKENS // TOK_DEV)
    expert_ids_turns = jax.random.permutation(jax.random.fold_in(key_list[13], 3), TOKENS // TOK_DEV)
    expert_ids = jax.vmap(lambda own, number: routed_block(jax.random.fold_in(key_list[13], 2), own, number, TOK_DEV, EXPERTS, TOP, CAP, 2))(expert_ids_keys, expert_ids_turns).reshape((TOKENS, TOP))
    w_expert_gate = scatter_about(key_list[14], (EXPERTS, D, EH), D ** -0.5, 0.0625, ((0, 16), (2, 8)))
    w_expert_up = scatter_about(key_list[15], (EXPERTS, D, EH), D ** -0.5, 0.0625, ((0, 16), (2, 8)))
    w_expert_down = scatter_about(key_list[16], (EXPERTS, EH, D), EH ** -0.5, 0.125, ((0, 16), (1, 8)))
    return dict(hidden=hidden, queries=queries, cache=cache, new_latent=new_latent, lengths=lengths, w_values=w_values, w_out=w_out, gain_attn=gain_attn, w_dense_gate=w_dense_gate, w_dense_up=w_dense_up, w_dense_down=w_dense_down, gain_moe=gain_moe, w_router=w_router, expert_ids=expert_ids, w_expert_gate=w_expert_gate, w_expert_up=w_expert_up, w_expert_down=w_expert_down)


EPSILON = 1e-06
ROUTE_SCALE = 2.5

def rms_scale(values, norm_gain):
    mean_square = lax.optimization_barrier(jnp.mean(values * values, axis=-1, keepdims=True))
    return values * lax.rsqrt(mean_square + EPSILON) * norm_gain

def attend_request(operands):
    query_rows, cache_rows, own_latent, length_value = operands
    score_scale = (VD + ROPE) ** (-0.5)
    scores = jnp.dot(query_rows, cache_rows.T, preferred_element_type=jnp.float32) * score_scale
    own_score = jnp.dot(query_rows, own_latent, preferred_element_type=jnp.float32) * score_scale
    places = jnp.arange(CACHE, dtype=jnp.int32)
    scores = jnp.where((places < length_value)[None, :], scores, -jnp.inf)
    peak = jnp.maximum(lax.optimization_barrier(jnp.max(scores, axis=1)), own_score)
    weights = jnp.exp(scores - peak[:, None])
    own_weight = jnp.exp(own_score - peak)
    sum_total = lax.optimization_barrier(jnp.sum(weights, axis=1)) + own_weight
    probability = (weights / sum_total[:, None]).astype(jnp.bfloat16)
    own_probability = (own_weight / sum_total).astype(jnp.bfloat16)
    context = jnp.dot(probability, cache_rows[:, :LAT], preferred_element_type=jnp.float32)
    context = context + own_probability.astype(jnp.float32)[:, None] * own_latent[:LAT].astype(jnp.float32)[None, :]
    return context.astype(jnp.bfloat16)

def reference(hidden, queries, cache, new_latent, lengths, w_values, w_out, gain_attn, w_dense_gate, w_dense_up, w_dense_down, gain_moe, w_router, expert_ids, w_expert_gate, w_expert_up, w_expert_down):
    contexts = lax.map(attend_request, (queries, cache, new_latent, lengths))
    head_values = jnp.einsum('thl,hlv->thv', contexts.astype(jnp.float32), w_values.astype(jnp.float32), precision=lax.Precision.HIGHEST).astype(jnp.bfloat16)
    attention = jnp.dot(head_values.reshape(TOKENS, H * VD), w_out.reshape(H * VD, D), preferred_element_type=jnp.float32)
    after_attn = hidden.astype(jnp.float32) + attention
    normed = rms_scale(after_attn, gain_attn).astype(jnp.bfloat16)
    gate_part = jnp.dot(normed, w_dense_gate, preferred_element_type=jnp.float32)
    up_part = jnp.dot(normed, w_dense_up, preferred_element_type=jnp.float32)
    dense_act = (jax.nn.silu(gate_part) * up_part).astype(jnp.bfloat16)
    second = after_attn + jnp.dot(dense_act, w_dense_down, preferred_element_type=jnp.float32)
    routed_in = rms_scale(second, gain_moe).astype(jnp.bfloat16)
    affinity = jax.nn.sigmoid(jnp.dot(routed_in, w_router, preferred_element_type=jnp.float32))
    picked = jnp.take_along_axis(affinity, expert_ids, axis=1)
    route_weight = ROUTE_SCALE * picked / lax.optimization_barrier(jnp.sum(picked, axis=1, keepdims=True))

    def expert_apply(expert):
        gate_rows = jnp.dot(routed_in, w_expert_gate[expert], preferred_element_type=jnp.float32)
        up_rows = jnp.dot(routed_in, w_expert_up[expert], preferred_element_type=jnp.float32)
        activated = (jax.nn.silu(gate_rows) * up_rows).astype(jnp.bfloat16)
        blocks = activated.reshape(TOKENS, N_TP, EH // N_TP).astype(jnp.float32)
        down_blocks = w_expert_down[expert].reshape(N_TP, EH // N_TP, D).astype(jnp.float32)
        partial_value = jnp.einsum('tsh,shd->tsd', blocks, down_blocks, precision=lax.Precision.HIGHEST).astype(jnp.bfloat16)
        return lax.optimization_barrier(jnp.sum(partial_value.astype(jnp.float32), axis=1)).astype(jnp.bfloat16)
    expert_rows = lax.map(expert_apply, jnp.arange(EXPERTS, dtype=jnp.int32))
    token_index = jnp.arange(TOKENS, dtype=jnp.int32)[:, None]
    chosen_rows = expert_rows[expert_ids, token_index].astype(jnp.float32)
    routed_sum = lax.optimization_barrier(jnp.sum(route_weight[:, :, None] * chosen_rows, axis=1))
    return (second + routed_sum).astype(jnp.bfloat16)
```

```python
import functools

import jax
import jax.numpy as jnp
from jax import lax
from jax.experimental import pallas as pl
from jax.experimental.pallas import tpu as pltpu
from jax.sharding import PartitionSpec as P

ROPE = 64
VD = 128
D = 7168
BLK = 896
EPSILON = 1e-06
ROUTE_SCALE = 2.5
MESH = pl.DeviceIdType.MESH
F32 = jnp.float32
BF16 = jnp.bfloat16
VMEM_LIMIT = 60 * 2**20


PORTIONS = ((0, 384, ("x", "y", "z")), (384, 256, ("y", "z", "x")), (640, 256, ("z", "x", "y")))
DIMS = ("z", "y", "x")


def coords():
    tp, ep = lax.axis_index("tp"), lax.axis_index("ep")
    return dict(x=tp // 2, c=tp % 2, z=ep // 4, y=ep % 4)


def device(at):
    return (at["x"] * 2 + at["c"], at["z"] * 4 + at["y"])


def moved(at, **steps):
    new = dict(at)
    for name, step in steps.items():
        new[name] = lax.rem(at[name] + step, 2 if name == "c" else 4)
    return new


def meet(partners):
    barrier = pltpu.get_barrier_semaphore()
    for partner in partners:
        pl.semaphore_signal(barrier, inc=1, device_id=device(partner), device_id_type=MESH)
    pl.semaphore_wait(barrier, len(partners))


def remote(src, dst, send, recv, partner):
    return pltpu.make_async_remote_copy(
        src_ref=src, dst_ref=dst, send_sem=send, recv_sem=recv, device_id=device(partner), device_id_type=MESH
    )


def dot_nt(a, b):
    return lax.dot_general(a, b, (((1,), (1,)), ((), ())), preferred_element_type=F32)


def dot(a, b):
    return jnp.dot(a, b, preferred_element_type=F32)


def attn_kernel(
    ctx_ref, hid_ref, wv_hbm, wo_hbm, out_ref,
    wv, wo, ctx_in, heads, part, part_in, hid_out, hid_in, load_sem,
    hid_s, hid_r, ctx_s, ctx_r, hv_s, hv_r, part_s, part_r,
):
    me = coords()
    x, c, z, y = me["x"], me["c"], me["z"], me["y"]
    yh, yl = y // 2, y % 2
    tp = x * 2 + c
    pad = pl.multiple_of(yl * 64, 64)
    load_wv = pltpu.make_async_copy(wv_hbm, wv, load_sem.at[0])
    load_wo = pltpu.make_async_copy(wo_hbm, wo.at[:, pl.ds(pad, 448), :], load_sem.at[1])
    load_wv.start()
    load_wo.start()
    wo[:, pl.ds(pl.multiple_of((1 - yl) * 448, 64), 64), :] = jnp.zeros((16, 64, 128), BF16)

    def at_tp(step):
        other = lax.rem(tp + step, 8)
        return dict(me, x=other // 2, c=other % 2)

    tp_steps = [(dt, dy) for dy in (0, 1) for dt in range(8) if dt or dy]
    part_to = [dict(at_tp(dt), y=yh * 2 + (yl + dy) % 2) for dt, dy in tp_steps]
    hid_steps = [(dz, dy) for dy in (0, 2) for dz in range(4) if dz or dy]
    hid_to = [moved(me, z=dz, y=dy) for dz, dy in hid_steps]
    other_odd = dict(me, y=lax.rem(yh * 2 + 2, 4) + (1 - yl))
    meet(part_to + hid_to + [other_odd])

    first = (z * 2 + yh) * 2
    row = lax.broadcasted_iota(jnp.int32, (16, BLK), 0)
    for f in range(8):
        both = hid_ref[:, f * BLK : (f + 1) * BLK].astype(F32)
        placed = jnp.where(row == first, both[0:1, :], jnp.where(row == first + 1, both[1:2, :], 0.0))
        hid_out[f // 2, f % 2] = placed.astype(BF16)
    copies = []
    ctx_copies = []
    for step in range(1, 8):
        to = at_tp(step)
        copy = remote(ctx_ref.at[:, to["x"] * 2 + to["c"]], ctx_in.at[tp], ctx_s.at[step - 1], ctx_r.at[step - 1], to)
        copy.start()
        ctx_copies.append(copy)
    hid_copies = []
    for i, to in enumerate(hid_to):
        copy = remote(hid_out.at[to["z"], to["y"] // 2], hid_in.at[z, yh], hid_s.at[i], hid_r.at[i], to)
        copy.start()
        hid_copies.append(copy)
    ctx_in[tp] = ctx_ref[:, tp]
    hid_in[z, yh] = hid_out[z, yh]
    for copy in ctx_copies:
        copy.wait_recv()
    load_wv.wait()

    i = lax.broadcasted_iota(jnp.int32, (256, 256), 0)
    j = lax.broadcasted_iota(jnp.int32, (256, 256), 1)
    turn = ((i & 15) * 16 + (i >> 4) == j).astype(BF16)
    by_head = dot(turn, ctx_in[...].reshape(256, 512)).astype(BF16)
    for h in range(16):
        heads[z, y, :, h * 128 : (h + 1) * 128] = dot(by_head[h * 16 : (h + 1) * 16, :], wv[h]).astype(BF16)

    halves = ((0, "z", "y"), (1, "y", "z"))
    sends = []
    for half, one, two in halves:
        lanes = pl.ds(half * 1024, 1024)
        for step in range(1, 4):
            mine = heads.at[z, y, :, lanes]
            copy = remote(mine, mine, hv_s.at[half, 0, step - 1], hv_r.at[half, 0, step - 1], moved(me, **{one: step}))
            copy.start()
            sends.append(copy)
    for half, one, two in halves:
        lanes = pl.ds(half * 1024, 1024)
        for step in range(1, 4):
            sends[half * 3 + step - 1].wait_recv()
        for step in range(1, 4):
            slab = heads.at[:, y, :, lanes] if two == "y" else heads.at[z, :, :, lanes]
            copy = remote(slab, slab, hv_s.at[half, 1, step - 1], hv_r.at[half, 1, step - 1], moved(me, **{two: step}))
            copy.start()
            sends.append(copy)
    load_wo.wait()
    for copy in sends[6:]:
        copy.wait_recv()

    total = jnp.zeros((256, 512), F32)
    for pair in range(8):
        rows = heads[:, :, :, pair * 256 : (pair + 1) * 256].reshape(256, 256)
        weights = jnp.concatenate([wo[2 * pair], wo[2 * pair + 1]], axis=1)
        total = total + dot_nt(rows, weights)
    t, from_yh, from_z = i & 1, (i >> 1) & 1, (i >> 2) & 3
    source = from_z * 64 + (from_yh * 2 + (i >> 7)) * 16 + ((i >> 4) & 7) * 2 + t
    order = (source == j).astype(BF16)
    part[...] = dot(order, total.astype(BF16)).astype(BF16).reshape(2, 8, 16, 512)
    part_copies = []
    for i_to, to in enumerate(part_to):
        copy = remote(
            part.at[to["y"] % 2, to["x"] * 2 + to["c"]], part_in.at[yl, tp], part_s.at[i_to], part_r.at[i_to], to
        )
        copy.start()
        part_copies.append(copy)
    part_in[yl, tp] = part[yl, tp]
    for copy in hid_copies:
        copy.wait_recv()
    out_ref[...] = jnp.sum(hid_in[...].astype(F32), axis=(0, 1))
    for copy in part_copies:
        copy.wait_recv()
    sums = jnp.sum(part_in[...].astype(F32), axis=1)
    out_ref[:, 0:512] += sums[0]
    out_ref[:, 384:896] += sums[1]
    for copy in ctx_copies + hid_copies + sends + part_copies:
        copy.wait_send()


def attn_exchange(context, hidden, w_values, w_out):
    any_space = pl.BlockSpec(memory_space=pl.ANY)
    vmem = pl.BlockSpec(memory_space=pltpu.VMEM)
    dma = pltpu.SemaphoreType.DMA
    return pl.pallas_call(
        attn_kernel,
        out_shape=jax.ShapeDtypeStruct((16, BLK), F32),
        in_specs=[vmem, vmem, any_space, any_space],
        out_specs=vmem,
        scratch_shapes=[
            pltpu.VMEM((16, 512, 128), BF16),
            pltpu.VMEM((16, 512, 128), BF16),
            pltpu.VMEM((8, 2, 16, 512), BF16),
            pltpu.VMEM((4, 4, 16, 2048), BF16),
            pltpu.VMEM((2, 8, 16, 512), BF16),
            pltpu.VMEM((2, 8, 16, 512), BF16),
            pltpu.VMEM((4, 2, 16, BLK), BF16),
            pltpu.VMEM((4, 2, 16, BLK), BF16),
            dma((2,)),
            dma((7,)), dma((7,)), dma((7,)), dma((7,)),
            dma((2, 2, 3)), dma((2, 2, 3)), dma((15,)), dma((15,)),
        ],
        compiler_params=pltpu.CompilerParams(collective_id=0, has_side_effects=True, vmem_limit_bytes=VMEM_LIMIT),
        name="attn_exchange",
    )(context, hidden, w_values, w_out)


def gather_region(at, portion, phase):
    start, width, order = PORTIONS[portion]
    done = order[::-1][:phase]
    index = tuple(pl.ds(0, 4) if name in done else at[name] for name in DIMS)
    return index + (at["c"], slice(None), pl.ds(start, width))


def ffn_kernel(routed, *refs):
    if routed:
        x_ref, gain_ref, wr_ref, ids_ref, wg_hbm, wu_hbm, wd_hbm, out_ref, *refs = refs
        own, final_in, final_s, final_r, *refs = refs
    else:
        x_ref, gain_ref, wg_hbm, wu_hbm, wd_hbm, out_ref, *refs = refs
    (
        wg, wu, wd, full, partial, core_in, acc, square, router_acc,
        in1a, in1b, in1c, b_a, b_b, b_c, in2a, in2b, in2c, c_a, c_b, c_c, in3a, in3b, in3c,
        load_sem, gather_s, gather_r, pair_s, pair_r, core_s, core_r, sum_s, sum_r,
    ) = refs
    in1, held2 = (in1a, in1b, in1c), (b_a, b_b, b_c)
    in2, held3 = (in2a, in2b, in2c), (c_a, c_b, c_c)
    in3 = (in3a, in3b, in3c)
    me = coords()
    z, y, x, c = me["z"], me["y"], me["x"], me["c"]
    yh, yl = y // 2, y % 2
    f_me = z * 2 + yh
    hidden = acc.shape[2]
    loads = [
        pltpu.make_async_copy(src, dst, load_sem.at[i])
        for i, (src, dst) in enumerate(((wg_hbm, wg), (wu_hbm, wu), (wd_hbm, wd)))
    ]
    for load in loads:
        load.start()
    sibling = moved(me, c=1)
    ring = {name: [moved(me, **{name: step}) for step in (1, 2, 3)] for name in DIMS}
    back = {name: [moved(me, **{name: 4 - step}) for step in (1, 2, 3)] for name in DIMS}
    partners = ring["x"] + ring["y"] + ring["z"] + [sibling]
    if routed:
        final_steps = [(dz, dy) for dy in (0, 2) for dz in range(4) if dz or dy]
        final_to = [moved(me, z=dz, y=dy) for dz, dy in final_steps]
        partners = partners + [moved(me, z=dz, y=2) for dz in (1, 2, 3)]
    full[z, y, x, c] = (x_ref[...] * gain_ref[pl.ds(f_me, 1), :]).astype(BF16)
    meet(partners)

    sends = []
    for phase in range(3):
        for p in range(3):
            axis = PORTIONS[p][2][2 - phase]
            if phase > 0:
                earlier = PORTIONS[p][2][3 - phase]
                for k in range(3):
                    region = full.at[gather_region(back[earlier][k], p, phase - 1)]
                    remote(
                        region, region, gather_s.at[p, phase - 1, k], gather_r.at[p, phase - 1, k], ring[earlier][k]
                    ).wait_recv()
            region = full.at[gather_region(me, p, phase)]
            for k in range(3):
                copy = remote(region, region, gather_s.at[p, phase, k], gather_r.at[p, phase, k], ring[axis][k])
                copy.start()
                sends.append(copy)
            if phase == 2:
                copy = remote(region, region, pair_s.at[p, 3], pair_r.at[p, 3], sibling)
                copy.start()
                sends.append(copy)
    for k in (0, 2, 1):
        for p in range(3):
            axis = PORTIONS[p][2][0]
            region = full.at[gather_region(back[axis][k], p, 2)]
            remote(region, region, gather_s.at[p, 2, k], gather_r.at[p, 2, k], ring[axis][k]).wait_recv()
            copy = remote(region, region, pair_s.at[p, k], pair_r.at[p, k], sibling)
            copy.start()
            sends.append(copy)
    for k in (3, 0, 2, 1):
        for p in range(3):
            axis = PORTIONS[p][2][0]
            place = dict(sibling) if k == 3 else dict(back[axis][k], c=sibling["c"])
            region = full.at[gather_region(place, p, 2)]
            remote(region, region, pair_s.at[p, k], pair_r.at[p, k], sibling).wait_recv()
    loads[0].wait()
    loads[1].wait()

    acc[...] = jnp.zeros_like(acc)
    square[...] = jnp.zeros_like(square)
    if routed:
        router_acc[...] = jnp.zeros_like(router_acc)

    def up_step(f, carry):
        rows = full[f // 2, pl.ds((f % 2) * 2, 2)].reshape(256, BLK)
        at = pl.ds(pl.multiple_of(f * BLK, 128), BLK)
        if routed:
            acc[0] += dot(rows, wg[at, :])
            acc[1] += dot(rows, wu[at, :])
            router_acc[...] += dot_nt(rows, wr_ref[:, at])
        else:
            acc[0] += dot_nt(rows, wg[:, at])
            acc[1] += dot_nt(rows, wu[:, at])
        gain = gain_ref[pl.ds(f, 1), :]
        plain = rows.astype(F32) * (1.0 / gain)
        plain = plain * plain
        piece = plain[:, 0:128]
        for k in range(1, 7):
            piece = piece + plain[:, k * 128 : (k + 1) * 128]
        square[...] += piece
        return carry

    lax.fori_loop(0, 8, up_step, 0)
    scale = lax.rsqrt(jnp.sum(square[...], axis=1, keepdims=True) * (1.0 / D) + EPSILON)
    gate = acc[0] * scale
    act = gate / (1.0 + jnp.exp(-gate)) * (acc[1] * scale)
    if routed:
        affinity = 1.0 / (1.0 + jnp.exp(-(router_acc[...] * scale)))
        lane = lax.broadcasted_iota(jnp.int32, (256, 16), 1)
        chosen = jnp.zeros((256, 16), F32)
        for k in range(ids_ref.shape[1]):
            chosen = chosen + jnp.where(ids_ref[:, k : k + 1] == lane, 1.0, 0.0)
        picked = jnp.where(chosen > 0.5, affinity, 0.0)
        below = jnp.sum(picked, axis=1, keepdims=True)
        mine = lane == z * 4 + y
        weight = ROUTE_SCALE * jnp.sum(jnp.where(mine, picked, 0.0), axis=1, keepdims=True) / below
        wanted = jnp.sum(jnp.where(mine, chosen, 0.0), axis=1, keepdims=True) > 0.5
        act = jnp.where(wanted, act * weight, 0.0)
    act = act.astype(BF16)
    loads[2].wait()

    core_copies = []

    def core_add(part):
        core_copies[part].wait_recv()

        def add(row, carry):
            both = partial[part, row, :, c].astype(F32) + core_in[part, row].astype(F32)
            partial[part, row, :, c] = both.astype(BF16)
            return carry

        lax.fori_loop(0, 4, add, 0)

    for part in range(4):
        for half in range(2):
            f = part * 2 + half
            block = dot(act, wd[:, f * BLK : (f + 1) * BLK])
            partial[part, half * 2 : half * 2 + 2] = block.astype(BF16).reshape(2, 4, 2, 16, BLK)
        copy = remote(
            partial.at[part, :, :, sibling["c"]], core_in.at[part], core_s.at[part], core_r.at[part], sibling
        )
        copy.start()
        core_copies.append(copy)
        if part:
            core_add(part - 1)
    core_add(3)

    def start(p, phase, source):
        axis = PORTIONS[p][2][phase]
        into = (in1, in2, in3)[phase][p]
        copies = []
        for k in range(3):
            copy = remote(source(ring[axis][k][axis]), into.at[k], sum_s.at[p, phase, k], sum_r.at[p, phase, k], ring[axis][k])
            copy.start()
            copies.append(copy)
        sends.extend(copies)
        return copies

    def cut(p, target):
        begin, width, order = PORTIONS[p]
        index = [slice(None)] * 3
        index[DIMS.index(order[0])] = target
        return tuple(index) + (c, slice(None), pl.ds(begin, width))

    flying = [start(p, 0, lambda target, p=p: partial.at[cut(p, target)]) for p in range(3)]
    next_flying = []
    for p in range(3):
        begin, width, order = PORTIONS[p]
        for copy in flying[p]:
            copy.wait_recv()

        def add(i, carry, p=p, begin=begin, width=width, order=order):
            left = [name for name in DIMS if name != order[0]]
            index = {order[0]: me[order[0]], left[0]: i, left[1]: slice(None)}
            index = tuple(index[name] for name in DIMS) + (c, slice(None), pl.ds(begin, width))
            value = partial[index].astype(F32)
            for k in range(3):
                value = value + in1[p][k, i].astype(F32)
            held2[p][i] = value.astype(BF16)
            return carry

        lax.fori_loop(0, 4, add, 0)
        left = [name for name in DIMS if name != order[0]]
        if order[1] == left[0]:
            next_flying.append(start(p, 1, lambda target, p=p: held2[p].at[target]))
        else:
            next_flying.append(start(p, 1, lambda target, p=p: held2[p].at[:, target]))
    flying, next_flying = next_flying, []
    for p in range(3):
        begin, width, order = PORTIONS[p]
        for copy in flying[p]:
            copy.wait_recv()
        left = [name for name in DIMS if name != order[0]]
        value = held2[p][me[order[1]]] if order[1] == left[0] else held2[p][:, me[order[1]]]
        value = value.astype(F32)
        for k in range(3):
            value = value + in2[p][k].astype(F32)
        held3[p][...] = value.astype(BF16)
        next_flying.append(start(p, 2, lambda target, p=p: held3[p].at[target]))
    for p in range(3):
        begin, width, order = PORTIONS[p]
        for copy in next_flying[p]:
            copy.wait_recv()
        value = held3[p][me[order[2]]].astype(F32)
        for k in range(3):
            value = value + in3[p][k].astype(F32)
        value = value + x_ref[:, begin : begin + width]
        if routed:
            own[:, begin : begin + width] = value.astype(BF16)
        else:
            out_ref[:, begin : begin + width] = value

    if routed:
        final_copies = []
        for i, to in enumerate(final_to):
            copy = remote(own, final_in.at[z, yh], final_s.at[i], final_r.at[i], to)
            copy.start()
            final_copies.append(copy)
        final_in[z, yh] = own[...]
        for copy in final_copies:
            copy.wait_recv()
        row = lax.broadcasted_iota(jnp.int32, (16, BLK), 0)
        for f in range(8):
            block = final_in[f // 2, f % 2].astype(F32)
            for t in range(2):
                out_ref[t : t + 1, f * BLK : (f + 1) * BLK] = jnp.sum(
                    jnp.where(row == f_me * 2 + t, block, 0.0), axis=0, keepdims=True
                )
        for copy in final_copies:
            copy.wait_send()
    for copy in sends + core_copies:
        copy.wait_send()


def ffn(routed, shard, gain, w_gate, w_up, w_down, w_router=None, ids=None):
    any_space = pl.BlockSpec(memory_space=pl.ANY)
    vmem = pl.BlockSpec(memory_space=pltpu.VMEM)
    dma = pltpu.SemaphoreType.DMA
    hidden = w_down.shape[0]
    widths = [width for _, width, _ in PORTIONS]
    extra_in, extra_specs, extra_scratch = [], [], []
    if routed:
        extra_in, extra_specs = [w_router, ids], [vmem, vmem]
        extra_scratch = [pltpu.VMEM((16, BLK), BF16), pltpu.VMEM((4, 2, 16, BLK), BF16), dma((7,)), dma((7,))]
    return pl.pallas_call(
        functools.partial(ffn_kernel, routed),
        out_shape=jax.ShapeDtypeStruct((2, D) if routed else (16, BLK), F32),
        in_specs=[vmem, vmem] + extra_specs + [any_space] * 3,
        out_specs=vmem,
        scratch_shapes=extra_scratch
        + [
            pltpu.VMEM(w_gate.shape, BF16),
            pltpu.VMEM(w_up.shape, BF16),
            pltpu.VMEM(w_down.shape, BF16),
            pltpu.VMEM((4, 4, 4, 2, 16, BLK), BF16),
            pltpu.VMEM((4, 4, 4, 2, 16, BLK), BF16),
            pltpu.VMEM((4, 4, 4, 16, BLK), BF16),
            pltpu.VMEM((2, 256, hidden), F32),
            pltpu.VMEM((256, 128), F32),
            pltpu.VMEM((256, 16), F32),
        ]
        + [pltpu.VMEM((3, 4, 4, 16, width), BF16) for width in widths]
        + [pltpu.VMEM((4, 4, 16, width), BF16) for width in widths]
        + [pltpu.VMEM((3, 4, 16, width), BF16) for width in widths]
        + [pltpu.VMEM((4, 16, width), BF16) for width in widths]
        + [pltpu.VMEM((3, 16, width), BF16) for width in widths]
        + [
            dma((3,)),
            dma((3, 3, 3)), dma((3, 3, 3)), dma((3, 4)), dma((3, 4)),
            dma((4,)), dma((4,)), dma((3, 3, 3)), dma((3, 3, 3)),
        ],
        compiler_params=pltpu.CompilerParams(
            collective_id=2 if routed else 1, has_side_effects=True, vmem_limit_bytes=VMEM_LIMIT
        ),
        name="routed_ffn" if routed else "dense_ffn",
    )(shard, gain, *extra_in, w_gate, w_up, w_down)


def latent_attention(queries, cache, new_latent, lengths, latent_dim):
    score_scale = (VD + ROPE) ** (-0.5)
    scores = (
        jnp.einsum("thc,tlc->thl", queries, cache, preferred_element_type=jnp.float32) * score_scale
    )
    own_score = (
        jnp.einsum("thc,tc->th", queries, new_latent, preferred_element_type=jnp.float32)
        * score_scale
    )
    places = jnp.arange(cache.shape[1], dtype=jnp.int32)
    in_range = places[None, None, :] < lengths[:, None, None]
    scores = jnp.where(in_range, scores, -jnp.inf)
    peak = jnp.maximum(jnp.max(scores, axis=2), own_score)
    weights = jnp.exp(scores - peak[:, :, None])
    own_weight = jnp.exp(own_score - peak)
    sum_total = jnp.sum(weights, axis=2) + own_weight
    probability = (weights / sum_total[:, :, None]).astype(jnp.bfloat16)
    own_probability = (own_weight / sum_total).astype(jnp.bfloat16)
    context = jnp.einsum(
        "thl,tlc->thc", probability, cache[:, :, :latent_dim], preferred_element_type=jnp.float32
    )
    context = context + own_probability.astype(jnp.float32)[:, :, None] * new_latent[
        :, None, :latent_dim
    ].astype(jnp.float32)
    return context.astype(jnp.bfloat16)


def body(
    hidden,
    queries,
    cache,
    new_latent,
    lengths,
    w_values,
    w_out,
    gain_attn,
    w_dense_gate,
    w_dense_up,
    w_dense_down,
    gain_moe,
    w_router,
    expert_ids,
    w_expert_gate,
    w_expert_up,
    w_expert_down,
):
    top_count = expert_ids.shape[1]
    everyone_ids = lax.all_gather(expert_ids, ("tp", "ep"), axis=0, tiled=True)
    ids = everyone_ids.reshape(8, 8, 2, 2, top_count).transpose(2, 0, 1, 3, 4).reshape(256, top_count)
    context = latent_attention(queries, cache, new_latent, lengths, w_values.shape[1])
    after_attn = attn_exchange(
        context.reshape(2, 8, 16, 512), hidden, w_values, jnp.swapaxes(w_out, 1, 2)
    )
    second = ffn(False, after_attn, gain_attn.reshape(8, BLK), w_dense_gate.T, w_dense_up.T, w_dense_down)
    out = ffn(
        True, second, gain_moe.reshape(8, BLK), w_expert_gate[0], w_expert_up[0], w_expert_down[0], w_router.T, ids
    )
    return out.astype(BF16)


def solution(mesh):
    in_specs = (
        P(("tp", "ep"), None),
        P(("tp", "ep"), None, None),
        P(("tp", "ep"), None, None),
        P(("tp", "ep"), None),
        P(("tp", "ep")),
        P("tp", None, None),
        P("tp", None, "ep"),
        P(),
        P(None, ("tp", "ep")),
        P(None, ("tp", "ep")),
        P(("tp", "ep"), None),
        P(),
        P(),
        P(("tp", "ep"), None),
        P("ep", None, "tp"),
        P("ep", None, "tp"),
        P("ep", "tp", None),
    )
    out_specs = P(("tp", "ep"), None)
    return jax.shard_map(body, mesh=mesh, in_specs=in_specs, out_specs=out_specs, check_vma=False)
```

```python
import jax
import jax.numpy as jnp
from jax import lax
from jax.experimental import pallas as pl
from jax.experimental.pallas import tpu as pltpu
from jax.sharding import PartitionSpec as P

ROPE = 64
VD = 128
D = 7168
BLK = 896
EPSILON = 1e-06
ROUTE_SCALE = 2.5
MESH = pl.DeviceIdType.MESH
F32 = jnp.float32
BF16 = jnp.bfloat16
VMEM_LIMIT = 60 * 2**20


PORTIONS = ((0, 384, ("x", "y", "z")), (384, 256, ("y", "z", "x")), (640, 256, ("z", "x", "y")))
DIMS = ("z", "y", "x")


def coords():
    tp, ep = lax.axis_index("tp"), lax.axis_index("ep")
    return dict(x=tp // 2, c=tp % 2, z=ep // 4, y=ep % 4)


def device(at):
    return (at["x"] * 2 + at["c"], at["z"] * 4 + at["y"])


def moved(at, **steps):
    new = dict(at)
    for name, step in steps.items():
        new[name] = lax.rem(at[name] + step, 2 if name == "c" else 4)
    return new


def meet(partners):
    barrier = pltpu.get_barrier_semaphore()
    for partner in partners:
        pl.semaphore_signal(barrier, inc=1, device_id=device(partner), device_id_type=MESH)
    pl.semaphore_wait(barrier, len(partners))


def remote(src, dst, send, recv, partner):
    return pltpu.make_async_remote_copy(
        src_ref=src, dst_ref=dst, send_sem=send, recv_sem=recv, device_id=device(partner), device_id_type=MESH
    )


def dot_nt(a, b):
    return lax.dot_general(a, b, (((1,), (1,)), ((), ())), preferred_element_type=F32)


def dot(a, b):
    return jnp.dot(a, b, preferred_element_type=F32)


def attn_kernel(
    ctx_ref, hid_ref, ids_ref, wv_hbm, wo_hbm, out_ref, chosen_ref,
    wv, wo, ctx_in, heads, part, part_in, hid_out, hid_in, mask_out, mask_in, load_sem,
    hid_s, hid_r, ctx_s, ctx_r, mask_s, mask_r, hv_s, hv_r, part_s, part_r,
):
    me = coords()
    x, c, z, y = me["x"], me["c"], me["z"], me["y"]
    yh, yl = y // 2, y % 2
    tp = x * 2 + c
    pad = pl.multiple_of(yl * 64, 64)
    load_wv = pltpu.make_async_copy(wv_hbm, wv, load_sem.at[0])
    load_wo = pltpu.make_async_copy(wo_hbm, wo.at[:, pl.ds(pad, 448), :], load_sem.at[1])
    load_wv.start()
    load_wo.start()
    wo[:, pl.ds(pl.multiple_of((1 - yl) * 448, 64), 64), :] = jnp.zeros((16, 64, 128), BF16)

    def at_tp(step):
        other = lax.rem(tp + step, 8)
        return dict(me, x=other // 2, c=other % 2)

    tp_steps = [(dt, dy) for dy in (0, 1) for dt in range(8) if dt or dy]
    part_to = [dict(at_tp(dt), y=yh * 2 + (yl + dy) % 2) for dt, dy in tp_steps]
    hid_steps = [(dz, dy) for dy in (0, 2) for dz in range(4) if dz or dy]
    hid_to = [moved(me, z=dz, y=dy) for dz, dy in hid_steps]
    other_odd = dict(me, y=lax.rem(yh * 2 + 2, 4) + (1 - yl))
    meet(part_to + hid_to + [other_odd])

    first = (z * 2 + yh) * 2
    row = lax.broadcasted_iota(jnp.int32, (16, BLK), 0)
    for f in range(8):
        both = hid_ref[:, f * BLK : (f + 1) * BLK].astype(F32)
        placed = jnp.where(row == first, both[0:1, :], jnp.where(row == first + 1, both[1:2, :], 0.0))
        hid_out[f // 2, f % 2] = placed.astype(BF16)
    lane = lax.broadcasted_iota(jnp.int32, (2, 128), 1)
    chosen = jnp.zeros((2, 128), F32)
    for k in range(ids_ref.shape[1]):
        chosen = chosen + jnp.where(ids_ref[:, k : k + 1] == lane, 1.0, 0.0)
    row = lax.broadcasted_iota(jnp.int32, (16, 128), 0)
    placed = jnp.where(row == tp * 2, chosen[0:1, :], jnp.where(row == tp * 2 + 1, chosen[1:2, :], 0.0))
    mask_out[...] = placed.astype(BF16)
    ctx_copies = []
    for step in range(1, 8):
        to = at_tp(step)
        copy = remote(ctx_ref.at[:, to["x"] * 2 + to["c"]], ctx_in.at[tp], ctx_s.at[step - 1], ctx_r.at[step - 1], to)
        copy.start()
        ctx_copies.append(copy)
    for step in range(1, 8):
        copy = remote(mask_out, mask_in.at[tp], mask_s.at[step - 1], mask_r.at[step - 1], at_tp(step))
        copy.start()
        ctx_copies.append(copy)
    hid_copies = []
    for i, to in enumerate(hid_to):
        copy = remote(hid_out.at[to["z"], to["y"] // 2], hid_in.at[z, yh], hid_s.at[i], hid_r.at[i], to)
        copy.start()
        hid_copies.append(copy)
    ctx_in[tp] = ctx_ref[:, tp]
    mask_in[tp] = mask_out[...]
    hid_in[z, yh] = hid_out[z, yh]
    for copy in ctx_copies:
        copy.wait_recv()
    load_wv.wait()

    i = lax.broadcasted_iota(jnp.int32, (256, 256), 0)
    j = lax.broadcasted_iota(jnp.int32, (256, 256), 1)
    turn = ((i & 15) * 16 + (i >> 4) == j).astype(BF16)
    by_head = dot(turn, ctx_in[...].reshape(256, 512)).astype(BF16)
    for h in range(16):
        heads[z, y, :, h * 128 : (h + 1) * 128] = dot(by_head[h * 16 : (h + 1) * 16, :], wv[h]).astype(BF16)

    heads[z, y, :, 2048:2176] = jnp.sum(mask_in[...].astype(F32), axis=0).astype(BF16)

    halves = ((0, "z", "y"), (1, "y", "z"))
    sends = []
    for half, one, two in halves:
        lanes = pl.ds(half * 1024, 1024 + half * 128)
        for step in range(1, 4):
            mine = heads.at[z, y, :, lanes]
            copy = remote(mine, mine, hv_s.at[half, 0, step - 1], hv_r.at[half, 0, step - 1], moved(me, **{one: step}))
            copy.start()
            sends.append(copy)
    for half, one, two in halves:
        lanes = pl.ds(half * 1024, 1024 + half * 128)
        for step in range(1, 4):
            sends[half * 3 + step - 1].wait_recv()
        for step in range(1, 4):
            slab = heads.at[:, y, :, lanes] if two == "y" else heads.at[z, :, :, lanes]
            copy = remote(slab, slab, hv_s.at[half, 1, step - 1], hv_r.at[half, 1, step - 1], moved(me, **{two: step}))
            copy.start()
            sends.append(copy)
    load_wo.wait()
    for copy in sends[6:]:
        copy.wait_recv()

    total = jnp.zeros((256, 512), F32)
    for pair in range(8):
        rows = heads[:, :, :, pair * 256 : (pair + 1) * 256].reshape(256, 256)
        weights = jnp.concatenate([wo[2 * pair], wo[2 * pair + 1]], axis=1)
        total = total + dot_nt(rows, weights)
    t, from_yh, from_z = i & 1, (i >> 1) & 1, (i >> 2) & 3
    source = from_z * 64 + (from_yh * 2 + (i >> 7)) * 16 + ((i >> 4) & 7) * 2 + t
    order = (source == j).astype(BF16)
    part[...] = dot(order, total.astype(BF16)).astype(BF16).reshape(2, 8, 16, 512)
    part_copies = []
    for i_to, to in enumerate(part_to):
        copy = remote(
            part.at[to["y"] % 2, to["x"] * 2 + to["c"]], part_in.at[yl, tp], part_s.at[i_to], part_r.at[i_to], to
        )
        copy.start()
        part_copies.append(copy)
    part_in[yl, tp] = part[yl, tp]
    plane = i >> 7
    to_yl = ((i >> 6) & 1) * (1 - plane) + ((i >> 4) & 1) * plane
    to_x = ((i >> 4) & 3) * (1 - plane) + ((i >> 5) & 3) * plane
    source = from_z * 64 + (from_yh * 2 + to_yl) * 16 + to_x * 4 + plane * 2 + t
    chosen_ref[...] = dot((source == j).astype(BF16), heads[:, :, :, 2048:2176].reshape(256, 128)).astype(BF16)
    for copy in hid_copies:
        copy.wait_recv()
    out_ref[...] = jnp.sum(hid_in[...].astype(F32), axis=(0, 1))
    for copy in part_copies:
        copy.wait_recv()
    sums = jnp.sum(part_in[...].astype(F32), axis=1)
    out_ref[:, 0:512] += sums[0]
    out_ref[:, 384:896] += sums[1]
    for copy in ctx_copies + hid_copies + sends + part_copies:
        copy.wait_send()


def attn_exchange(context, hidden, ids, w_values, w_out):
    any_space = pl.BlockSpec(memory_space=pl.ANY)
    vmem = pl.BlockSpec(memory_space=pltpu.VMEM)
    dma = pltpu.SemaphoreType.DMA
    return pl.pallas_call(
        attn_kernel,
        out_shape=(jax.ShapeDtypeStruct((16, BLK), F32), jax.ShapeDtypeStruct((256, 128), BF16)),
        in_specs=[vmem, vmem, vmem, any_space, any_space],
        out_specs=(vmem, vmem),
        scratch_shapes=[
            pltpu.VMEM((16, 512, 128), BF16),
            pltpu.VMEM((16, 512, 128), BF16),
            pltpu.VMEM((8, 2, 16, 512), BF16),
            pltpu.VMEM((4, 4, 16, 2176), BF16),
            pltpu.VMEM((2, 8, 16, 512), BF16),
            pltpu.VMEM((2, 8, 16, 512), BF16),
            pltpu.VMEM((4, 2, 16, BLK), BF16),
            pltpu.VMEM((4, 2, 16, BLK), BF16),
            pltpu.VMEM((16, 128), BF16),
            pltpu.VMEM((8, 16, 128), BF16),
            dma((2,)),
            dma((7,)), dma((7,)), dma((7,)), dma((7,)), dma((7,)), dma((7,)),
            dma((2, 2, 3)), dma((2, 2, 3)), dma((15,)), dma((15,)),
        ],
        compiler_params=pltpu.CompilerParams(collective_id=0, has_side_effects=True, vmem_limit_bytes=VMEM_LIMIT),
        name="attn_exchange",
    )(context, hidden, ids, w_values, w_out)


def turned(at):
    c = at["c"]
    return dict(
        z=at["z"] * (1 - c) + at["x"] * c, y=at["y"] * (1 - c) + at["z"] * c, x=at["x"] * (1 - c) + at["y"] * c, c=c
    )


def straight(at):
    c = at["c"]
    return dict(
        z=at["z"] * (1 - c) + at["y"] * c, y=at["y"] * (1 - c) + at["x"] * c, x=at["x"] * (1 - c) + at["z"] * c, c=c
    )


def region_of(at, portion, phase):
    start, width, order = PORTIONS[portion]
    done = order[::-1][:phase]
    index = tuple(pl.ds(0, 4) if name in done else at[name] for name in DIMS)
    return (at["c"],) + index + (slice(None), pl.ds(start, width))


def plane_cut(plane, part, half=None):
    ys = slice(None) if half is None else slice(half * 2, half * 2 + 2)
    return (0, part, ys) if plane == 0 else (1, slice(None), part, ys)


class Layer:
    def __init__(self, number, me, sibling, x_ref, gain_ref, refs):
        self.number, self.me, self.sibling, self.x, self.gain = number, me, sibling, x_ref, gain_ref
        (
            self.full, self.partial, self.core_in, self.acc, self.square,
            *lists, self.gather_s, self.gather_r, self.pair_s, self.pair_r, self.core_s, self.core_r, self.sum_s, self.sum_r,
        ) = refs
        self.in1, self.held2, self.in2, self.held3, self.in3 = [lists[i * 3 : i * 3 + 3] for i in range(5)]
        self.ring = {name: [moved(me, **{name: step}) for step in (1, 2, 3)] for name in DIMS}
        self.back = {name: [moved(me, **{name: 4 - step}) for step in (1, 2, 3)] for name in DIMS}
        self.sends = []

    def begin(self, p, f_me):
        start, width, order = PORTIONS[p]
        me = self.me
        lanes = pl.ds(start, width)
        scaled = self.x[:, lanes] * self.gain[pl.ds(f_me, 1), lanes]
        self.full[me["c"], me["z"], me["y"], me["x"], :, lanes] = scaled.astype(BF16)
        self.send(p, 0)

    def send(self, p, phase):
        axis = PORTIONS[p][2][2 - phase]
        region = self.full.at[region_of(self.me, p, phase)]
        for k in range(3):
            copy = remote(
                region, region, self.gather_s.at[p, phase, k], self.gather_r.at[p, phase, k], straight(self.ring[axis][k])
            )
            copy.start()
            self.sends.append(copy)

    def take(self, p, phase, k):
        axis = PORTIONS[p][2][2 - phase]
        region = self.full.at[region_of(self.back[axis][k], p, phase)]
        remote(
            region, region, self.gather_s.at[p, phase, k], self.gather_r.at[p, phase, k], straight(self.ring[axis][k])
        ).wait_recv()
        return region

    def pair(self, p, k, plane):
        place = self.me if k == 3 else self.back[PORTIONS[p][2][0]][k]
        region = self.full.at[region_of(dict(place, c=plane), p, 2)]
        return remote(region, region, self.pair_s.at[p, k], self.pair_r.at[p, k], self.sibling)

    def spread(self):
        for phase in (1, 2):
            for p in range(3):
                for k in range(3):
                    self.take(p, phase - 1, k)
                self.send(p, phase)
                if phase == 2:
                    self.pair(p, 3, self.me["c"]).start()

    def forward(self):
        for k in (0, 2, 1):
            for p in range(3):
                self.take(p, 2, k)
                self.pair(p, k, self.me["c"]).start()

    def take_pair(self, plane):
        other = turned(self.sibling_real)
        for k in (3, 0, 2, 1):
            for p in range(3):
                axis = PORTIONS[p][2][0]
                place = other if k == 3 else moved(other, **{axis: 3 - k})
                region = self.full.at[region_of(dict(place, c=plane), p, 2)]
                remote(region, region, self.pair_s.at[p, k], self.pair_r.at[p, k], self.sibling).wait_recv()

    def core_copy(self, plane, part):
        cut = plane_cut(plane, part)
        return remote(
            self.partial.at[cut], self.core_in.at[cut[1:]], self.core_s.at[part], self.core_r.at[part], self.sibling
        )

    def core_sum(self, plane):
        for part in range(4):
            self.core_copy(plane, part).wait_recv()

            def add(row, carry, part=part):
                cut = (0, part, row) if plane == 0 else (1, row, part)
                both = self.partial[cut].astype(F32) + self.core_in[cut[1:]].astype(F32)
                self.partial[cut] = both.astype(BF16)
                return carry

            lax.fori_loop(0, 4, add, 0)

    def start(self, p, phase, source):
        axis = PORTIONS[p][2][phase]
        into = (self.in1, self.in2, self.in3)[phase][p]
        copies = []
        for k in range(3):
            to = self.ring[axis][k]
            copy = remote(
                source(to[axis]), into.at[k], self.sum_s.at[p, phase, k], self.sum_r.at[p, phase, k], straight(to)
            )
            copies.append(copy)
        return copies

    def first_sums(self, p):
        begin, width, order = PORTIONS[p]

        def source(target):
            index = [slice(None)] * 3
            index[DIMS.index(order[0])] = target
            return self.partial.at[(self.me["c"],) + tuple(index) + (slice(None), pl.ds(begin, width))]

        return self.start(p, 0, source)

    def sums(self, finish):
        me = self.me
        second, third = [], []
        for p in range(3):
            begin, width, order = PORTIONS[p]
            for copy in self.first_sums(p):
                copy.wait_recv()
            left = [name for name in DIMS if name != order[0]]

            def add(i, carry, p=p, begin=begin, width=width, order=order, left=left):
                index = {order[0]: me[order[0]], left[0]: i, left[1]: slice(None)}
                index = (me["c"],) + tuple(index[name] for name in DIMS) + (slice(None), pl.ds(begin, width))
                value = self.partial[index].astype(F32)
                for k in range(3):
                    value = value + self.in1[p][k, i].astype(F32)
                self.held2[p][i] = value.astype(BF16)
                return carry

            lax.fori_loop(0, 4, add, 0)
            if order[1] == left[0]:
                second.append(self.start(p, 1, lambda target, p=p: self.held2[p].at[target]))
            else:
                second.append(self.start(p, 1, lambda target, p=p: self.held2[p].at[:, target]))
            for copy in second[p]:
                copy.start()
        for p in range(3):
            begin, width, order = PORTIONS[p]
            for copy in second[p]:
                copy.wait_recv()
            left = [name for name in DIMS if name != order[0]]
            mine = me[order[1]]
            value = self.held2[p][mine] if order[1] == left[0] else self.held2[p][:, mine]
            value = value.astype(F32)
            for k in range(3):
                value = value + self.in2[p][k].astype(F32)
            self.held3[p][...] = value.astype(BF16)
            third.append(self.start(p, 2, lambda target, p=p: self.held3[p].at[target]))
            for copy in third[p]:
                copy.start()
        for p in range(3):
            begin, width, order = PORTIONS[p]
            for copy in third[p]:
                copy.wait_recv()
            value = self.held3[p][me[order[2]]].astype(F32)
            for k in range(3):
                value = value + self.in3[p][k].astype(F32)
            finish(p, begin, width, value + self.x[:, begin : begin + width])
        self.sends += second[0] + second[1] + second[2] + third[0] + third[1] + third[2]

    def run(self, multiply, activate, down):
        c = self.me["c"]
        self.spread()
        for plane in (0, 1):

            @pl.when(c == plane)
            def _():
                self.forward()

            @pl.when(c != plane)
            def _(plane=plane):
                self.take_pair(plane)

            self.acc[...] = jnp.zeros_like(self.acc)
            self.square[...] = jnp.zeros_like(self.square)

            def step(f, carry, plane=plane):
                part, ys = f // 2, pl.ds((f % 2) * 2, 2)
                rows = self.full[0, part, ys] if plane == 0 else self.full[1, :, part, ys]
                rows = rows.reshape(128, BLK)
                multiply(rows, pl.ds(pl.multiple_of(f * BLK, 128), BLK))
                plain = rows.astype(F32) * (1.0 / self.gain[pl.ds(f, 1), :])
                plain = plain * plain
                piece = plain[:, 0:128]
                for k in range(1, 7):
                    piece = piece + plain[:, k * 128 : (k + 1) * 128]
                self.square[...] += piece
                return carry

            lax.fori_loop(0, 8, step, 0)
            scale = lax.rsqrt(jnp.sum(self.square[...], axis=1, keepdims=True) * (1.0 / D) + EPSILON)
            act = activate(plane, scale)
            for part in range(4):
                for half in range(2):
                    block = down(act, part * 2 + half).astype(BF16)
                    shape = (2, 4, 16, BLK) if plane == 0 else (4, 2, 16, BLK)
                    self.partial[plane_cut(plane, part, half)] = block.reshape(shape)

                @pl.when(c != plane)
                def _(plane=plane, part=part):
                    self.core_copy(plane, part).start()

            @pl.when(c == plane)
            def _(plane=plane):
                self.core_sum(plane)
                for p in range(3):
                    for copy in self.first_sums(p):
                        copy.start()

    def end(self):
        c = self.me["c"]
        for copy in self.sends:
            copy.wait_send()
        for p in range(3):
            for k in range(4):
                self.pair(p, k, c).wait_send()
            for copy in self.first_sums(p):
                copy.wait_send()
        for plane in (0, 1):

            @pl.when(c != plane)
            def _(plane=plane):
                for part in range(4):
                    self.core_copy(plane, part).wait_send()


def silu(value):
    return value / (1.0 + jnp.exp(-value))


def ffn_kernel(
    x_ref, gain1_ref, gain2_ref, wr_ref, chosen_ref, wg1_hbm, wu1_hbm, wd1_hbm, wg2_hbm, wu2_hbm, wd2_hbm, out_ref,
    wg1, wu1, wd1, wg2, wu2, wd2, mid, router_acc, own, final_in, load_sem, final_s, final_r, *refs,
):
    here = coords()
    f_me = here["z"] * 2 + here["y"] // 2
    yh = here["y"] // 2
    me = turned(here)
    sibling = moved(here, c=1)
    pairs = ((wg1_hbm, wg1), (wu1_hbm, wu1), (wd1_hbm, wd1), (wg2_hbm, wg2), (wu2_hbm, wu2), (wd2_hbm, wd2))
    loads = [pltpu.make_async_copy(src, dst, load_sem.at[i]) for i, (src, dst) in enumerate(pairs)]
    for load in loads:
        load.start()
    half = len(refs) // 2
    dense = Layer(0, me, sibling, x_ref, gain1_ref, refs[:half])
    routed = Layer(1, me, sibling, mid, gain2_ref, refs[half:])
    dense.sibling_real = routed.sibling_real = sibling
    final_steps = [(dz, dy) for dy in (0, 2) for dz in range(4) if dz or dy]
    final_to = [moved(here, z=dz, y=dy) for dz, dy in final_steps]
    partners = [moved(here, **{name: step}) for name in DIMS for step in (1, 2, 3)] + [sibling]
    meet(partners + [moved(here, z=dz, y=2) for dz in (1, 2, 3)])

    for p in range(3):
        dense.begin(p, f_me)
    for load in loads[:3]:
        load.wait()

    def multiply_dense(rows, at):
        dense.acc[0] += dot_nt(rows, wg1[:, at])
        dense.acc[1] += dot_nt(rows, wu1[:, at])

    def activate_dense(plane, scale):
        return (silu(dense.acc[0] * scale) * (dense.acc[1] * scale)).astype(BF16)

    def down_dense(act, f):
        return dot(act, wd1[:, f * BLK : (f + 1) * BLK])

    dense.run(multiply_dense, activate_dense, down_dense)

    def between(p, begin, width, value):
        mid[:, begin : begin + width] = value
        routed.begin(p, f_me)

    dense.sums(between)
    for load in loads[3:]:
        load.wait()

    def multiply_routed(rows, at):
        routed.acc[0] += dot(rows, wg2[at, :])
        routed.acc[1] += dot(rows, wu2[at, :])
        router_acc[...] += dot_nt(rows, wr_ref[:, at])

    def activate_routed(plane, scale):
        affinity = 1.0 / (1.0 + jnp.exp(-(router_acc[...] * scale)))
        router_acc[...] = jnp.zeros_like(router_acc)
        chosen = chosen_ref[plane * 128 : plane * 128 + 128, 0:16].astype(F32)
        picked = jnp.where(chosen > 0.5, affinity, 0.0)
        below = jnp.sum(picked, axis=1, keepdims=True)
        mine = lax.broadcasted_iota(jnp.int32, (128, 16), 1) == here["z"] * 4 + here["y"]
        weight = ROUTE_SCALE * jnp.sum(jnp.where(mine, picked, 0.0), axis=1, keepdims=True) / below
        wanted = jnp.sum(jnp.where(mine, chosen, 0.0), axis=1, keepdims=True) > 0.5
        act = silu(routed.acc[0] * scale) * (routed.acc[1] * scale)
        return jnp.where(wanted, act * weight, 0.0).astype(BF16)

    def down_routed(act, f):
        return dot(act, wd2[:, f * BLK : (f + 1) * BLK])

    router_acc[...] = jnp.zeros_like(router_acc)
    routed.run(multiply_routed, activate_routed, down_routed)

    def last(p, begin, width, value):
        own[:, begin : begin + width] = value.astype(BF16)

    routed.sums(last)

    final_copies = []
    for i, to in enumerate(final_to):
        copy = remote(own, final_in.at[here["z"], yh], final_s.at[i], final_r.at[i], to)
        copy.start()
        final_copies.append(copy)
    final_in[here["z"], yh] = own[...]
    for copy in final_copies:
        copy.wait_recv()
    row = lax.broadcasted_iota(jnp.int32, (16, BLK), 0)
    for f in range(8):
        block = final_in[f // 2, f % 2].astype(F32)
        for t in range(2):
            out_ref[t : t + 1, f * BLK : (f + 1) * BLK] = jnp.sum(
                jnp.where(row == f_me * 2 + t, block, 0.0), axis=0, keepdims=True
            )
    for copy in final_copies:
        copy.wait_send()
    dense.end()
    routed.end()


def layer_scratch(hidden):
    dma = pltpu.SemaphoreType.DMA
    widths = [width for _, width, _ in PORTIONS]
    return (
        [
            pltpu.VMEM((2, 4, 4, 4, 16, BLK), BF16),
            pltpu.VMEM((2, 4, 4, 4, 16, BLK), BF16),
            pltpu.VMEM((4, 4, 4, 16, BLK), BF16),
            pltpu.VMEM((2, 128, hidden), F32),
            pltpu.VMEM((128, 128), F32),
        ]
        + [pltpu.VMEM((3, 4, 4, 16, width), BF16) for width in widths]
        + [pltpu.VMEM((4, 4, 16, width), BF16) for width in widths]
        + [pltpu.VMEM((3, 4, 16, width), BF16) for width in widths]
        + [pltpu.VMEM((4, 16, width), BF16) for width in widths]
        + [pltpu.VMEM((3, 16, width), BF16) for width in widths]
        + [
            dma((3, 3, 3)), dma((3, 3, 3)), dma((3, 4)), dma((3, 4)),
            dma((4,)), dma((4,)), dma((3, 3, 3)), dma((3, 3, 3)),
        ]
    )


def feed_forwards(shard, gain1, gain2, w_router, chosen, dense, expert):
    any_space = pl.BlockSpec(memory_space=pl.ANY)
    vmem = pl.BlockSpec(memory_space=pltpu.VMEM)
    dma = pltpu.SemaphoreType.DMA
    return pl.pallas_call(
        ffn_kernel,
        out_shape=jax.ShapeDtypeStruct((2, D), F32),
        in_specs=[vmem] * 5 + [any_space] * 6,
        out_specs=vmem,
        scratch_shapes=[pltpu.VMEM(w.shape, BF16) for w in dense + expert]
        + [
            pltpu.VMEM((16, BLK), F32),
            pltpu.VMEM((128, 16), F32),
            pltpu.VMEM((16, BLK), BF16),
            pltpu.VMEM((4, 2, 16, BLK), BF16),
            dma((6,)), dma((7,)), dma((7,)),
        ]
        + layer_scratch(dense[2].shape[0])
        + layer_scratch(expert[2].shape[0]),
        compiler_params=pltpu.CompilerParams(collective_id=1, has_side_effects=True, vmem_limit_bytes=VMEM_LIMIT),
        name="feed_forwards",
    )(shard, gain1, gain2, w_router, chosen, *dense, *expert)


def latent_attention(queries, cache, new_latent, lengths, latent_dim):
    score_scale = (VD + ROPE) ** (-0.5)
    scores = (
        jnp.einsum("thc,tlc->thl", queries, cache, preferred_element_type=jnp.float32) * score_scale
    )
    own_score = (
        jnp.einsum("thc,tc->th", queries, new_latent, preferred_element_type=jnp.float32)
        * score_scale
    )
    places = jnp.arange(cache.shape[1], dtype=jnp.int32)
    in_range = places[None, None, :] < lengths[:, None, None]
    scores = jnp.where(in_range, scores, -jnp.inf)
    peak = jnp.maximum(jnp.max(scores, axis=2), own_score)
    weights = jnp.exp(scores - peak[:, :, None])
    own_weight = jnp.exp(own_score - peak)
    sum_total = jnp.sum(weights, axis=2) + own_weight
    probability = (weights / sum_total[:, :, None]).astype(jnp.bfloat16)
    own_probability = (own_weight / sum_total).astype(jnp.bfloat16)
    context = jnp.einsum(
        "thl,tlc->thc", probability, cache[:, :, :latent_dim], preferred_element_type=jnp.float32
    )
    context = context + own_probability.astype(jnp.float32)[:, :, None] * new_latent[
        :, None, :latent_dim
    ].astype(jnp.float32)
    return context.astype(jnp.bfloat16)


def body(
    hidden,
    queries,
    cache,
    new_latent,
    lengths,
    w_values,
    w_out,
    gain_attn,
    w_dense_gate,
    w_dense_up,
    w_dense_down,
    gain_moe,
    w_router,
    expert_ids,
    w_expert_gate,
    w_expert_up,
    w_expert_down,
):
    context = latent_attention(queries, cache, new_latent, lengths, w_values.shape[1])
    after_attn, chosen = attn_exchange(
        context.reshape(2, 8, 16, 512), hidden, expert_ids, w_values, jnp.swapaxes(w_out, 1, 2)
    )
    out = feed_forwards(
        after_attn,
        gain_attn.reshape(8, BLK),
        gain_moe.reshape(8, BLK),
        w_router.T,
        chosen,
        (w_dense_gate.T, w_dense_up.T, w_dense_down),
        (w_expert_gate[0], w_expert_up[0], w_expert_down[0]),
    )
    return out.astype(BF16)


def solution(mesh):
    in_specs = (
        P(("tp", "ep"), None),
        P(("tp", "ep"), None, None),
        P(("tp", "ep"), None, None),
        P(("tp", "ep"), None),
        P(("tp", "ep")),
        P("tp", None, None),
        P("tp", None, "ep"),
        P(),
        P(None, ("tp", "ep")),
        P(None, ("tp", "ep")),
        P(("tp", "ep"), None),
        P(),
        P(),
        P(("tp", "ep"), None),
        P("ep", None, "tp"),
        P("ep", None, "tp"),
        P("ep", "tp", None),
    )
    out_specs = P(("tp", "ep"), None)
    return jax.shard_map(body, mesh=mesh, in_specs=in_specs, out_specs=out_specs, check_vma=False)
```

```python
import jax
import jax.numpy as jnp
from jax import lax
from jax.experimental import pallas as pl
from jax.experimental.pallas import tpu as pltpu
from jax.sharding import PartitionSpec as P

ROPE = 64
VD = 128
D = 7168
BLK = 896
UP_AT = 384
EPSILON = 1e-06
ROUTE_SCALE = 2.5
MESH = pl.DeviceIdType.MESH
F32 = jnp.float32
BF16 = jnp.bfloat16
VMEM_LIMIT = 60 * 2**20


PORTIONS = ((0, 384, ("x", "y", "z")), (384, 256, ("y", "z", "x")), (640, 256, ("z", "x", "y")))
DIMS = ("z", "y", "x")
PLANE = sorted(((i, j) for i in range(4) for j in range(4) if i or j), key=lambda d: -sum(min(k, 4 - k) for k in d))


def coords():
    tp, ep = lax.axis_index("tp"), lax.axis_index("ep")
    return dict(x=tp // 2, c=tp % 2, z=ep // 4, y=ep % 4)


def device(at):
    return (at["x"] * 2 + at["c"], at["z"] * 4 + at["y"])


def moved(at, **steps):
    new = dict(at)
    for name, step in steps.items():
        new[name] = lax.rem(at[name] + step, 2 if name == "c" else 4)
    return new


def meet(partners):
    barrier = pltpu.get_barrier_semaphore()
    for partner in partners:
        pl.semaphore_signal(barrier, inc=1, device_id=device(partner), device_id_type=MESH)
    pl.semaphore_wait(barrier, len(partners))


def remote(src, dst, send, recv, partner):
    return pltpu.make_async_remote_copy(
        src_ref=src, dst_ref=dst, send_sem=send, recv_sem=recv, device_id=device(partner), device_id_type=MESH
    )


def dot_nt(a, b):
    return lax.dot_general(a, b, (((1,), (1,)), ((), ())), preferred_element_type=F32)


def dot(a, b):
    return jnp.dot(a, b, preferred_element_type=F32)


def attn_kernel(
    ctx_ref, hid_ref, ids_ref, wv_hbm, wo_hbm, out_ref, chosen_ref,
    wv, wo, ctx_in, heads, part, part_in, hid_out, hid_in, mask_out, mask_in, load_sem,
    hid_s, hid_r, ctx_s, ctx_r, mask_s, mask_r, hv_s, hv_r, part_s, part_r,
):
    me = coords()
    x, c, z, y = me["x"], me["c"], me["z"], me["y"]
    yh, yl = y // 2, y % 2
    tp = x * 2 + c
    pad = pl.multiple_of(yl * 64, 64)
    load_wv = pltpu.make_async_copy(wv_hbm, wv, load_sem.at[0])
    load_wo = pltpu.make_async_copy(wo_hbm, wo.at[:, pl.ds(pad, 448), :], load_sem.at[1])
    load_wv.start()
    load_wo.start()
    wo[:, pl.ds(pl.multiple_of((1 - yl) * 448, 64), 64), :] = jnp.zeros((16, 64, 128), BF16)

    def at_tp(step):
        other = lax.rem(tp + step, 8)
        return dict(me, x=other // 2, c=other % 2)

    tp_steps = [(dt, dy) for dy in (0, 1) for dt in range(8) if dt or dy]
    part_to = [dict(at_tp(dt), y=yh * 2 + (yl + dy) % 2) for dt, dy in tp_steps]
    hid_steps = [(dz, dy) for dy in (0, 2) for dz in range(4) if dz or dy]
    hid_to = [moved(me, z=dz, y=dy) for dz, dy in hid_steps]
    other_odd = dict(me, y=lax.rem(yh * 2 + 2, 4) + (1 - yl))
    meet(part_to + hid_to + [other_odd])

    first = (z * 2 + yh) * 2
    row = lax.broadcasted_iota(jnp.int32, (16, BLK), 0)
    for f in range(8):
        both = hid_ref[:, f * BLK : (f + 1) * BLK].astype(F32)
        placed = jnp.where(row == first, both[0:1, :], jnp.where(row == first + 1, both[1:2, :], 0.0))
        hid_out[f // 2, f % 2] = placed.astype(BF16)
    lane = lax.broadcasted_iota(jnp.int32, (2, 128), 1)
    chosen = jnp.zeros((2, 128), F32)
    for k in range(ids_ref.shape[1]):
        chosen = chosen + jnp.where(ids_ref[:, k : k + 1] == lane, 1.0, 0.0)
    row = lax.broadcasted_iota(jnp.int32, (16, 128), 0)
    placed = jnp.where(row == tp * 2, chosen[0:1, :], jnp.where(row == tp * 2 + 1, chosen[1:2, :], 0.0))
    mask_out[...] = placed.astype(BF16)
    ctx_copies = []
    for step in range(1, 8):
        to = at_tp(step)
        copy = remote(ctx_ref.at[:, to["x"] * 2 + to["c"]], ctx_in.at[tp], ctx_s.at[step - 1], ctx_r.at[step - 1], to)
        copy.start()
        ctx_copies.append(copy)
    for step in range(1, 8):
        copy = remote(mask_out, mask_in.at[tp], mask_s.at[step - 1], mask_r.at[step - 1], at_tp(step))
        copy.start()
        ctx_copies.append(copy)
    hid_copies = []
    for i, to in enumerate(hid_to):
        copy = remote(hid_out.at[to["z"], to["y"] // 2], hid_in.at[z, yh], hid_s.at[i], hid_r.at[i], to)
        copy.start()
        hid_copies.append(copy)
    ctx_in[tp] = ctx_ref[:, tp]
    mask_in[tp] = mask_out[...]
    hid_in[z, yh] = hid_out[z, yh]
    for copy in ctx_copies:
        copy.wait_recv()
    load_wv.wait()

    i = lax.broadcasted_iota(jnp.int32, (256, 256), 0)
    j = lax.broadcasted_iota(jnp.int32, (256, 256), 1)
    turn = ((i & 15) * 16 + (i >> 4) == j).astype(BF16)
    by_head = dot(turn, ctx_in[...].reshape(256, 512)).astype(BF16)
    for h in range(16):
        heads[z, y, :, h * 128 : (h + 1) * 128] = dot(by_head[h * 16 : (h + 1) * 16, :], wv[h]).astype(BF16)

    heads[z, y, :, 2048:2176] = jnp.sum(mask_in[...].astype(F32), axis=0).astype(BF16)

    halves = ((0, "z", "y"), (1, "y", "z"))
    sends = []
    for half, one, two in halves:
        lanes = pl.ds(half * 1024, 1024 + half * 128)
        for step in range(1, 4):
            mine = heads.at[z, y, :, lanes]
            copy = remote(mine, mine, hv_s.at[half, 0, step - 1], hv_r.at[half, 0, step - 1], moved(me, **{one: step}))
            copy.start()
            sends.append(copy)
    for half, one, two in halves:
        lanes = pl.ds(half * 1024, 1024 + half * 128)
        for step in range(1, 4):
            sends[half * 3 + step - 1].wait_recv()
        for step in range(1, 4):
            slab = heads.at[:, y, :, lanes] if two == "y" else heads.at[z, :, :, lanes]
            copy = remote(slab, slab, hv_s.at[half, 1, step - 1], hv_r.at[half, 1, step - 1], moved(me, **{two: step}))
            copy.start()
            sends.append(copy)
    load_wo.wait()
    for copy in sends[6:]:
        copy.wait_recv()

    total = jnp.zeros((256, 512), F32)
    for pair in range(8):
        rows = heads[:, :, :, pair * 256 : (pair + 1) * 256].reshape(256, 256)
        weights = jnp.concatenate([wo[2 * pair], wo[2 * pair + 1]], axis=1)
        total = total + dot_nt(rows, weights)
    t, from_yh, from_z = i & 1, (i >> 1) & 1, (i >> 2) & 3
    source = from_z * 64 + (from_yh * 2 + (i >> 7)) * 16 + ((i >> 4) & 7) * 2 + t
    order = (source == j).astype(BF16)
    part[...] = dot(order, total.astype(BF16)).astype(BF16).reshape(2, 8, 16, 512)
    part_copies = []
    for i_to, to in enumerate(part_to):
        copy = remote(
            part.at[to["y"] % 2, to["x"] * 2 + to["c"]], part_in.at[yl, tp], part_s.at[i_to], part_r.at[i_to], to
        )
        copy.start()
        part_copies.append(copy)
    part_in[yl, tp] = part[yl, tp]
    plane = i >> 7
    to_yl = ((i >> 6) & 1) * (1 - plane) + ((i >> 4) & 1) * plane
    to_x = ((i >> 4) & 3) * (1 - plane) + ((i >> 5) & 3) * plane
    source = from_z * 64 + (from_yh * 2 + to_yl) * 16 + to_x * 4 + plane * 2 + t
    chosen_ref[...] = dot((source == j).astype(BF16), heads[:, :, :, 2048:2176].reshape(256, 128)).astype(BF16)
    for copy in hid_copies:
        copy.wait_recv()
    out_ref[...] = jnp.sum(hid_in[...].astype(F32), axis=(0, 1))
    for copy in part_copies:
        copy.wait_recv()
    sums = jnp.sum(part_in[...].astype(F32), axis=1)
    out_ref[:, 0:512] += sums[0]
    out_ref[:, 384:896] += sums[1]
    for copy in ctx_copies + hid_copies + sends + part_copies:
        copy.wait_send()


def attn_exchange(context, hidden, ids, w_values, w_out):
    any_space = pl.BlockSpec(memory_space=pl.ANY)
    vmem = pl.BlockSpec(memory_space=pltpu.VMEM)
    dma = pltpu.SemaphoreType.DMA
    return pl.pallas_call(
        attn_kernel,
        out_shape=(jax.ShapeDtypeStruct((16, BLK), F32), jax.ShapeDtypeStruct((256, 128), BF16)),
        in_specs=[vmem, vmem, vmem, any_space, any_space],
        out_specs=(vmem, vmem),
        scratch_shapes=[
            pltpu.VMEM((16, 512, 128), BF16),
            pltpu.VMEM((16, 512, 128), BF16),
            pltpu.VMEM((8, 2, 16, 512), BF16),
            pltpu.VMEM((4, 4, 16, 2176), BF16),
            pltpu.VMEM((2, 8, 16, 512), BF16),
            pltpu.VMEM((2, 8, 16, 512), BF16),
            pltpu.VMEM((4, 2, 16, BLK), BF16),
            pltpu.VMEM((4, 2, 16, BLK), BF16),
            pltpu.VMEM((16, 128), BF16),
            pltpu.VMEM((8, 16, 128), BF16),
            dma((2,)),
            dma((7,)), dma((7,)), dma((7,)), dma((7,)), dma((7,)), dma((7,)),
            dma((2, 2, 3)), dma((2, 2, 3)), dma((15,)), dma((15,)),
        ],
        compiler_params=pltpu.CompilerParams(collective_id=0, has_side_effects=True, vmem_limit_bytes=VMEM_LIMIT),
        name="attn_exchange",
    )(context, hidden, ids, w_values, w_out)


def turned(at):
    c = at["c"]
    return dict(
        z=at["z"] * (1 - c) + at["x"] * c, y=at["y"] * (1 - c) + at["z"] * c, x=at["x"] * (1 - c) + at["y"] * c, c=c
    )


def straight(at):
    c = at["c"]
    return dict(
        z=at["z"] * (1 - c) + at["y"] * c, y=at["y"] * (1 - c) + at["x"] * c, x=at["x"] * (1 - c) + at["z"] * c, c=c
    )


def region_of(at, portion, phase):
    start, width, order = PORTIONS[portion]
    done = order[::-1][:phase]
    index = tuple(pl.ds(0, 4) if name in done else at[name] for name in DIMS)
    return index + (slice(None), pl.ds(start, width))


def plane_cut(plane, part, ys):
    return (part, ys) if plane == 0 else (slice(None), part, ys)


class Layer:
    def __init__(self, me, x_ref, gain_ref, refs):
        self.me, self.x, self.gain = me, x_ref, gain_ref
        self.full, self.partial, self.acc, self.square, *lists = refs
        (
            self.plane_s, self.plane_r, self.slab_s, self.slab_r, self.sum_s, self.sum_r, self.last_s, self.last_r
        ) = lists[9:]
        self.in1, self.held2, self.in2 = [lists[i * 3 : i * 3 + 3] for i in range(3)]
        self.ring = {name: [moved(me, **{name: step}) for step in (1, 2, 3)] for name in DIMS}
        self.back = {name: [moved(me, **{name: 4 - step}) for step in (1, 2, 3)] for name in DIMS}
        self.sends = []

    def begin(self, p, f_me):
        start, width, order = PORTIONS[p]
        me = self.me
        lanes = pl.ds(start, width)
        scaled = self.x[:, lanes] * self.gain[:, pl.ds(pl.multiple_of(f_me * BLK + start, 128), width)]
        self.full[me["z"], me["y"], me["x"], :, lanes] = scaled.astype(BF16)
        region = self.full.at[region_of(me, p, 0)]
        for k, step in enumerate(PLANE):
            to = straight(moved(me, **dict(zip(order[1:], step))))
            copy = remote(region, region, self.plane_s.at[p, k], self.plane_r.at[p, k], to)
            copy.start()
            self.sends.append(copy)

    def gather(self):
        me = self.me
        for p in range(3):
            start, width, order = PORTIONS[p]
            for k, step in enumerate(PLANE):
                there = moved(me, **{name: 4 - by for name, by in zip(order[1:], step)})
                region = self.full.at[region_of(there, p, 0)]
                remote(region, region, self.plane_s.at[p, k], self.plane_r.at[p, k], straight(me)).wait_recv()
            region = self.full.at[region_of(me, p, 2)]
            for k in range(3):
                to = straight(self.ring[order[0]][k])
                copy = remote(region, region, self.slab_s.at[p, k], self.slab_r.at[p, k], to)
                copy.start()
                self.sends.append(copy)
        for k in (0, 2, 1):
            for p in range(3):
                axis = PORTIONS[p][2][0]
                region = self.full.at[region_of(self.back[axis][k], p, 2)]
                remote(region, region, self.slab_s.at[p, k], self.slab_r.at[p, k], straight(me)).wait_recv()

    def first_sums(self, p):
        begin, width, order = PORTIONS[p]
        copies = []
        for k in range(3):
            to = self.ring[order[0]][k]
            index = [slice(None)] * 3
            index[DIMS.index(order[0])] = to[order[0]]
            source = self.partial.at[tuple(index) + (slice(None), pl.ds(begin, width))]
            copies.append(remote(source, self.in1[p].at[k], self.sum_s.at[p, k], self.sum_r.at[p, k], straight(to)))
        return copies

    def sums(self, finish):
        me = self.me
        second = []
        for p in range(3):
            begin, width, order = PORTIONS[p]
            for copy in self.first_sums(p):
                copy.wait_recv()
            left = [name for name in DIMS if name != order[0]]

            def add(i, carry, p=p, begin=begin, width=width, order=order, left=left):
                index = {order[0]: me[order[0]], left[0]: i, left[1]: slice(None)}
                index = tuple(index[name] for name in DIMS) + (slice(None), pl.ds(begin, width))
                value = self.partial[index].astype(F32)
                for k in range(3):
                    value = value + self.in1[p][k, i].astype(F32)
                self.held2[p][i] = value.astype(BF16)
                return carry

            lax.fori_loop(0, 4, add, 0)
            copies = []
            for k, step in enumerate(PLANE):
                to = moved(me, **dict(zip(left, step)))
                source = self.held2[p].at[to[left[0]], to[left[1]]]
                copy = remote(source, self.in2[p].at[k], self.last_s.at[p, k], self.last_r.at[p, k], straight(to))
                copy.start()
                copies.append(copy)
            second.append(copies)
        for p in range(3):
            begin, width, order = PORTIONS[p]
            for copy in second[p]:
                copy.wait_recv()
            left = [name for name in DIMS if name != order[0]]
            value = self.held2[p][me[left[0]], me[left[1]]].astype(F32)
            value = value + jnp.sum(self.in2[p][...].astype(F32), axis=0)
            finish(p, begin, width, value + self.x[:, begin : begin + width])
            self.sends += second[p]

    def run(self, multiply, activate, down, weights):
        self.gather()
        for wait in weights:
            wait()
        for plane in (0, 1):

            @pl.when(self.me["c"] == plane)
            def _(plane=plane):
                self.acc[...] = jnp.zeros_like(self.acc)
                self.square[...] = jnp.zeros_like(self.square)

                def step(f, carry):
                    rows = self.full[plane_cut(plane, f // 2, pl.ds((f % 2) * 2, 2))].reshape(128, BLK)
                    at = pl.ds(pl.multiple_of(f * BLK, 128), BLK)
                    multiply(rows, at)
                    plain = rows.astype(F32) * (1.0 / self.gain[:, at])
                    plain = plain * plain
                    piece = plain[:, 0:128]
                    for k in range(1, 7):
                        piece = piece + plain[:, k * 128 : (k + 1) * 128]
                    self.square[...] += piece
                    return carry

                lax.fori_loop(0, 8, step, 0)
                scale = lax.rsqrt(jnp.sum(self.square[...], axis=1, keepdims=True) * (1.0 / D) + EPSILON)
                act = activate(plane, scale)
                for f in range(8):
                    block = down(act, f).astype(BF16)
                    shape = (2, 4, 16, BLK) if plane == 0 else (4, 2, 16, BLK)
                    ys = slice(f % 2 * 2, f % 2 * 2 + 2)
                    self.partial[plane_cut(plane, f // 2, ys)] = block.reshape(shape)

        for p in range(3):
            for copy in self.first_sums(p):
                copy.start()

    def end(self):
        for copy in self.sends:
            copy.wait_send()
        for p in range(3):
            for copy in self.first_sums(p):
                copy.wait_send()


def silu(value):
    return value / (1.0 + jnp.exp(-value))


def ffn_kernel(
    x_ref, gain1_ref, gain2_ref, wr_ref, chosen_ref, wg1_hbm, wu1_hbm, wd1_hbm, wg2_hbm, wu2_hbm, wd2_hbm, out_ref,
    up1, down1, up2, down2, mid, router_acc, own, final_in, load_sem, give_s, give_r, final_s, final_r, *refs,
):
    here = coords()
    f_me = here["z"] * 2 + here["y"] // 2
    yh = here["y"] // 2
    me = turned(here)
    sibling = moved(here, c=1)
    n1, n2 = wd1_hbm.shape[0], wd2_hbm.shape[0]
    sources = (wg1_hbm, wu1_hbm, wd1_hbm, wg2_hbm, wu2_hbm, wd2_hbm)

    def places(k):
        return (
            up1.at[pl.ds(k * n1, n1), :], up1.at[pl.ds(UP_AT + k * n1, n1), :], down1.at[pl.ds(k * n1, n1), :],
            up2.at[k], up2.at[2 + k], down2.at[pl.ds(k * n2, n2), :],
        )

    loads = [pltpu.make_async_copy(src, dst, load_sem.at[i]) for i, (src, dst) in enumerate(zip(sources, places(0)))]
    gives = [
        remote(src, dst, give_s.at[i], give_r.at[i], sibling) for i, (src, dst) in enumerate(zip(sources, places(1)))
    ]
    for load in loads:
        load.start()
    half = len(refs) // 2
    dense = Layer(me, x_ref, gain1_ref, refs[:half])
    routed = Layer(me, mid, gain2_ref, refs[half:])
    final_steps = [(dz, dy) for dy in (0, 2) for dz in range(4) if dz or dy]
    final_to = [moved(here, z=dz, y=dy) for dz, dy in final_steps]
    partners = [moved(here, **{name: step}) for name in DIMS for step in (1, 2, 3)] + [sibling]
    for one, two in (("x", "y"), ("y", "z"), ("z", "x")):
        partners += [moved(here, **{one: i, two: j}) for i in (1, 2, 3) for j in (1, 2, 3)]
    meet(partners)

    for p in range(3):
        dense.begin(p, f_me)
    for give in gives:
        give.start()
    for first in (2 * n1, UP_AT + 2 * n1):
        up1[first : first + UP_AT - 2 * n1, :] = jnp.zeros((UP_AT - 2 * n1, D), BF16)

    def multiply_dense(rows, at):
        dense.acc[...] += dot_nt(rows, up1[:, at])

    def activate_dense(plane, scale):
        gate, up = dense.acc[:, 0 : 2 * n1], dense.acc[:, UP_AT : UP_AT + 2 * n1]
        return (silu(gate * scale) * (up * scale)).astype(BF16)

    def down_dense(act, f):
        return dot(act, down1[:, f * BLK : (f + 1) * BLK])

    dense.run(multiply_dense, activate_dense, down_dense, [q.wait for q in loads[:3]] + [q.wait_recv for q in gives[:3]])

    def between(p, begin, width, value):
        mid[:, begin : begin + width] = value
        routed.begin(p, f_me)

    dense.sums(between)
    def multiply_routed(rows, at):
        for k in range(4):
            routed.acc[:, k * n2 : (k + 1) * n2] += dot(rows, up2[k, at, :])
        router_acc[...] += dot_nt(rows, wr_ref[:, at])

    def activate_routed(plane, scale):
        affinity = 1.0 / (1.0 + jnp.exp(-(router_acc[...] * scale)))
        router_acc[...] = jnp.zeros_like(router_acc)
        chosen = chosen_ref[plane * 128 : plane * 128 + 128, 0:16].astype(F32)
        picked = jnp.where(chosen > 0.5, affinity, 0.0)
        below = jnp.sum(picked, axis=1, keepdims=True)
        mine = lax.broadcasted_iota(jnp.int32, (128, 16), 1) == here["z"] * 4 + here["y"]
        weight = ROUTE_SCALE * jnp.sum(jnp.where(mine, picked, 0.0), axis=1, keepdims=True) / below
        wanted = jnp.sum(jnp.where(mine, chosen, 0.0), axis=1, keepdims=True) > 0.5
        act = silu(routed.acc[:, : 2 * n2] * scale) * (routed.acc[:, 2 * n2 :] * scale)
        return jnp.where(wanted, act * weight, 0.0).astype(BF16)

    def down_routed(act, f):
        return dot(act, down2[:, f * BLK : (f + 1) * BLK])

    router_acc[...] = jnp.zeros_like(router_acc)
    routed.run(multiply_routed, activate_routed, down_routed, [q.wait for q in loads[3:]] + [q.wait_recv for q in gives[3:]])

    def last(p, begin, width, value):
        own[:, begin : begin + width] = value.astype(BF16)

    routed.sums(last)

    final_copies = []
    for i, to in enumerate(final_to):
        copy = remote(own, final_in.at[here["z"], yh], final_s.at[i], final_r.at[i], to)
        copy.start()
        final_copies.append(copy)
    final_in[here["z"], yh] = own[...]
    for copy in final_copies:
        copy.wait_recv()
    row = lax.broadcasted_iota(jnp.int32, (16, BLK), 0)
    for f in range(8):
        block = final_in[f // 2, f % 2].astype(F32)
        both = [jnp.sum(jnp.where(row == f_me * 2 + t, block, 0.0), axis=0, keepdims=True) for t in range(2)]
        out_ref[:, f * BLK : (f + 1) * BLK] = jnp.concatenate(both, axis=0).astype(BF16)
    for copy in final_copies:
        copy.wait_send()
    for give in gives:
        give.wait_send()
    dense.end()
    routed.end()


def layer_scratch(columns):
    dma = pltpu.SemaphoreType.DMA
    widths = [width for _, width, _ in PORTIONS]
    return (
        [
            pltpu.VMEM((4, 4, 4, 16, BLK), BF16),
            pltpu.VMEM((4, 4, 4, 16, BLK), BF16),
            pltpu.VMEM((128, columns), F32),
            pltpu.VMEM((128, 128), F32),
        ]
        + [pltpu.VMEM((3, 4, 4, 16, width), BF16) for width in widths]
        + [pltpu.VMEM((4, 4, 16, width), BF16) for width in widths]
        + [pltpu.VMEM((15, 16, width), BF16) for width in widths]
        + [dma((3, 15)), dma((3, 15)), dma((3, 3)), dma((3, 3)), dma((3, 3)), dma((3, 3)), dma((3, 15)), dma((3, 15))]
    )


def feed_forwards(shard, gain1, gain2, w_router, chosen, dense, expert):
    any_space = pl.BlockSpec(memory_space=pl.ANY)
    vmem = pl.BlockSpec(memory_space=pltpu.VMEM)
    dma = pltpu.SemaphoreType.DMA
    n1, n2 = dense[2].shape[0], expert[2].shape[0]
    return pl.pallas_call(
        ffn_kernel,
        out_shape=jax.ShapeDtypeStruct((2, D), BF16),
        in_specs=[vmem] * 5 + [any_space] * 6,
        out_specs=vmem,
        scratch_shapes=[
            pltpu.VMEM((2 * UP_AT, D), BF16),
            pltpu.VMEM((2 * n1, D), BF16),
            pltpu.VMEM((4, D, n2), BF16),
            pltpu.VMEM((2 * n2, D), BF16),
            pltpu.VMEM((16, BLK), F32),
            pltpu.VMEM((128, 16), F32),
            pltpu.VMEM((16, BLK), BF16),
            pltpu.VMEM((4, 2, 16, BLK), BF16),
            dma((6,)), dma((6,)), dma((6,)), dma((7,)), dma((7,)),
        ]
        + layer_scratch(2 * UP_AT)
        + layer_scratch(4 * n2),
        compiler_params=pltpu.CompilerParams(collective_id=1, has_side_effects=True, vmem_limit_bytes=VMEM_LIMIT),
        name="feed_forwards",
    )(shard, gain1, gain2, w_router, chosen, *dense, *expert)


def latent_attention(queries, cache, new_latent, lengths, latent_dim):
    score_scale = (VD + ROPE) ** (-0.5)
    scores = (
        jnp.einsum("thc,tlc->thl", queries, cache, preferred_element_type=jnp.float32) * score_scale
    )
    own_score = (
        jnp.einsum("thc,tc->th", queries, new_latent, preferred_element_type=jnp.float32)
        * score_scale
    )
    places = jnp.arange(cache.shape[1], dtype=jnp.int32)
    in_range = places[None, None, :] < lengths[:, None, None]
    scores = jnp.where(in_range, scores, -jnp.inf)
    peak = jnp.maximum(jnp.max(scores, axis=2), own_score)
    weights = jnp.exp(scores - peak[:, :, None])
    own_weight = jnp.exp(own_score - peak)
    sum_total = jnp.sum(weights, axis=2) + own_weight
    probability = (weights / sum_total[:, :, None]).astype(jnp.bfloat16)
    own_probability = (own_weight / sum_total).astype(jnp.bfloat16)
    context = jnp.einsum(
        "thl,tlc->thc", probability, cache[:, :, :latent_dim], preferred_element_type=jnp.float32
    )
    context = context + own_probability.astype(jnp.float32)[:, :, None] * new_latent[
        :, None, :latent_dim
    ].astype(jnp.float32)
    return context.astype(jnp.bfloat16)


def body(
    hidden,
    queries,
    cache,
    new_latent,
    lengths,
    w_values,
    w_out,
    gain_attn,
    w_dense_gate,
    w_dense_up,
    w_dense_down,
    gain_moe,
    w_router,
    expert_ids,
    w_expert_gate,
    w_expert_up,
    w_expert_down,
):
    context = latent_attention(queries, cache, new_latent, lengths, w_values.shape[1])
    after_attn, chosen = attn_exchange(
        context.reshape(2, 8, 16, 512), hidden, expert_ids, w_values, jnp.swapaxes(w_out, 1, 2)
    )
    out = feed_forwards(
        after_attn,
        gain_attn.reshape(1, D),
        gain_moe.reshape(1, D),
        w_router.T,
        chosen,
        (w_dense_gate.T, w_dense_up.T, w_dense_down),
        (w_expert_gate[0], w_expert_up[0], w_expert_down[0]),
    )
    return out


def solution(mesh):
    in_specs = (
        P(("tp", "ep"), None),
        P(("tp", "ep"), None, None),
        P(("tp", "ep"), None, None),
        P(("tp", "ep"), None),
        P(("tp", "ep")),
        P("tp", None, None),
        P("tp", None, "ep"),
        P(),
        P(None, ("tp", "ep")),
        P(None, ("tp", "ep")),
        P(("tp", "ep"), None),
        P(),
        P(),
        P(("tp", "ep"), None),
        P("ep", None, "tp"),
        P("ep", None, "tp"),
        P("ep", "tp", None),
    )
    out_specs = P(("tp", "ep"), None)
    return jax.shard_map(body, mesh=mesh, in_specs=in_specs, out_specs=out_specs, check_vma=False)
```

```python
import jax
import jax.numpy as jnp
from jax import lax
from jax.experimental import pallas as pl
from jax.experimental.pallas import tpu as pltpu
from jax.sharding import PartitionSpec as P

ROPE = 64
VD = 128
D = 7168
BLK = 896
UP_AT = 384
EPSILON = 1e-06
ROUTE_SCALE = 2.5
MESH = pl.DeviceIdType.MESH
F32 = jnp.float32
BF16 = jnp.bfloat16
VMEM_LIMIT = 60 * 2**20


PORTIONS = ((0, 384, ("x", "y", "z")), (384, 256, ("y", "z", "x")), (640, 256, ("z", "x", "y")))
DIMS = ("z", "y", "x")
PLANE = sorted(((i, j) for i in range(4) for j in range(4) if i or j), key=lambda d: -sum(min(k, 4 - k) for k in d))


def coords():
    tp, ep = lax.axis_index("tp"), lax.axis_index("ep")
    return dict(x=tp // 2, c=tp % 2, z=ep // 4, y=ep % 4)


def device(at):
    return (at["x"] * 2 + at["c"], at["z"] * 4 + at["y"])


def moved(at, **steps):
    new = dict(at)
    for name, step in steps.items():
        new[name] = lax.rem(at[name] + step, 2 if name == "c" else 4)
    return new


def greet(partners):
    barrier = pltpu.get_barrier_semaphore()
    for partner in partners:
        pl.semaphore_signal(barrier, inc=1, device_id=device(partner), device_id_type=MESH)


def gathered(partners):
    pl.semaphore_wait(pltpu.get_barrier_semaphore(), len(partners))


def remote(src, dst, send, recv, partner):
    return pltpu.make_async_remote_copy(
        src_ref=src, dst_ref=dst, send_sem=send, recv_sem=recv, device_id=device(partner), device_id_type=MESH
    )


def dot_nt(a, b):
    return lax.dot_general(a, b, (((1,), (1,)), ((), ())), preferred_element_type=F32)


def dot(a, b):
    return jnp.dot(a, b, preferred_element_type=F32)


def attend(t, q, cache, latent, length):
    scale = (VD + ROPE) ** (-0.5)
    scores = lax.dot_general(q[t], cache[t], (((0,), (0,)), ((), ())), preferred_element_type=F32) * scale
    own = lax.dot_general(q[t], latent, (((0,), (1,)), ((), ())), preferred_element_type=F32) * scale
    own = own[:, t : t + 1]
    place = lax.broadcasted_iota(jnp.int32, scores.shape, 1)
    scores = jnp.where(place < length, scores, -jnp.inf)
    peak = jnp.maximum(jnp.max(scores, axis=1, keepdims=True), own)
    weights = jnp.exp(scores - peak)
    own_weight = jnp.exp(own - peak)
    total = jnp.sum(weights, axis=1, keepdims=True) + own_weight
    probability = (weights / total).astype(BF16)
    own_probability = (own_weight / total).astype(BF16).astype(F32)
    context = dot_nt(probability, cache[t, 0:512, :])
    return (context + own_probability * latent[t : t + 1, 0:512].astype(F32)).astype(BF16)


def attention_part(me, len_ref, nl_ref, hid_ref, ids_ref, wv_hbm, wo_hbm, q_hbm, cache_hbm, shard, chosen_all, refs, meeting, early):
    (
        q, cache, latent, ctx, wv, wo, ctx_in, heads, part, part_in, hid_out, hid_in, mask_out, mask_in, load_sem,
        hid_s, hid_r, ctx_s, ctx_r, mask_s, mask_r, hv_s, hv_r, hw_s, hw_r, part_s, part_r,
    ) = refs
    x, c, z, y = me["x"], me["c"], me["z"], me["y"]
    yh, yl = y // 2, y % 2
    tp = x * 2 + c
    pad = pl.multiple_of(yl * 64, 64)
    requests = []
    for t in range(2):
        pairs = ((q_hbm.at[t], q.at[t]), (cache_hbm.at[t], cache.at[t]))
        requests.append([pltpu.make_async_copy(src, dst, load_sem.at[t * 2 + k]) for k, (src, dst) in enumerate(pairs)])
    load_wv = pltpu.make_async_copy(wv_hbm, wv, load_sem.at[4])
    load_wo = pltpu.make_async_copy(wo_hbm, wo.at[:, pl.ds(pad, 448), :], load_sem.at[5])
    for load in requests[0] + requests[1] + [load_wv, load_wo]:
        load.start()

    def at_tp(step):
        other = lax.rem(tp + step, 8)
        return dict(me, x=other // 2, c=other % 2)

    tp_steps = [(dt, dy) for dy in (0, 1) for dt in range(8) if dt or dy]
    part_to = [dict(at_tp(dt), y=yh * 2 + (yl + dy) % 2) for dt, dy in tp_steps]
    hid_steps = [(dz, dy) for dy in (0, 2) for dz in range(4) if dz or dy]
    hid_to = [moved(me, z=dz, y=dy) for dz, dy in hid_steps]
    greet(meeting)
    wo[:, pl.ds(pl.multiple_of((1 - yl) * 448, 64), 64), :] = jnp.zeros((16, 64, 128), BF16)
    latent[...] = jnp.zeros_like(latent)
    latent[0:2, :] = nl_ref[...].astype(F32)
    latents = latent[...].astype(BF16)
    for t in range(2):
        for load in requests[t]:
            load.wait()
        ctx[t] = attend(t, q, cache, latents, len_ref[t]).reshape(8, 16, 512)

    first = (z * 2 + yh) * 2
    row = lax.broadcasted_iota(jnp.int32, (16, BLK), 0)
    for f in range(8):
        both = hid_ref[:, f * BLK : (f + 1) * BLK].astype(F32)
        placed = jnp.where(row == first, both[0:1, :], jnp.where(row == first + 1, both[1:2, :], 0.0))
        hid_out[f // 2, f % 2] = placed.astype(BF16)
    lane = lax.broadcasted_iota(jnp.int32, (2, 128), 1)
    chosen = jnp.zeros((2, 128), F32)
    for k in range(ids_ref.shape[1]):
        chosen = chosen + jnp.where(ids_ref[:, k : k + 1] == lane, 1.0, 0.0)
    row = lax.broadcasted_iota(jnp.int32, (16, 128), 0)
    placed = jnp.where(row == tp * 2, chosen[0:1, :], jnp.where(row == tp * 2 + 1, chosen[1:2, :], 0.0))
    mask_out[...] = placed.astype(BF16)
    gathered(meeting)
    ctx_copies = []
    for step in range(1, 8):
        to = at_tp(step)
        copy = remote(ctx.at[:, to["x"] * 2 + to["c"]], ctx_in.at[tp], ctx_s.at[step - 1], ctx_r.at[step - 1], to)
        copy.start()
        ctx_copies.append(copy)
    for step in range(1, 8):
        copy = remote(mask_out, mask_in.at[tp], mask_s.at[step - 1], mask_r.at[step - 1], at_tp(step))
        copy.start()
        ctx_copies.append(copy)
    hid_copies = []
    for i, to in enumerate(hid_to):
        copy = remote(hid_out.at[to["z"], to["y"] // 2], hid_in.at[z, yh], hid_s.at[i], hid_r.at[i], to)
        copy.start()
        hid_copies.append(copy)
    ctx_in[tp] = ctx[:, tp]
    mask_in[tp] = mask_out[...]
    hid_in[z, yh] = hid_out[z, yh]
    for copy in ctx_copies:
        copy.wait_recv()
    load_wv.wait()
    early()

    i = lax.broadcasted_iota(jnp.int32, (256, 256), 0)
    j = lax.broadcasted_iota(jnp.int32, (256, 256), 1)
    turn = ((i & 15) * 16 + (i >> 4) == j).astype(BF16)
    by_head = dot(turn, ctx_in[...].reshape(256, 512)).astype(BF16)
    halves = ((0, "z", "y"), (1, "y", "z"))
    sends = []

    def lanes_of(half):
        return pl.ds(half * 1024, 1024 + half * 128)

    for half, one, two in halves:
        for h in range(half * 8, half * 8 + 8):
            heads[z, y, :, h * 128 : (h + 1) * 128] = dot(by_head[h * 16 : (h + 1) * 16, :], wv[h]).astype(BF16)
        if half:
            heads[z, y, :, 2048:2176] = jnp.sum(mask_in[...].astype(F32), axis=0).astype(BF16)
        mine = heads.at[z, y, :, lanes_of(half)]
        for k in (2, 1, 3):
            to = moved(me, **{one: k})
            sends.append(remote(mine, mine, hv_s.at[half, k - 1], hv_r.at[half, k - 1], to))
            sends[-1].start()
        for k in (2, 1, 3):
            to = moved(me, **{two: k})
            sends.append(remote(mine, mine, hw_s.at[half, 0, k - 1], hw_r.at[half, 0, k - 1], to))
            sends[-1].start()
    for k in (1, 3, 2):
        for half, one, two in halves:
            there = moved(me, **{one: 4 - k})
            piece = heads.at[there["z"], there["y"], :, lanes_of(half)]
            remote(piece, piece, hv_s.at[half, k - 1], hv_r.at[half, k - 1], me).wait_recv()
            for hop in (2, 1, 3):
                to = moved(me, **{two: hop})
                sends.append(remote(piece, piece, hw_s.at[half, k, hop - 1], hw_r.at[half, k, hop - 1], to))
                sends[-1].start()
    load_wo.wait()

    total = jnp.zeros((256, 512), F32)
    for half, one, two in halves:
        for k in range(4):
            for hop in (1, 3, 2):
                there = moved(me, **{one: (4 - k) % 4, two: 4 - hop})
                piece = heads.at[there["z"], there["y"], :, lanes_of(half)]
                remote(piece, piece, hw_s.at[half, k, hop - 1], hw_r.at[half, k, hop - 1], me).wait_recv()
        for pair in range(half * 4, half * 4 + 4):
            rows = heads[:, :, :, pair * 256 : (pair + 1) * 256].reshape(256, 256)
            weights = jnp.concatenate([wo[2 * pair], wo[2 * pair + 1]], axis=1)
            total = total + dot_nt(rows, weights)
    t, from_yh, from_z = i & 1, (i >> 1) & 1, (i >> 2) & 3
    source = from_z * 64 + (from_yh * 2 + (i >> 7)) * 16 + ((i >> 4) & 7) * 2 + t
    order = (source == j).astype(BF16)
    part[...] = dot(order, total.astype(BF16)).astype(BF16).reshape(2, 8, 16, 512)
    part_copies = []
    for i_to, to in enumerate(part_to):
        copy = remote(
            part.at[to["y"] % 2, to["x"] * 2 + to["c"]], part_in.at[yl, tp], part_s.at[i_to], part_r.at[i_to], to
        )
        copy.start()
        part_copies.append(copy)
    part_in[yl, tp] = part[yl, tp]
    plane = i >> 7
    to_yl = ((i >> 6) & 1) * (1 - plane) + ((i >> 4) & 1) * plane
    to_x = ((i >> 4) & 3) * (1 - plane) + ((i >> 5) & 3) * plane
    source = from_z * 64 + (from_yh * 2 + to_yl) * 16 + to_x * 4 + plane * 2 + t
    chosen_all[...] = dot((source == j).astype(BF16), heads[:, :, :, 2048:2176].reshape(256, 128)).astype(BF16)
    for copy in hid_copies:
        copy.wait_recv()
    shard[...] = jnp.sum(hid_in[...].astype(F32), axis=(0, 1))
    for copy in part_copies:
        copy.wait_recv()
    sums = jnp.sum(part_in[...].astype(F32), axis=1)
    shard[:, 0:512] += sums[0]
    shard[:, 384:896] += sums[1]
    return ctx_copies + hid_copies + sends + part_copies


def attention_scratch():
    dma = pltpu.SemaphoreType.DMA
    return [
        pltpu.VMEM((2, 576, 128), BF16),
        pltpu.VMEM((2, 576, 1024), BF16),
        pltpu.VMEM((16, 576), F32),
        pltpu.VMEM((2, 8, 16, 512), BF16),
        pltpu.VMEM((16, 512, 128), BF16),
        pltpu.VMEM((16, 512, 128), BF16),
        pltpu.VMEM((8, 2, 16, 512), BF16),
        pltpu.VMEM((4, 4, 16, 2176), BF16),
        pltpu.VMEM((2, 8, 16, 512), BF16),
        pltpu.VMEM((2, 8, 16, 512), BF16),
        pltpu.VMEM((4, 2, 16, BLK), BF16),
        pltpu.VMEM((4, 2, 16, BLK), BF16),
        pltpu.VMEM((16, 128), BF16),
        pltpu.VMEM((8, 16, 128), BF16),
        dma((6,)),
        dma((7,)), dma((7,)), dma((7,)), dma((7,)), dma((7,)), dma((7,)),
        dma((2, 3)), dma((2, 3)), dma((2, 4, 3)), dma((2, 4, 3)), dma((15,)), dma((15,)),
    ]


def turned(at):
    c = at["c"]
    return dict(
        z=at["z"] * (1 - c) + at["x"] * c, y=at["y"] * (1 - c) + at["z"] * c, x=at["x"] * (1 - c) + at["y"] * c, c=c
    )


def straight(at):
    c = at["c"]
    return dict(
        z=at["z"] * (1 - c) + at["y"] * c, y=at["y"] * (1 - c) + at["x"] * c, x=at["x"] * (1 - c) + at["z"] * c, c=c
    )


def region_of(at, portion, phase):
    start, width, order = PORTIONS[portion]
    done = order[::-1][:phase]
    index = tuple(pl.ds(0, 4) if name in done else at[name] for name in DIMS)
    return index + (slice(None), pl.ds(start, width))


def portion_cut(plane, part, ys, p):
    start, width, order = PORTIONS[p]
    place = (part, ys, slice(None)) if plane == 0 else (slice(None), part, ys)
    return place + (slice(None), pl.ds(start, width))


def plane_cut(plane, part, ys):
    return (part, ys) if plane == 0 else (slice(None), part, ys)


class Layer:
    def __init__(self, me, x_ref, gain_ref, refs):
        self.me, self.x, self.gain = me, x_ref, gain_ref
        self.full, self.partial, self.acc, self.square, *lists = refs
        (
            self.plane_s, self.plane_r, self.slab_s, self.slab_r, self.sum_s, self.sum_r, self.last_s, self.last_r
        ) = lists[9:]
        self.in1, self.held2, self.in2 = [lists[i * 3 : i * 3 + 3] for i in range(3)]
        self.ring = {name: [moved(me, **{name: step}) for step in (1, 2, 3)] for name in DIMS}
        self.back = {name: [moved(me, **{name: 4 - step}) for step in (1, 2, 3)] for name in DIMS}
        self.sends = []

    def begin(self, p, f_me):
        start, width, order = PORTIONS[p]
        me = self.me
        lanes = pl.ds(start, width)
        scaled = self.x[:, lanes] * self.gain[:, pl.ds(pl.multiple_of(f_me * BLK + start, 128), width)]
        self.full[me["z"], me["y"], me["x"], :, lanes] = scaled.astype(BF16)
        region = self.full.at[region_of(me, p, 0)]
        for k, step in enumerate(PLANE):
            to = straight(moved(me, **dict(zip(order[1:], step))))
            copy = remote(region, region, self.plane_s.at[p, k], self.plane_r.at[p, k], to)
            copy.start()
            self.sends.append(copy)

    def gather(self):
        me = self.me
        for p in range(3):
            start, width, order = PORTIONS[p]
            for k, step in enumerate(PLANE):
                there = moved(me, **{name: 4 - by for name, by in zip(order[1:], step)})
                region = self.full.at[region_of(there, p, 0)]
                remote(region, region, self.plane_s.at[p, k], self.plane_r.at[p, k], straight(me)).wait_recv()
            region = self.full.at[region_of(me, p, 2)]
            for k in range(3):
                to = straight(self.ring[order[0]][k])
                copy = remote(region, region, self.slab_s.at[p, k], self.slab_r.at[p, k], to)
                copy.start()
                self.sends.append(copy)
        for k in (0, 2, 1):
            for p in range(3):
                axis = PORTIONS[p][2][0]
                region = self.full.at[region_of(self.back[axis][k], p, 2)]
                remote(region, region, self.slab_s.at[p, k], self.slab_r.at[p, k], straight(me)).wait_recv()

    def first_sums(self, p):
        begin, width, order = PORTIONS[p]
        copies = []
        for k in range(3):
            to = self.ring[order[0]][k]
            index = [slice(None)] * 3
            index[DIMS.index(order[0])] = to[order[0]]
            source = self.partial.at[tuple(index) + (slice(None), pl.ds(begin, width))]
            copies.append(remote(source, self.in1[p].at[k], self.sum_s.at[p, k], self.sum_r.at[p, k], straight(to)))
        return copies

    def sums(self, finish):
        me = self.me
        second = []
        for p in range(3):
            begin, width, order = PORTIONS[p]
            for copy in self.first_sums(p):
                copy.wait_recv()
            left = [name for name in DIMS if name != order[0]]

            def add(i, carry, p=p, begin=begin, width=width, order=order, left=left):
                index = {order[0]: me[order[0]], left[0]: i, left[1]: slice(None)}
                index = tuple(index[name] for name in DIMS) + (slice(None), pl.ds(begin, width))
                value = self.partial[index].astype(F32)
                for k in range(3):
                    value = value + self.in1[p][k, i].astype(F32)
                self.held2[p][i] = value.astype(BF16)
                return carry

            lax.fori_loop(0, 4, add, 0)
            copies = []
            for k, step in enumerate(PLANE):
                to = moved(me, **dict(zip(left, step)))
                source = self.held2[p].at[to[left[0]], to[left[1]]]
                copy = remote(source, self.in2[p].at[k], self.last_s.at[p, k], self.last_r.at[p, k], straight(to))
                copy.start()
                copies.append(copy)
            second.append(copies)
        for p in range(3):
            begin, width, order = PORTIONS[p]
            for copy in second[p]:
                copy.wait_recv()
            left = [name for name in DIMS if name != order[0]]
            value = self.held2[p][me[left[0]], me[left[1]]].astype(F32)
            value = value + jnp.sum(self.in2[p][...].astype(F32), axis=0)
            finish(p, begin, width, value + self.x[:, begin : begin + width])
            self.sends += second[p]

    def run(self, multiply, activate, down, weights):
        self.gather()
        for wait in weights:
            wait()
        for plane in (0, 1):

            @pl.when(self.me["c"] == plane)
            def _(plane=plane):
                self.acc[...] = jnp.zeros_like(self.acc)
                self.square[...] = jnp.zeros_like(self.square)

                def step(f, carry):
                    rows = self.full[plane_cut(plane, f // 2, pl.ds((f % 2) * 2, 2))].reshape(128, BLK)
                    at = pl.ds(pl.multiple_of(f * BLK, 128), BLK)
                    multiply(rows, at)
                    plain = rows.astype(F32) * (1.0 / self.gain[:, at])
                    plain = plain * plain
                    piece = plain[:, 0:128]
                    for k in range(1, 7):
                        piece = piece + plain[:, k * 128 : (k + 1) * 128]
                    self.square[...] += piece
                    return carry

                lax.fori_loop(0, 8, step, 0)
                scale = lax.rsqrt(jnp.sum(self.square[...], axis=1, keepdims=True) * (1.0 / D) + EPSILON)
                act = activate(plane, scale)
                for p in range(3):
                    start, width, order = PORTIONS[p]
                    for f in range(8):
                        block = down(act, slice(f * BLK + start, f * BLK + start + width)).astype(BF16)
                        shape = (2, 4, 16, width) if plane == 0 else (4, 2, 16, width)
                        ys = slice(f % 2 * 2, f % 2 * 2 + 2)
                        self.partial[portion_cut(plane, f // 2, ys, p)] = block.reshape(shape)
                    for copy in self.first_sums(p):
                        copy.start()

    def end(self):
        for copy in self.sends:
            copy.wait_send()
        for p in range(3):
            for copy in self.first_sums(p):
                copy.wait_send()


def silu(value):
    return value / (1.0 + jnp.exp(-value))


def layer_kernel(
    len_ref, nl_ref, hid_ref, ids_ref, gain1_ref, gain2_ref, wr_ref, q_hbm, cache_hbm, wv_hbm, wo_hbm,
    wg1_hbm, wu1_hbm, wd1_hbm, wg2_hbm, wu2_hbm, wd2_hbm, out_ref,
    up1, down1, up2, down2, x_ref, chosen_ref, mid, router_acc, own, final_in, load_sem, give_s, give_r, final_s, final_r,
    *refs,
):
    here = coords()
    f_me = here["z"] * 2 + here["y"] // 2
    yh = here["y"] // 2
    me = turned(here)
    sibling = moved(here, c=1)
    n1, n2 = wd1_hbm.shape[0], wd2_hbm.shape[0]
    sources = (wg1_hbm, wu1_hbm, wd1_hbm, wg2_hbm, wu2_hbm, wd2_hbm)

    def places(k):
        return (
            up1.at[pl.ds(k * n1, n1), :], up1.at[pl.ds(UP_AT + k * n1, n1), :], down1.at[pl.ds(k * n1, n1), :],
            up2.at[k], up2.at[2 + k], down2.at[pl.ds(k * n2, n2), :],
        )

    loads = [pltpu.make_async_copy(src, dst, load_sem.at[i]) for i, (src, dst) in enumerate(zip(sources, places(0)))]
    gives = [
        remote(src, dst, give_s.at[i], give_r.at[i], sibling) for i, (src, dst) in enumerate(zip(sources, places(1)))
    ]
    count = len(attention_scratch())
    attention_refs, refs = refs[:count], refs[count:]
    half = len(refs) // 2
    dense = Layer(me, x_ref, gain1_ref, refs[:half])
    routed = Layer(me, mid, gain2_ref, refs[half:])
    final_steps = [(dz, dy) for dy in (0, 2) for dz in range(4) if dz or dy]
    final_to = [moved(here, z=dz, y=dy) for dz, dy in final_steps]
    partners = [moved(here, **{name: step}) for name in DIMS for step in (1, 2, 3)] + [sibling]
    for one, two in (("x", "y"), ("y", "z"), ("z", "x")):
        partners += [moved(here, **{one: i, two: j}) for i in (1, 2, 3) for j in (1, 2, 3)]
    partners += [moved(here, x=i, c=1) for i in (1, 2, 3)]
    across = dict(here, y=yh * 2 + (1 - here["y"] % 2), c=1 - here["c"])
    partners += [moved(across, x=i) for i in range(4)]

    def early():
        for load in loads:
            load.start()
        for give in gives[:3]:
            give.start()

    sent = attention_part(
        here, len_ref, nl_ref, hid_ref, ids_ref, wv_hbm, wo_hbm, q_hbm, cache_hbm, x_ref, chosen_ref, attention_refs,
        partners, early,
    )
    for p in range(3):
        dense.begin(p, f_me)
    for give in gives[3:]:
        give.start()
    for first in (2 * n1, UP_AT + 2 * n1):
        up1[first : first + UP_AT - 2 * n1, :] = jnp.zeros((UP_AT - 2 * n1, D), BF16)

    def multiply_dense(rows, at):
        dense.acc[...] += dot_nt(rows, up1[:, at])

    def activate_dense(plane, scale):
        gate, up = dense.acc[:, 0 : 2 * n1], dense.acc[:, UP_AT : UP_AT + 2 * n1]
        return (silu(gate * scale) * (up * scale)).astype(BF16)

    def down_dense(act, at):
        return dot(act, down1[:, at])

    dense.run(multiply_dense, activate_dense, down_dense, [q.wait for q in loads[:3]] + [q.wait_recv for q in gives[:3]])

    def between(p, begin, width, value):
        mid[:, begin : begin + width] = value
        routed.begin(p, f_me)

    dense.sums(between)
    def multiply_routed(rows, at):
        for k in range(4):
            routed.acc[:, k * n2 : (k + 1) * n2] += dot(rows, up2[k, at, :])
        router_acc[...] += dot_nt(rows, wr_ref[:, at])

    def activate_routed(plane, scale):
        affinity = 1.0 / (1.0 + jnp.exp(-(router_acc[...] * scale)))
        router_acc[...] = jnp.zeros_like(router_acc)
        chosen = chosen_ref[plane * 128 : plane * 128 + 128, 0:16].astype(F32)
        picked = jnp.where(chosen > 0.5, affinity, 0.0)
        below = jnp.sum(picked, axis=1, keepdims=True)
        mine = lax.broadcasted_iota(jnp.int32, (128, 16), 1) == here["z"] * 4 + here["y"]
        weight = ROUTE_SCALE * jnp.sum(jnp.where(mine, picked, 0.0), axis=1, keepdims=True) / below
        wanted = jnp.sum(jnp.where(mine, chosen, 0.0), axis=1, keepdims=True) > 0.5
        act = silu(routed.acc[:, : 2 * n2] * scale) * (routed.acc[:, 2 * n2 :] * scale)
        return jnp.where(wanted, act * weight, 0.0).astype(BF16)

    def down_routed(act, at):
        return dot(act, down2[:, at])

    router_acc[...] = jnp.zeros_like(router_acc)
    routed.run(multiply_routed, activate_routed, down_routed, [q.wait for q in loads[3:]] + [q.wait_recv for q in gives[3:]])

    def last(p, begin, width, value):
        own[:, begin : begin + width] = value.astype(BF16)

    routed.sums(last)

    final_copies = []
    for i, to in enumerate(final_to):
        copy = remote(own, final_in.at[here["z"], yh], final_s.at[i], final_r.at[i], to)
        copy.start()
        final_copies.append(copy)
    final_in[here["z"], yh] = own[...]
    for copy in final_copies:
        copy.wait_recv()
    row = lax.broadcasted_iota(jnp.int32, (16, BLK), 0)
    for f in range(8):
        block = final_in[f // 2, f % 2].astype(F32)
        both = [jnp.sum(jnp.where(row == f_me * 2 + t, block, 0.0), axis=0, keepdims=True) for t in range(2)]
        out_ref[:, f * BLK : (f + 1) * BLK] = jnp.concatenate(both, axis=0).astype(BF16)
    for copy in final_copies:
        copy.wait_send()
    for give in gives:
        give.wait_send()
    for copy in sent:
        copy.wait_send()
    dense.end()
    routed.end()


def layer_scratch(columns):
    dma = pltpu.SemaphoreType.DMA
    widths = [width for _, width, _ in PORTIONS]
    return (
        [
            pltpu.VMEM((4, 4, 4, 16, BLK), BF16),
            pltpu.VMEM((4, 4, 4, 16, BLK), BF16),
            pltpu.VMEM((128, columns), F32),
            pltpu.VMEM((128, 128), F32),
        ]
        + [pltpu.VMEM((3, 4, 4, 16, width), BF16) for width in widths]
        + [pltpu.VMEM((4, 4, 16, width), BF16) for width in widths]
        + [pltpu.VMEM((15, 16, width), BF16) for width in widths]
        + [dma((3, 15)), dma((3, 15)), dma((3, 3)), dma((3, 3)), dma((3, 3)), dma((3, 3)), dma((3, 15)), dma((3, 15))]
    )


def layer(lengths, latent, hidden, ids, gain1, gain2, w_router, queries, cache, w_values, w_out, dense, expert):
    any_space = pl.BlockSpec(memory_space=pl.ANY)
    vmem = pl.BlockSpec(memory_space=pltpu.VMEM)
    dma = pltpu.SemaphoreType.DMA
    n1, n2 = dense[2].shape[0], expert[2].shape[0]
    return pl.pallas_call(
        layer_kernel,
        out_shape=jax.ShapeDtypeStruct((2, D), BF16),
        in_specs=[pl.BlockSpec(memory_space=pltpu.SMEM)] + [vmem] * 6 + [any_space] * 10,
        out_specs=vmem,
        scratch_shapes=[
            pltpu.VMEM((2 * UP_AT, D), BF16),
            pltpu.VMEM((2 * n1, D), BF16),
            pltpu.VMEM((4, D, n2), BF16),
            pltpu.VMEM((2 * n2, D), BF16),
            pltpu.VMEM((16, BLK), F32),
            pltpu.VMEM((256, 128), BF16),
            pltpu.VMEM((16, BLK), F32),
            pltpu.VMEM((128, 16), F32),
            pltpu.VMEM((16, BLK), BF16),
            pltpu.VMEM((4, 2, 16, BLK), BF16),
            dma((6,)), dma((6,)), dma((6,)), dma((7,)), dma((7,)),
        ]
        + attention_scratch()
        + layer_scratch(2 * UP_AT)
        + layer_scratch(4 * n2),
        compiler_params=pltpu.CompilerParams(collective_id=0, has_side_effects=True, vmem_limit_bytes=VMEM_LIMIT),
        name="decode_layer",
    )(
        lengths, latent, hidden, ids, gain1, gain2, w_router, queries, cache, w_values, w_out, *dense, *expert
    )


def body(
    hidden,
    queries,
    cache,
    new_latent,
    lengths,
    w_values,
    w_out,
    gain_attn,
    w_dense_gate,
    w_dense_up,
    w_dense_down,
    gain_moe,
    w_router,
    expert_ids,
    w_expert_gate,
    w_expert_up,
    w_expert_down,
):
    out = layer(
        lengths,
        new_latent,
        hidden,
        expert_ids,
        gain_attn.reshape(1, D),
        gain_moe.reshape(1, D),
        w_router.T,
        jnp.swapaxes(queries, 1, 2),
        jnp.swapaxes(cache, 1, 2),
        w_values,
        jnp.swapaxes(w_out, 1, 2),
        (w_dense_gate.T, w_dense_up.T, w_dense_down),
        (w_expert_gate[0], w_expert_up[0], w_expert_down[0]),
    )
    return out


def solution(mesh):
    in_specs = (
        P(("tp", "ep"), None),
        P(("tp", "ep"), None, None),
        P(("tp", "ep"), None, None),
        P(("tp", "ep"), None),
        P(("tp", "ep")),
        P("tp", None, None),
        P("tp", None, "ep"),
        P(),
        P(None, ("tp", "ep")),
        P(None, ("tp", "ep")),
        P(("tp", "ep"), None),
        P(),
        P(),
        P(("tp", "ep"), None),
        P("ep", None, "tp"),
        P("ep", None, "tp"),
        P("ep", "tp", None),
    )
    out_specs = P(("tp", "ep"), None)
    return jax.shard_map(body, mesh=mesh, in_specs=in_specs, out_specs=out_specs, check_vma=False)
```

```python
import jax
import jax.numpy as jnp
from jax import lax
from jax.experimental import pallas as pl
from jax.experimental.pallas import tpu as pltpu
from jax.sharding import PartitionSpec as P

ROPE = 64
VD = 128
D = 7168
BLK = 896
EPSILON = 1e-06
ROUTE_SCALE = 2.5
MESH = pl.DeviceIdType.MESH
F32 = jnp.float32
BF16 = jnp.bfloat16
VMEM_LIMIT = 60 * 2**20


PORTIONS = ((0, 384, ("x", "y", "z")), (384, 256, ("y", "z", "x")), (640, 256, ("z", "x", "y")))
DIMS = ("z", "y", "x")
PLANE = sorted(((i, j) for i in range(4) for j in range(4) if i or j), key=lambda d: -sum(min(k, 4 - k) for k in d))

ROWS = (2, 1, 3, 0)


def coords():
    tp, ep = lax.axis_index("tp"), lax.axis_index("ep")
    return dict(x=tp // 2, c=tp % 2, z=ep // 4, y=ep % 4)


def device(at):
    return (at["x"] * 2 + at["c"], at["z"] * 4 + at["y"])


def moved(at, **steps):
    new = dict(at)
    for name, step in steps.items():
        new[name] = lax.rem(at[name] + step, 2 if name == "c" else 4)
    return new


def greet(partners):
    barrier = pltpu.get_barrier_semaphore()
    for partner in partners:
        pl.semaphore_signal(barrier, inc=1, device_id=device(partner), device_id_type=MESH)


def gathered(partners):
    pl.semaphore_wait(pltpu.get_barrier_semaphore(), len(partners))


def remote(src, dst, send, recv, partner):
    return pltpu.make_async_remote_copy(
        src_ref=src, dst_ref=dst, send_sem=send, recv_sem=recv, device_id=device(partner), device_id_type=MESH
    )


def dot_nt(a, b):
    return lax.dot_general(a, b, (((1,), (1,)), ((), ())), preferred_element_type=F32)


def dot(a, b):
    return jnp.dot(a, b, preferred_element_type=F32)


def attend(t, q, cache, latent, length):
    scale = (VD + ROPE) ** (-0.5)
    scores = lax.dot_general(q[t], cache[t], (((0,), (0,)), ((), ())), preferred_element_type=F32) * scale
    own = lax.dot_general(q[t], latent, (((0,), (1,)), ((), ())), preferred_element_type=F32) * scale
    own = own[:, t : t + 1]
    place = lax.broadcasted_iota(jnp.int32, scores.shape, 1)
    scores = jnp.where(place < length, scores, -jnp.inf)
    peak = jnp.maximum(jnp.max(scores, axis=1, keepdims=True), own)
    weights = jnp.exp(scores - peak)
    own_weight = jnp.exp(own - peak)
    total = jnp.sum(weights, axis=1, keepdims=True) + own_weight
    probability = (weights / total).astype(BF16)
    own_probability = (own_weight / total).astype(BF16).astype(F32)
    context = dot_nt(probability, cache[t, 0:512, :])
    return (context + own_probability * latent[t : t + 1, 0:512].astype(F32)).astype(BF16)


def attention_part(me, len_ref, nl_ref, hid_ref, ids_ref, wv_hbm, wo_hbm, q_hbm, cache_hbm, shard, chosen_all, refs, meeting, early):
    (
        q, cache, latent, ctx, wv, wo, ctx_in, heads, part, part_in, hid_out, hid_in, mask_out, mask_in, load_sem,
        hid_s, hid_r, ctx_s, ctx_r, mask_s, mask_r, hv_s, hv_r, hw_s, hw_r, part_s, part_r,
    ) = refs
    x, c, z, y = me["x"], me["c"], me["z"], me["y"]
    yh, yl = y // 2, y % 2
    tp = x * 2 + c
    pad = pl.multiple_of(yl * 64, 64)
    requests = []
    for t in range(2):
        pairs = ((q_hbm.at[t], q.at[t]), (cache_hbm.at[t], cache.at[t]))
        requests.append([pltpu.make_async_copy(src, dst, load_sem.at[t * 2 + k]) for k, (src, dst) in enumerate(pairs)])
    load_wv = pltpu.make_async_copy(wv_hbm, wv, load_sem.at[4])
    load_wo = pltpu.make_async_copy(wo_hbm, wo.at[:, pl.ds(pad, 448), :], load_sem.at[5])
    for load in requests[0] + requests[1] + [load_wv, load_wo]:
        load.start()

    def at_tp(step):
        other = lax.rem(tp + step, 8)
        return dict(me, x=other // 2, c=other % 2)

    tp_steps = [(dt, dy) for dy in (0, 1) for dt in range(8) if dt or dy]
    part_to = [dict(at_tp(dt), y=yh * 2 + (yl + dy) % 2) for dt, dy in tp_steps]
    hid_steps = [(dz, dy) for dy in (0, 2) for dz in range(4) if dz or dy]
    hid_to = [moved(me, z=dz, y=dy) for dz, dy in hid_steps]
    greet(meeting)
    wo[:, pl.ds(pl.multiple_of((1 - yl) * 448, 64), 64), :] = jnp.zeros((16, 64, 128), BF16)
    latent[...] = jnp.zeros_like(latent)
    latent[0:2, :] = nl_ref[...].astype(F32)
    latents = latent[...].astype(BF16)
    ctx_copies = []
    for t in range(2):
        for load in requests[t]:
            load.wait()
        ctx[t] = attend(t, q, cache, latents, len_ref[t]).reshape(8, 16, 512)
        if t == 0:
            gathered(meeting)
        for step in (4, 3, 5, 2, 6, 1, 7):
            to = at_tp(step)
            source, into = ctx.at[t, to["x"] * 2 + to["c"]], ctx_in.at[tp, t]
            copy = remote(source, into, ctx_s.at[t, step - 1], ctx_r.at[t, step - 1], to)
            copy.start()
            ctx_copies.append(copy)

    first = (z * 2 + yh) * 2
    row = lax.broadcasted_iota(jnp.int32, (16, BLK), 0)
    for f in range(8):
        both = hid_ref[:, f * BLK : (f + 1) * BLK].astype(F32)
        placed = jnp.where(row == first, both[0:1, :], jnp.where(row == first + 1, both[1:2, :], 0.0))
        hid_out[f // 2, f % 2] = placed.astype(BF16)
    lane = lax.broadcasted_iota(jnp.int32, (2, 128), 1)
    chosen = jnp.zeros((2, 128), F32)
    for k in range(ids_ref.shape[1]):
        chosen = chosen + jnp.where(ids_ref[:, k : k + 1] == lane, 1.0, 0.0)
    row = lax.broadcasted_iota(jnp.int32, (16, 128), 0)
    placed = jnp.where(row == tp * 2, chosen[0:1, :], jnp.where(row == tp * 2 + 1, chosen[1:2, :], 0.0))
    mask_out[...] = placed.astype(BF16)
    for step in range(1, 8):
        copy = remote(mask_out, mask_in.at[tp], mask_s.at[step - 1], mask_r.at[step - 1], at_tp(step))
        copy.start()
        ctx_copies.append(copy)
    hid_copies = []
    for i, to in enumerate(hid_to):
        copy = remote(hid_out.at[to["z"], to["y"] // 2], hid_in.at[z, yh], hid_s.at[i], hid_r.at[i], to)
        copy.start()
        hid_copies.append(copy)
    ctx_in[tp] = ctx[:, tp]
    mask_in[tp] = mask_out[...]
    hid_in[z, yh] = hid_out[z, yh]
    for copy in ctx_copies:
        copy.wait_recv()
    load_wv.wait()
    early()

    i = lax.broadcasted_iota(jnp.int32, (256, 256), 0)
    j = lax.broadcasted_iota(jnp.int32, (256, 256), 1)
    turn = ((i & 15) * 16 + (i >> 4) == j).astype(BF16)
    by_head = dot(turn, ctx_in[...].reshape(256, 512)).astype(BF16)
    halves = ((0, "z", "y"), (1, "y", "z"))
    sends = []

    def lanes_of(half):
        return pl.ds(half * 1024, 1024 + half * 128)

    for half, one, two in halves:
        for h in range(half * 8, half * 8 + 8):
            heads[z, y, :, h * 128 : (h + 1) * 128] = dot(by_head[h * 16 : (h + 1) * 16, :], wv[h]).astype(BF16)
        if half:
            heads[z, y, :, 2048:2176] = jnp.sum(mask_in[...].astype(F32), axis=0).astype(BF16)
        mine = heads.at[z, y, :, lanes_of(half)]
        for k in (2, 1, 3):
            to = moved(me, **{one: k})
            sends.append(remote(mine, mine, hv_s.at[half, k - 1], hv_r.at[half, k - 1], to))
            sends[-1].start()
        for k in (2, 1, 3):
            to = moved(me, **{two: k})
            sends.append(remote(mine, mine, hw_s.at[half, 0, k - 1], hw_r.at[half, 0, k - 1], to))
            sends[-1].start()
    for k in (1, 3, 2):
        for half, one, two in halves:
            there = moved(me, **{one: 4 - k})
            piece = heads.at[there["z"], there["y"], :, lanes_of(half)]
            remote(piece, piece, hv_s.at[half, k - 1], hv_r.at[half, k - 1], me).wait_recv()
            for hop in (2, 1, 3):
                to = moved(me, **{two: hop})
                sends.append(remote(piece, piece, hw_s.at[half, k, hop - 1], hw_r.at[half, k, hop - 1], to))
                sends[-1].start()
    load_wo.wait()

    total = jnp.zeros((256, 512), F32)
    for half, one, two in halves:
        for k in range(4):
            for hop in (1, 3, 2):
                there = moved(me, **{one: (4 - k) % 4, two: 4 - hop})
                piece = heads.at[there["z"], there["y"], :, lanes_of(half)]
                remote(piece, piece, hw_s.at[half, k, hop - 1], hw_r.at[half, k, hop - 1], me).wait_recv()
        for pair in range(half * 4, half * 4 + 4):
            rows = heads[:, :, :, pair * 256 : (pair + 1) * 256].reshape(256, 256)
            weights = jnp.concatenate([wo[2 * pair], wo[2 * pair + 1]], axis=1)
            total = total + dot_nt(rows, weights)
    t, from_yh, from_z = i & 1, (i >> 1) & 1, (i >> 2) & 3
    source = from_z * 64 + (from_yh * 2 + (i >> 7)) * 16 + ((i >> 4) & 7) * 2 + t
    order = (source == j).astype(BF16)
    part[...] = dot(order, total.astype(BF16)).astype(BF16).reshape(2, 8, 16, 512)
    part_copies = []
    for i_to, to in enumerate(part_to):
        copy = remote(
            part.at[to["y"] % 2, to["x"] * 2 + to["c"]], part_in.at[yl, tp], part_s.at[i_to], part_r.at[i_to], to
        )
        copy.start()
        part_copies.append(copy)
    part_in[yl, tp] = part[yl, tp]
    plane = i >> 7
    to_yl = ((i >> 6) & 1) * (1 - plane) + ((i >> 4) & 1) * plane
    to_x = ((i >> 4) & 3) * (1 - plane) + ((i >> 5) & 3) * plane
    source = from_z * 64 + (from_yh * 2 + to_yl) * 16 + to_x * 4 + plane * 2 + t
    chosen_all[...] = dot((source == j).astype(BF16), heads[:, :, :, 2048:2176].reshape(256, 128)).astype(BF16)
    for copy in hid_copies:
        copy.wait_recv()
    shard[...] = jnp.sum(hid_in[...].astype(F32), axis=(0, 1))
    for copy in part_copies:
        copy.wait_recv()
    sums = jnp.sum(part_in[...].astype(F32), axis=1)
    shard[:, 0:512] += sums[0]
    shard[:, 384:896] += sums[1]
    return ctx_copies + hid_copies + sends + part_copies


def attention_scratch():
    dma = pltpu.SemaphoreType.DMA
    return [
        pltpu.VMEM((2, 576, 128), BF16),
        pltpu.VMEM((2, 576, 1024), BF16),
        pltpu.VMEM((16, 576), F32),
        pltpu.VMEM((2, 8, 16, 512), BF16),
        pltpu.VMEM((16, 512, 128), BF16),
        pltpu.VMEM((16, 512, 128), BF16),
        pltpu.VMEM((8, 2, 16, 512), BF16),
        pltpu.VMEM((4, 4, 16, 2176), BF16),
        pltpu.VMEM((2, 8, 16, 512), BF16),
        pltpu.VMEM((2, 8, 16, 512), BF16),
        pltpu.VMEM((4, 2, 16, BLK), BF16),
        pltpu.VMEM((4, 2, 16, BLK), BF16),
        pltpu.VMEM((16, 128), BF16),
        pltpu.VMEM((8, 16, 128), BF16),
        dma((6,)),
        dma((7,)), dma((7,)), dma((2, 7)), dma((2, 7)), dma((7,)), dma((7,)),
        dma((2, 3)), dma((2, 3)), dma((2, 4, 3)), dma((2, 4, 3)), dma((15,)), dma((15,)),
    ]


def turned(at):
    c = at["c"]
    return dict(
        z=at["z"] * (1 - c) + at["x"] * c, y=at["y"] * (1 - c) + at["z"] * c, x=at["x"] * (1 - c) + at["y"] * c, c=c
    )


def straight(at):
    c = at["c"]
    return dict(
        z=at["z"] * (1 - c) + at["y"] * c, y=at["y"] * (1 - c) + at["x"] * c, x=at["x"] * (1 - c) + at["z"] * c, c=c
    )


def region_of(at, portion, phase):
    start, width, order = PORTIONS[portion]
    done = order[::-1][:phase]
    index = tuple(pl.ds(0, 4) if name in done else at[name] for name in DIMS)
    return index + (slice(None), pl.ds(start, width))


def portion_cut(plane, part, ys, p):
    start, width, order = PORTIONS[p]
    place = (part, ys, slice(None)) if plane == 0 else (slice(None), part, ys)
    return place + (slice(None), pl.ds(start, width))


def plane_cut(plane, part, ys):
    return (part, ys) if plane == 0 else (slice(None), part, ys)


class Layer:
    def __init__(self, me, x_ref, gain_ref, refs):
        self.me, self.x, self.gain = me, x_ref, gain_ref
        self.full, self.partial, self.acc, self.square, *lists = refs
        (
            self.plane_s, self.plane_r, self.slab_s, self.slab_r, self.sum_s, self.sum_r, self.last_s, self.last_r
        ) = lists[9:]
        self.in1, self.held2, self.in2 = [lists[i * 3 : i * 3 + 3] for i in range(3)]
        self.ring = {name: [moved(me, **{name: step}) for step in (1, 2, 3)] for name in DIMS}
        self.back = {name: [moved(me, **{name: 4 - step}) for step in (1, 2, 3)] for name in DIMS}
        self.sends = []

    def begin(self, p, f_me):
        start, width, order = PORTIONS[p]
        me = self.me
        lanes = pl.ds(start, width)
        scaled = self.x[:, lanes] * self.gain[:, pl.ds(pl.multiple_of(f_me * BLK + start, 128), width)]
        self.full[me["z"], me["y"], me["x"], :, lanes] = scaled.astype(BF16)
        region = self.full.at[region_of(me, p, 0)]
        for k, step in enumerate(PLANE):
            to = straight(moved(me, **dict(zip(order[1:], step))))
            copy = remote(region, region, self.plane_s.at[p, k], self.plane_r.at[p, k], to)
            copy.start()
            self.sends.append(copy)

    def gather(self):
        me = self.me
        for row in (0, 1, 3, 2):
            for p in range(3):
                start, width, order = PORTIONS[p]
                for k, step in enumerate(PLANE):
                    if step[0] == row:
                        there = moved(me, **{name: 4 - by for name, by in zip(order[1:], step)})
                        region = self.full.at[region_of(there, p, 0)]
                        remote(region, region, self.plane_s.at[p, k], self.plane_r.at[p, k], straight(me)).wait_recv()
                region = self.full.at[region_of(moved(me, **{order[1]: 4 - row}), p, 1)]
                for k in (1, 0, 2):
                    to = straight(self.ring[order[0]][k])
                    copy = remote(region, region, self.slab_s.at[p, row, k], self.slab_r.at[p, row, k], to)
                    copy.start()
                    self.sends.append(copy)

    def take(self, p):
        order = PORTIONS[p][2]
        for row in (0, 1, 3, 2):
            for k in (0, 2, 1):
                there = moved(self.back[order[0]][k], **{order[1]: 4 - row})
                region = self.full.at[region_of(there, p, 1)]
                remote(region, region, self.slab_s.at[p, row, k], self.slab_r.at[p, row, k], straight(self.me)).wait_recv()

    def first_sums(self, p, row):
        begin, width, order = PORTIONS[p]
        left = [name for name in DIMS if name != order[0]]
        there = moved(self.me, **{left[0]: row})
        copies = []
        for k in (1, 0, 2):
            to = self.ring[order[0]][k]
            index = dict(there, **{order[0]: to[order[0]], left[1]: slice(None)})
            source = self.partial.at[tuple(index[name] for name in DIMS) + (slice(None), pl.ds(begin, width))]
            into = self.in1[p].at[k, there[left[0]]]
            copies.append(remote(source, into, self.sum_s.at[p, row, k], self.sum_r.at[p, row, k], straight(to)))
        return copies

    def sums(self, finish):
        me = self.me
        second = []
        for row in ROWS:
            for p in range(3):
                begin, width, order = PORTIONS[p]
                for copy in self.first_sums(p, row):
                    copy.wait_recv()
                left = [name for name in DIMS if name != order[0]]
                there = moved(me, **{left[0]: row})
                index = dict(there, **{left[1]: slice(None)})
                value = self.partial[tuple(index[name] for name in DIMS) + (slice(None), pl.ds(begin, width))].astype(F32)
                for k in range(3):
                    value = value + self.in1[p][k, there[left[0]]].astype(F32)
                self.held2[p][there[left[0]]] = value.astype(BF16)
                for k, step in enumerate(PLANE):
                    if step[0] == row:
                        to = moved(me, **dict(zip(left, step)))
                        source = self.held2[p].at[to[left[0]], to[left[1]]]
                        into = self.in2[p].at[k]
                        copy = remote(source, into, self.last_s.at[p, k], self.last_r.at[p, k], straight(to))
                        copy.start()
                        second.append((p, copy))
        for p in range(3):
            begin, width, order = PORTIONS[p]
            for at, copy in second:
                if at == p:
                    copy.wait_recv()
            left = [name for name in DIMS if name != order[0]]
            value = self.held2[p][me[left[0]], me[left[1]]].astype(F32)
            value = value + jnp.sum(self.in2[p][...].astype(F32), axis=0)
            finish(p, begin, width, value + self.x[:, begin : begin + width])
        self.sends += [copy for at, copy in second]

    def run(self, multiply, activate, down, weights):
        self.gather()
        for p in range(3):
            self.take(p)
        for wait in weights:
            wait()
        for plane in (0, 1):

            @pl.when(self.me["c"] == plane)
            def _(plane=plane):
                for f in range(8):
                    rows = self.full[plane_cut(plane, f // 2, slice(f % 2 * 2, f % 2 * 2 + 2))].reshape(128, BLK)
                    at = slice(f * BLK, (f + 1) * BLK)
                    multiply(rows, at, f == 0)
                    plain = rows.astype(F32) * (1.0 / self.gain[:, at])
                    plain = plain * plain
                    piece = plain[:, 0:128]
                    for k in range(1, 7):
                        piece = piece + plain[:, k * 128 : (k + 1) * 128]
                    put(self.square, piece, f == 0)

                scale = lax.rsqrt(jnp.sum(self.square[...], axis=1, keepdims=True) * (1.0 / D) + EPSILON)
                act = activate(plane, scale)
                for p in range(3):
                    start, width, order = PORTIONS[p]
                    for f in range(8):
                        block = down(act, slice(f * BLK + start, f * BLK + start + width)).astype(BF16)
                        shape = (2, 4, 16, width) if plane == 0 else (4, 2, 16, width)
                        ys = slice(f % 2 * 2, f % 2 * 2 + 2)
                        self.partial[portion_cut(plane, f // 2, ys, p)] = block.reshape(shape)
                    for row in ROWS:
                        for copy in self.first_sums(p, row):
                            copy.start()

    def end(self):
        for copy in self.sends:
            copy.wait_send()
        for p in range(3):
            for row in ROWS:
                for copy in self.first_sums(p, row):
                    copy.wait_send()


def put(ref, value, first):
    if first:
        ref[...] = value
    else:
        ref[...] += value


def silu(value):
    return value / (1.0 + jnp.exp(-value))


def layer_kernel(
    len_ref, nl_ref, hid_ref, ids_ref, gain1_ref, gain2_ref, wr_ref, q_hbm, cache_hbm, wv_hbm, wo_hbm,
    wg1_hbm, wu1_hbm, wd1_hbm, wg2_hbm, wu2_hbm, wd2_hbm, out_ref,
    up1, down1, up2, down2, x_ref, chosen_ref, mid, router_acc, own, final_in, load_sem, give_s, give_r, final_s, final_r,
    *refs,
):
    here = coords()
    f_me = here["z"] * 2 + here["y"] // 2
    yh = here["y"] // 2
    me = turned(here)
    sibling = moved(here, c=1)
    n1, n2 = wd1_hbm.shape[0], wd2_hbm.shape[0]
    sources = (wg1_hbm, wu1_hbm, wd1_hbm, wg2_hbm, wu2_hbm, wd2_hbm)

    def places(k):
        return (
            up1.at[pl.ds(k * n1, n1), :], up1.at[pl.ds((2 + k) * n1, n1), :], down1.at[pl.ds(k * n1, n1), :],
            up2.at[k], up2.at[2 + k], down2.at[pl.ds(k * n2, n2), :],
        )

    loads = [pltpu.make_async_copy(src, dst, load_sem.at[i]) for i, (src, dst) in enumerate(zip(sources, places(0)))]
    gives = [
        remote(src, dst, give_s.at[i], give_r.at[i], sibling) for i, (src, dst) in enumerate(zip(sources, places(1)))
    ]
    count = len(attention_scratch())
    attention_refs, refs = refs[:count], refs[count:]
    half = len(refs) // 2
    dense = Layer(me, x_ref, gain1_ref, refs[:half])
    routed = Layer(me, mid, gain2_ref, refs[half:])
    final_steps = [(dz, dy) for dy in (0, 2) for dz in range(4) if dz or dy]
    final_to = [moved(here, z=dz, y=dy) for dz, dy in final_steps]
    partners = [moved(here, **{name: step}) for name in DIMS for step in (1, 2, 3)] + [sibling]
    for one, two in (("x", "y"), ("y", "z"), ("z", "x")):
        partners += [moved(here, **{one: i, two: j}) for i in (1, 2, 3) for j in (1, 2, 3)]
    partners += [moved(here, x=i, c=1) for i in (1, 2, 3)]
    across = dict(here, y=yh * 2 + (1 - here["y"] % 2), c=1 - here["c"])
    partners += [moved(across, x=i) for i in range(4)]

    def early():
        for load in loads:
            load.start()
        for give in gives[:3]:
            give.start()

    sent = attention_part(
        here, len_ref, nl_ref, hid_ref, ids_ref, wv_hbm, wo_hbm, q_hbm, cache_hbm, x_ref, chosen_ref, attention_refs,
        partners, early,
    )
    for p in range(3):
        dense.begin(p, f_me)
    for give in gives[3:]:
        give.start()
    def multiply_dense(rows, at, first):
        put(dense.acc, dot_nt(up1[:, at], rows), first)

    def activate_dense(plane, scale):
        gate, up = dense.acc[0 : 2 * n1, :].T, dense.acc[2 * n1 :, :].T
        return (silu(gate * scale) * (up * scale)).astype(BF16)

    def down_dense(act, at):
        return dot(act, down1[:, at])

    dense.run(multiply_dense, activate_dense, down_dense, [q.wait for q in loads[:3]] + [q.wait_recv for q in gives[:3]])

    def between(p, begin, width, value):
        mid[:, begin : begin + width] = value
        routed.begin(p, f_me)

    dense.sums(between)
    def multiply_routed(rows, at, first):
        for k in range(4):
            put(routed.acc.at[:, k * n2 : (k + 1) * n2], dot(rows, up2[k, at, :]), first)
        put(router_acc, dot_nt(rows, wr_ref[:, at]), first)

    def activate_routed(plane, scale):
        affinity = 1.0 / (1.0 + jnp.exp(-(router_acc[...] * scale)))
        chosen = chosen_ref[plane * 128 : plane * 128 + 128, 0:16].astype(F32)
        picked = jnp.where(chosen > 0.5, affinity, 0.0)
        below = jnp.sum(picked, axis=1, keepdims=True)
        mine = lax.broadcasted_iota(jnp.int32, (128, 16), 1) == here["z"] * 4 + here["y"]
        weight = ROUTE_SCALE * jnp.sum(jnp.where(mine, picked, 0.0), axis=1, keepdims=True) / below
        wanted = jnp.sum(jnp.where(mine, chosen, 0.0), axis=1, keepdims=True) > 0.5
        act = silu(routed.acc[:, : 2 * n2] * scale) * (routed.acc[:, 2 * n2 :] * scale)
        return jnp.where(wanted, act * weight, 0.0).astype(BF16)

    def down_routed(act, at):
        return dot(act, down2[:, at])

    routed.run(multiply_routed, activate_routed, down_routed, [q.wait for q in loads[3:]] + [q.wait_recv for q in gives[3:]])

    def last(p, begin, width, value):
        own[:, begin : begin + width] = value.astype(BF16)

    routed.sums(last)

    final_copies = []
    for i, to in enumerate(final_to):
        copy = remote(own, final_in.at[here["z"], yh], final_s.at[i], final_r.at[i], to)
        copy.start()
        final_copies.append(copy)
    final_in[here["z"], yh] = own[...]
    for copy in final_copies:
        copy.wait_recv()
    row = lax.broadcasted_iota(jnp.int32, (16, BLK), 0)
    for f in range(8):
        block = final_in[f // 2, f % 2].astype(F32)
        both = [jnp.sum(jnp.where(row == f_me * 2 + t, block, 0.0), axis=0, keepdims=True) for t in range(2)]
        out_ref[:, f * BLK : (f + 1) * BLK] = jnp.concatenate(both, axis=0).astype(BF16)
    for copy in final_copies:
        copy.wait_send()
    for give in gives:
        give.wait_send()
    for copy in sent:
        copy.wait_send()
    dense.end()
    routed.end()


def layer_scratch(products):
    dma = pltpu.SemaphoreType.DMA
    widths = [width for _, width, _ in PORTIONS]
    return (
        [
            pltpu.VMEM((4, 4, 4, 16, BLK), BF16),
            pltpu.VMEM((4, 4, 4, 16, BLK), BF16),
            pltpu.VMEM(products, F32),
            pltpu.VMEM((128, 128), F32),
        ]
        + [pltpu.VMEM((3, 4, 4, 16, width), BF16) for width in widths]
        + [pltpu.VMEM((4, 4, 16, width), BF16) for width in widths]
        + [pltpu.VMEM((15, 16, width), BF16) for width in widths]
        + [dma((3, 15)), dma((3, 15)), dma((3, 4, 3)), dma((3, 4, 3)), dma((3, 4, 3)), dma((3, 4, 3)), dma((3, 15)), dma((3, 15))]
    )


def layer(lengths, latent, hidden, ids, gain1, gain2, w_router, queries, cache, w_values, w_out, dense, expert):
    any_space = pl.BlockSpec(memory_space=pl.ANY)
    vmem = pl.BlockSpec(memory_space=pltpu.VMEM)
    dma = pltpu.SemaphoreType.DMA
    n1, n2 = dense[2].shape[0], expert[2].shape[0]
    return pl.pallas_call(
        layer_kernel,
        out_shape=jax.ShapeDtypeStruct((2, D), BF16),
        in_specs=[pl.BlockSpec(memory_space=pltpu.SMEM)] + [vmem] * 6 + [any_space] * 10,
        out_specs=vmem,
        scratch_shapes=[
            pltpu.VMEM((4 * n1, D), BF16),
            pltpu.VMEM((2 * n1, D), BF16),
            pltpu.VMEM((4, D, n2), BF16),
            pltpu.VMEM((2 * n2, D), BF16),
            pltpu.VMEM((16, BLK), F32),
            pltpu.VMEM((256, 128), BF16),
            pltpu.VMEM((16, BLK), F32),
            pltpu.VMEM((128, 16), F32),
            pltpu.VMEM((16, BLK), BF16),
            pltpu.VMEM((4, 2, 16, BLK), BF16),
            dma((6,)), dma((6,)), dma((6,)), dma((7,)), dma((7,)),
        ]
        + attention_scratch()
        + layer_scratch((4 * n1, 128))
        + layer_scratch((128, 4 * n2)),
        compiler_params=pltpu.CompilerParams(collective_id=0, has_side_effects=True, vmem_limit_bytes=VMEM_LIMIT),
        name="decode_layer",
    )(
        lengths, latent, hidden, ids, gain1, gain2, w_router, queries, cache, w_values, w_out, *dense, *expert
    )


def body(
    hidden,
    queries,
    cache,
    new_latent,
    lengths,
    w_values,
    w_out,
    gain_attn,
    w_dense_gate,
    w_dense_up,
    w_dense_down,
    gain_moe,
    w_router,
    expert_ids,
    w_expert_gate,
    w_expert_up,
    w_expert_down,
):
    out = layer(
        lengths,
        new_latent,
        hidden,
        expert_ids,
        gain_attn.reshape(1, D),
        gain_moe.reshape(1, D),
        w_router.T,
        jnp.swapaxes(queries, 1, 2),
        jnp.swapaxes(cache, 1, 2),
        w_values,
        jnp.swapaxes(w_out, 1, 2),
        (w_dense_gate.T, w_dense_up.T, w_dense_down),
        (w_expert_gate[0], w_expert_up[0], w_expert_down[0]),
    )
    return out


def solution(mesh):
    in_specs = (
        P(("tp", "ep"), None),
        P(("tp", "ep"), None, None),
        P(("tp", "ep"), None, None),
        P(("tp", "ep"), None),
        P(("tp", "ep")),
        P("tp", None, None),
        P("tp", None, "ep"),
        P(),
        P(None, ("tp", "ep")),
        P(None, ("tp", "ep")),
        P(("tp", "ep"), None),
        P(),
        P(),
        P(("tp", "ep"), None),
        P("ep", None, "tp"),
        P("ep", None, "tp"),
        P("ep", "tp", None),
    )
    out_specs = P(("tp", "ep"), None)
    return jax.shard_map(body, mesh=mesh, in_specs=in_specs, out_specs=out_specs, check_vma=False)
```

```python
import jax
import jax.numpy as jnp
from jax import lax
from jax.experimental import pallas as pl
from jax.experimental.pallas import tpu as pltpu
from jax.sharding import PartitionSpec as P

ROPE = 64
VD = 128
D = 7168
BLK = 896
EPSILON = 1e-06
ROUTE_SCALE = 2.5
MESH = pl.DeviceIdType.MESH
F32 = jnp.float32
BF16 = jnp.bfloat16
VMEM_LIMIT = 60 * 2**20


PORTIONS = ((0, 384, ("x", "y", "z")), (384, 256, ("y", "z", "x")), (640, 256, ("z", "x", "y")))
DIMS = ("z", "y", "x")
PLANE = sorted(((i, j) for i in range(4) for j in range(4) if i or j), key=lambda d: -sum(min(k, 4 - k) for k in d))

ROWS = (2, 1, 3, 0)

LAUNCH = [(k, p) for k in sorted(range(15), key=lambda k: (PLANE[k][0] != 0, k)) for p in range(3)]


def coords():
    tp, ep = lax.axis_index("tp"), lax.axis_index("ep")
    return dict(x=tp // 2, c=tp % 2, z=ep // 4, y=ep % 4)


def device(at):
    return (at["x"] * 2 + at["c"], at["z"] * 4 + at["y"])


def moved(at, **steps):
    new = dict(at)
    for name, step in steps.items():
        new[name] = lax.rem(at[name] + step, 2 if name == "c" else 4)
    return new


def greet(partners):
    barrier = pltpu.get_barrier_semaphore()
    for partner in partners:
        pl.semaphore_signal(barrier, inc=1, device_id=device(partner), device_id_type=MESH)


def gathered(partners):
    pl.semaphore_wait(pltpu.get_barrier_semaphore(), len(partners))


def remote(src, dst, send, recv, partner):
    return pltpu.make_async_remote_copy(
        src_ref=src, dst_ref=dst, send_sem=send, recv_sem=recv, device_id=device(partner), device_id_type=MESH
    )


def dot_nt(a, b):
    return lax.dot_general(a, b, (((1,), (1,)), ((), ())), preferred_element_type=F32)


def dot(a, b):
    return jnp.dot(a, b, preferred_element_type=F32)


def attend(t, q, cache, latent, length):
    scale = (VD + ROPE) ** (-0.5)
    scores = lax.dot_general(q[t], cache[t], (((0,), (0,)), ((), ())), preferred_element_type=F32) * scale
    own = lax.dot_general(q[t], latent, (((0,), (1,)), ((), ())), preferred_element_type=F32) * scale
    own = own[:, t : t + 1]
    place = lax.broadcasted_iota(jnp.int32, scores.shape, 1)
    scores = jnp.where(place < length, scores, -jnp.inf)
    peak = jnp.maximum(jnp.max(scores, axis=1, keepdims=True), own)
    weights = jnp.exp(scores - peak)
    own_weight = jnp.exp(own - peak)
    total = jnp.sum(weights, axis=1, keepdims=True) + own_weight
    probability = (weights / total).astype(BF16)
    own_probability = (own_weight / total).astype(BF16).astype(F32)
    context = dot_nt(probability, cache[t, 0:512, :])
    return (context + own_probability * latent[t : t + 1, 0:512].astype(F32)).astype(BF16)


def attention_part(me, len_ref, nl_ref, hid_ref, ids_ref, wv_hbm, wo_hbm, q_hbm, cache_hbm, shard, chosen_all, refs, meeting, early):
    (
        q, cache, latent, ctx, wv, wo, ctx_in, heads, part, part_in, hid_out, hid_in, mask_out, mask_in, load_sem,
        hid_s, hid_r, ctx_s, ctx_r, mask_s, mask_r, hv_s, hv_r, hw_s, hw_r, part_s, part_r,
    ) = refs
    x, c, z, y = me["x"], me["c"], me["z"], me["y"]
    yh, yl = y // 2, y % 2
    tp = x * 2 + c
    pad = pl.multiple_of(yl * 64, 64)
    requests = []
    for t in range(2):
        pairs = ((q_hbm.at[t], q.at[t]), (cache_hbm.at[t], cache.at[t]))
        requests.append([pltpu.make_async_copy(src, dst, load_sem.at[t * 2 + k]) for k, (src, dst) in enumerate(pairs)])
    load_wv = pltpu.make_async_copy(wv_hbm, wv, load_sem.at[4])
    load_wo = pltpu.make_async_copy(wo_hbm, wo.at[:, pl.ds(pad, 448), :], load_sem.at[5])
    for load in requests[0] + requests[1] + [load_wv, load_wo]:
        load.start()

    def at_tp(step):
        other = lax.rem(tp + step, 8)
        return dict(me, x=other // 2, c=other % 2)

    tp_steps = [(dt, dy) for dy in (1, 0) for dt in (4, 5, 3, 2, 6, 7, 1, 0) if dt or dy]
    part_to = [dict(at_tp(dt), y=yh * 2 + (yl + dy) % 2) for dt, dy in tp_steps]
    hid_steps = [(dz, dy) for dy in (0, 2) for dz in range(4) if dz or dy]
    hid_to = [moved(me, z=dz, y=dy) for dz, dy in hid_steps]
    greet(meeting)
    wo[:, pl.ds(pl.multiple_of((1 - yl) * 448, 64), 64), :] = jnp.zeros((16, 64, 128), BF16)
    latent[...] = jnp.zeros_like(latent)
    latent[0:2, :] = nl_ref[...].astype(F32)
    latents = latent[...].astype(BF16)
    ctx_copies = []
    for t in range(2):
        for load in requests[t]:
            load.wait()
        ctx[t] = attend(t, q, cache, latents, len_ref[t]).reshape(8, 16, 512)
        if t == 0:
            gathered(meeting)
        for step in (4, 3, 5, 2, 6, 1, 7):
            to = at_tp(step)
            source, into = ctx.at[t, to["x"] * 2 + to["c"]], ctx_in.at[tp, t]
            copy = remote(source, into, ctx_s.at[t, step - 1], ctx_r.at[t, step - 1], to)
            copy.start()
            ctx_copies.append(copy)

    first = (z * 2 + yh) * 2
    row = lax.broadcasted_iota(jnp.int32, (16, BLK), 0)
    for f in range(8):
        both = hid_ref[:, f * BLK : (f + 1) * BLK].astype(F32)
        placed = jnp.where(row == first, both[0:1, :], jnp.where(row == first + 1, both[1:2, :], 0.0))
        hid_out[f // 2, f % 2] = placed.astype(BF16)
    lane = lax.broadcasted_iota(jnp.int32, (2, 128), 1)
    chosen = jnp.zeros((2, 128), F32)
    for k in range(ids_ref.shape[1]):
        chosen = chosen + jnp.where(ids_ref[:, k : k + 1] == lane, 1.0, 0.0)
    row = lax.broadcasted_iota(jnp.int32, (16, 128), 0)
    placed = jnp.where(row == tp * 2, chosen[0:1, :], jnp.where(row == tp * 2 + 1, chosen[1:2, :], 0.0))
    mask_out[...] = placed.astype(BF16)
    for step in range(1, 8):
        copy = remote(mask_out, mask_in.at[tp], mask_s.at[step - 1], mask_r.at[step - 1], at_tp(step))
        copy.start()
        ctx_copies.append(copy)
    hid_copies = []
    for i, to in enumerate(hid_to):
        copy = remote(hid_out.at[to["z"], to["y"] // 2], hid_in.at[z, yh], hid_s.at[i], hid_r.at[i], to)
        copy.start()
        hid_copies.append(copy)
    ctx_in[tp] = ctx[:, tp]
    mask_in[tp] = mask_out[...]
    hid_in[z, yh] = hid_out[z, yh]
    for copy in ctx_copies:
        copy.wait_recv()
    load_wv.wait()
    early()

    i = lax.broadcasted_iota(jnp.int32, (256, 256), 0)
    j = lax.broadcasted_iota(jnp.int32, (256, 256), 1)
    turn = ((i & 15) * 16 + (i >> 4) == j).astype(BF16)
    by_head = dot(turn, ctx_in[...].reshape(256, 512)).astype(BF16)
    halves = ((0, "z", "y"), (1, "y", "z"))
    sends = []

    def lanes_of(half):
        return pl.ds(half * 1024, 1024 + half * 128)

    for half, one, two in halves:
        for h in range(half * 8, half * 8 + 8):
            heads[z, y, :, h * 128 : (h + 1) * 128] = dot(by_head[h * 16 : (h + 1) * 16, :], wv[h]).astype(BF16)
        if half:
            heads[z, y, :, 2048:2176] = jnp.sum(mask_in[...].astype(F32), axis=0).astype(BF16)
        mine = heads.at[z, y, :, lanes_of(half)]
        for k in (2, 1, 3):
            to = moved(me, **{one: k})
            sends.append(remote(mine, mine, hv_s.at[half, k - 1], hv_r.at[half, k - 1], to))
            sends[-1].start()
        for k in (2, 1, 3):
            to = moved(me, **{two: k})
            sends.append(remote(mine, mine, hw_s.at[half, 0, k - 1], hw_r.at[half, 0, k - 1], to))
            sends[-1].start()
    for k in (1, 3, 2):
        for half, one, two in halves:
            there = moved(me, **{one: 4 - k})
            piece = heads.at[there["z"], there["y"], :, lanes_of(half)]
            remote(piece, piece, hv_s.at[half, k - 1], hv_r.at[half, k - 1], me).wait_recv()
            for hop in (2, 1, 3):
                to = moved(me, **{two: hop})
                sends.append(remote(piece, piece, hw_s.at[half, k, hop - 1], hw_r.at[half, k, hop - 1], to))
                sends[-1].start()
    load_wo.wait()

    total = jnp.zeros((256, 512), F32)
    for half, one, two in halves:
        for k in range(4):
            for hop in (1, 3, 2):
                there = moved(me, **{one: (4 - k) % 4, two: 4 - hop})
                piece = heads.at[there["z"], there["y"], :, lanes_of(half)]
                remote(piece, piece, hw_s.at[half, k, hop - 1], hw_r.at[half, k, hop - 1], me).wait_recv()
        for pair in range(half * 4, half * 4 + 4):
            rows = heads[:, :, :, pair * 256 : (pair + 1) * 256].reshape(256, 256)
            weights = jnp.concatenate([wo[2 * pair], wo[2 * pair + 1]], axis=1)
            total = total + dot_nt(rows, weights)
    t, from_yh, from_z = i & 1, (i >> 1) & 1, (i >> 2) & 3
    source = from_z * 64 + (from_yh * 2 + (i >> 7)) * 16 + ((i >> 4) & 7) * 2 + t
    order = (source == j).astype(BF16)
    part[...] = dot(order, total.astype(BF16)).astype(BF16).reshape(2, 8, 16, 512)
    part_copies = []
    for i_to, to in enumerate(part_to):
        copy = remote(
            part.at[to["y"] % 2, to["x"] * 2 + to["c"]], part_in.at[yl, tp], part_s.at[i_to], part_r.at[i_to], to
        )
        copy.start()
        part_copies.append(copy)
    part_in[yl, tp] = part[yl, tp]
    plane = i >> 7
    to_yl = ((i >> 6) & 1) * (1 - plane) + ((i >> 4) & 1) * plane
    to_x = ((i >> 4) & 3) * (1 - plane) + ((i >> 5) & 3) * plane
    source = from_z * 64 + (from_yh * 2 + to_yl) * 16 + to_x * 4 + plane * 2 + t
    chosen_all[...] = dot((source == j).astype(BF16), heads[:, :, :, 2048:2176].reshape(256, 128)).astype(BF16)
    for copy in hid_copies:
        copy.wait_recv()
    shard[...] = jnp.sum(hid_in[...].astype(F32), axis=(0, 1))
    for copy in part_copies:
        copy.wait_recv()
    sums = jnp.sum(part_in[...].astype(F32), axis=1)
    shard[:, 0:512] += sums[0]
    shard[:, 384:896] += sums[1]
    return ctx_copies + hid_copies + sends + part_copies


def attention_scratch():
    dma = pltpu.SemaphoreType.DMA
    return [
        pltpu.VMEM((2, 576, 128), BF16),
        pltpu.VMEM((2, 576, 1024), BF16),
        pltpu.VMEM((16, 576), F32),
        pltpu.VMEM((2, 8, 16, 512), BF16),
        pltpu.VMEM((16, 512, 128), BF16),
        pltpu.VMEM((16, 512, 128), BF16),
        pltpu.VMEM((8, 2, 16, 512), BF16),
        pltpu.VMEM((4, 4, 16, 2176), BF16),
        pltpu.VMEM((2, 8, 16, 512), BF16),
        pltpu.VMEM((2, 8, 16, 512), BF16),
        pltpu.VMEM((4, 2, 16, BLK), BF16),
        pltpu.VMEM((4, 2, 16, BLK), BF16),
        pltpu.VMEM((16, 128), BF16),
        pltpu.VMEM((8, 16, 128), BF16),
        dma((6,)),
        dma((7,)), dma((7,)), dma((2, 7)), dma((2, 7)), dma((7,)), dma((7,)),
        dma((2, 3)), dma((2, 3)), dma((2, 4, 3)), dma((2, 4, 3)), dma((15,)), dma((15,)),
    ]


def turned(at):
    c = at["c"]
    return dict(
        z=at["z"] * (1 - c) + at["x"] * c, y=at["y"] * (1 - c) + at["z"] * c, x=at["x"] * (1 - c) + at["y"] * c, c=c
    )


def straight(at):
    c = at["c"]
    return dict(
        z=at["z"] * (1 - c) + at["y"] * c, y=at["y"] * (1 - c) + at["x"] * c, x=at["x"] * (1 - c) + at["z"] * c, c=c
    )


def region_of(at, portion, phase):
    start, width, order = PORTIONS[portion]
    done = order[::-1][:phase]
    index = tuple(pl.ds(0, 4) if name in done else at[name] for name in DIMS)
    return index + (slice(None), pl.ds(start, width))


def portion_cut(plane, part, ys, p):
    start, width, order = PORTIONS[p]
    place = (part, ys, slice(None)) if plane == 0 else (slice(None), part, ys)
    return place + (slice(None), pl.ds(start, width))


def plane_cut(plane, part, ys):
    return (part, ys) if plane == 0 else (slice(None), part, ys)


class Layer:
    def __init__(self, me, x_ref, gain_ref, refs):
        self.me, self.x, self.gain = me, x_ref, gain_ref
        self.full, self.partial, self.acc, self.square, *lists = refs
        (
            self.plane_s, self.plane_r, self.slab_s, self.slab_r, self.sum_s, self.sum_r, self.last_s, self.last_r
        ) = lists[9:]
        self.in1, self.held2, self.in2 = [lists[i * 3 : i * 3 + 3] for i in range(3)]
        self.ring = {name: [moved(me, **{name: step}) for step in (1, 2, 3)] for name in DIMS}
        self.back = {name: [moved(me, **{name: 4 - step}) for step in (1, 2, 3)] for name in DIMS}
        self.sends = []

    def begin(self, p, f_me):
        start, width, order = PORTIONS[p]
        me = self.me
        lanes = pl.ds(start, width)
        scaled = self.x[:, lanes] * self.gain[:, pl.ds(pl.multiple_of(f_me * BLK + start, 128), width)]
        self.full[me["z"], me["y"], me["x"], :, lanes] = scaled.astype(BF16)

    def launch(self):
        for k, p in LAUNCH:
            order = PORTIONS[p][2]
            region = self.full.at[region_of(self.me, p, 0)]
            to = straight(moved(self.me, **dict(zip(order[1:], PLANE[k]))))
            copy = remote(region, region, self.plane_s.at[p, k], self.plane_r.at[p, k], to)
            copy.start()
            self.sends.append(copy)

    def gather(self):
        me = self.me
        self.launch()
        for row in (0, 1, 3, 2):
            for p in range(3):
                start, width, order = PORTIONS[p]
                for k, step in enumerate(PLANE):
                    if step[0] == row:
                        there = moved(me, **{name: 4 - by for name, by in zip(order[1:], step)})
                        region = self.full.at[region_of(there, p, 0)]
                        remote(region, region, self.plane_s.at[p, k], self.plane_r.at[p, k], straight(me)).wait_recv()
                region = self.full.at[region_of(moved(me, **{order[1]: 4 - row}), p, 1)]
                for k in (1, 0, 2):
                    to = straight(self.ring[order[0]][k])
                    copy = remote(region, region, self.slab_s.at[p, row, k], self.slab_r.at[p, row, k], to)
                    copy.start()
                    self.sends.append(copy)

    def take(self, p):
        order = PORTIONS[p][2]
        for row in (0, 1, 3, 2):
            for k in (0, 2, 1):
                there = moved(self.back[order[0]][k], **{order[1]: 4 - row})
                region = self.full.at[region_of(there, p, 1)]
                remote(region, region, self.slab_s.at[p, row, k], self.slab_r.at[p, row, k], straight(self.me)).wait_recv()

    def first_sums(self, p, row):
        begin, width, order = PORTIONS[p]
        left = [name for name in DIMS if name != order[0]]
        there = moved(self.me, **{left[0]: row})
        copies = []
        for k in (1, 0, 2):
            to = self.ring[order[0]][k]
            index = dict(there, **{order[0]: to[order[0]], left[1]: slice(None)})
            source = self.partial.at[tuple(index[name] for name in DIMS) + (slice(None), pl.ds(begin, width))]
            into = self.in1[p].at[k, there[left[0]]]
            copies.append(remote(source, into, self.sum_s.at[p, row, k], self.sum_r.at[p, row, k], straight(to)))
        return copies

    def sums(self, finish):
        me = self.me
        second = []
        for row in ROWS:
            for p in range(3):
                begin, width, order = PORTIONS[p]
                for copy in self.first_sums(p, row):
                    copy.wait_recv()
                left = [name for name in DIMS if name != order[0]]
                there = moved(me, **{left[0]: row})
                index = dict(there, **{left[1]: slice(None)})
                value = self.partial[tuple(index[name] for name in DIMS) + (slice(None), pl.ds(begin, width))].astype(F32)
                for k in range(3):
                    value = value + self.in1[p][k, there[left[0]]].astype(F32)
                self.held2[p][there[left[0]]] = value.astype(BF16)
                for k, step in enumerate(PLANE):
                    if step[0] == row:
                        to = moved(me, **dict(zip(left, step)))
                        source = self.held2[p].at[to[left[0]], to[left[1]]]
                        into = self.in2[p].at[k]
                        copy = remote(source, into, self.last_s.at[p, k], self.last_r.at[p, k], straight(to))
                        copy.start()
                        second.append((p, copy))
        for p in range(3):
            begin, width, order = PORTIONS[p]
            for at, copy in second:
                if at == p:
                    copy.wait_recv()
            left = [name for name in DIMS if name != order[0]]
            value = self.held2[p][me[left[0]], me[left[1]]].astype(F32)
            value = value + jnp.sum(self.in2[p][...].astype(F32), axis=0)
            finish(p, begin, width, value + self.x[:, begin : begin + width])
        self.sends += [copy for at, copy in second]

    def run(self, multiply, activate, down, weights):
        self.gather()
        for p in range(3):
            self.take(p)
        for wait in weights:
            wait()
        for plane in (0, 1):

            @pl.when(self.me["c"] == plane)
            def _(plane=plane):
                for f in range(8):
                    rows = self.full[plane_cut(plane, f // 2, slice(f % 2 * 2, f % 2 * 2 + 2))].reshape(128, BLK)
                    at = slice(f * BLK, (f + 1) * BLK)
                    multiply(rows, at, f == 0)
                    plain = rows.astype(F32) * (1.0 / self.gain[:, at])
                    plain = plain * plain
                    piece = plain[:, 0:128]
                    for k in range(1, 7):
                        piece = piece + plain[:, k * 128 : (k + 1) * 128]
                    put(self.square, piece, f == 0)

                scale = lax.rsqrt(jnp.sum(self.square[...], axis=1, keepdims=True) * (1.0 / D) + EPSILON)
                act = activate(plane, scale)
                for p in range(3):
                    start, width, order = PORTIONS[p]
                    for f in range(8):
                        block = down(act, slice(f * BLK + start, f * BLK + start + width)).astype(BF16)
                        shape = (2, 4, 16, width) if plane == 0 else (4, 2, 16, width)
                        ys = slice(f % 2 * 2, f % 2 * 2 + 2)
                        self.partial[portion_cut(plane, f // 2, ys, p)] = block.reshape(shape)
                    for row in ROWS:
                        for copy in self.first_sums(p, row):
                            copy.start()

    def end(self):
        for copy in self.sends:
            copy.wait_send()
        for p in range(3):
            for row in ROWS:
                for copy in self.first_sums(p, row):
                    copy.wait_send()


def put(ref, value, first):
    if first:
        ref[...] = value
    else:
        ref[...] += value


def silu(value):
    return value / (1.0 + jnp.exp(-value))


def layer_kernel(
    len_ref, nl_ref, hid_ref, ids_ref, gain1_ref, gain2_ref, wr_ref, q_hbm, cache_hbm, wv_hbm, wo_hbm,
    wg1_hbm, wu1_hbm, wd1_hbm, wg2_hbm, wu2_hbm, wd2_hbm, out_ref,
    up1, down1, up2, down2, x_ref, chosen_ref, mid, router_acc, own, packed, final_in, load_sem, give_s, give_r, final_s, final_r,
    *refs,
):
    here = coords()
    f_me = here["z"] * 2 + here["y"] // 2
    yh = here["y"] // 2
    me = turned(here)
    sibling = moved(here, c=1)
    n1, n2 = wd1_hbm.shape[0], wd2_hbm.shape[0]
    sources = (wg1_hbm, wu1_hbm, wd1_hbm, wg2_hbm, wu2_hbm, wd2_hbm)

    def places(k):
        return (
            up1.at[pl.ds(k * n1, n1), :], up1.at[pl.ds((2 + k) * n1, n1), :], down1.at[pl.ds(k * n1, n1), :],
            up2.at[k], up2.at[2 + k], down2.at[pl.ds(k * n2, n2), :],
        )

    loads = [pltpu.make_async_copy(src, dst, load_sem.at[i]) for i, (src, dst) in enumerate(zip(sources, places(0)))]
    gives = [
        remote(src, dst, give_s.at[i], give_r.at[i], sibling) for i, (src, dst) in enumerate(zip(sources, places(1)))
    ]
    count = len(attention_scratch())
    attention_refs, refs = refs[:count], refs[count:]
    half = len(refs) // 2
    dense = Layer(me, x_ref, gain1_ref, refs[:half])
    routed = Layer(me, mid, gain2_ref, refs[half:])
    final_steps = [(dz, dy) for dz in (2, 1, 3, 0) for dy in (2, 0) if dz or dy]
    final_to = [moved(here, z=dz, y=dy) for dz, dy in final_steps]
    partners = [moved(here, **{name: step}) for name in DIMS for step in (1, 2, 3)] + [sibling]
    for one, two in (("x", "y"), ("y", "z"), ("z", "x")):
        partners += [moved(here, **{one: i, two: j}) for i in (1, 2, 3) for j in (1, 2, 3)]
    partners += [moved(here, x=i, c=1) for i in (1, 2, 3)]
    across = dict(here, y=yh * 2 + (1 - here["y"] % 2), c=1 - here["c"])
    partners += [moved(across, x=i) for i in range(4)]

    def early():
        for load in loads:
            load.start()
        for give in gives[:3]:
            give.start()

    sent = attention_part(
        here, len_ref, nl_ref, hid_ref, ids_ref, wv_hbm, wo_hbm, q_hbm, cache_hbm, x_ref, chosen_ref, attention_refs,
        partners, early,
    )
    for p in range(3):
        dense.begin(p, f_me)
    for give in gives[3:]:
        give.start()
    def multiply_dense(rows, at, first):
        put(dense.acc, dot_nt(up1[:, at], rows), first)

    def activate_dense(plane, scale):
        gate, up = dense.acc[0 : 2 * n1, :].T, dense.acc[2 * n1 :, :].T
        return (silu(gate * scale) * (up * scale)).astype(BF16)

    def down_dense(act, at):
        return dot(act, down1[:, at])

    dense.run(multiply_dense, activate_dense, down_dense, [q.wait for q in loads[:3]] + [q.wait_recv for q in gives[:3]])

    def between(p, begin, width, value):
        mid[:, begin : begin + width] = value
        routed.begin(p, f_me)

    dense.sums(between)
    def multiply_routed(rows, at, first):
        for k in range(4):
            put(routed.acc.at[:, k * n2 : (k + 1) * n2], dot(rows, up2[k, at, :]), first)
        put(router_acc, dot_nt(rows, wr_ref[:, at]), first)

    def activate_routed(plane, scale):
        affinity = 1.0 / (1.0 + jnp.exp(-(router_acc[...] * scale)))
        chosen = chosen_ref[plane * 128 : plane * 128 + 128, 0:16].astype(F32)
        picked = jnp.where(chosen > 0.5, affinity, 0.0)
        below = jnp.sum(picked, axis=1, keepdims=True)
        mine = lax.broadcasted_iota(jnp.int32, (128, 16), 1) == here["z"] * 4 + here["y"]
        weight = ROUTE_SCALE * jnp.sum(jnp.where(mine, picked, 0.0), axis=1, keepdims=True) / below
        wanted = jnp.sum(jnp.where(mine, chosen, 0.0), axis=1, keepdims=True) > 0.5
        act = silu(routed.acc[:, : 2 * n2] * scale) * (routed.acc[:, 2 * n2 :] * scale)
        return jnp.where(wanted, act * weight, 0.0).astype(BF16)

    def down_routed(act, at):
        return dot(act, down2[:, at])

    routed.run(multiply_routed, activate_routed, down_routed, [q.wait for q in loads[3:]] + [q.wait_recv for q in gives[3:]])

    def last(p, begin, width, value):
        own[:, begin : begin + width] = value.astype(BF16)

    routed.sums(last)

    tiles = [own[:, k * 128 : (k + 1) * 128] for k in range(7)] + [jnp.zeros((16, 128), BF16)]
    i = lax.broadcasted_iota(jnp.int32, (128, 128), 0)
    j = lax.broadcasted_iota(jnp.int32, (128, 128), 1)
    spot = i & 15
    token = (spot >= 7).astype(jnp.int32)
    source = (spot - 7 * token) * 16 + (i >> 4) * 2 + token
    pick = jnp.where(spot < 14, source, -1) == j
    packed[...] = dot(pick.astype(BF16), jnp.concatenate(tiles, axis=0)).astype(BF16).reshape(4, 2, 16, 128)
    final_copies = []
    for i, to in enumerate(final_to):
        copy = remote(packed.at[to["z"], to["y"] // 2], final_in.at[here["z"], yh], final_s.at[i], final_r.at[i], to)
        copy.start()
        final_copies.append(copy)
    final_in[here["z"], yh] = packed[here["z"], yh]
    for copy in final_copies:
        copy.wait_recv()
    for f in range(8):
        block = final_in[f // 2, f % 2].astype(F32)
        both = [jnp.concatenate([block[t * 7 + k : t * 7 + k + 1, :] for k in range(7)], axis=1) for t in range(2)]
        out_ref[:, f * BLK : (f + 1) * BLK] = jnp.concatenate(both, axis=0).astype(BF16)
    for copy in final_copies:
        copy.wait_send()
    for give in gives:
        give.wait_send()
    for copy in sent:
        copy.wait_send()
    dense.end()
    routed.end()


def layer_scratch(products):
    dma = pltpu.SemaphoreType.DMA
    widths = [width for _, width, _ in PORTIONS]
    return (
        [
            pltpu.VMEM((4, 4, 4, 16, BLK), BF16),
            pltpu.VMEM((4, 4, 4, 16, BLK), BF16),
            pltpu.VMEM(products, F32),
            pltpu.VMEM((128, 128), F32),
        ]
        + [pltpu.VMEM((3, 4, 4, 16, width), BF16) for width in widths]
        + [pltpu.VMEM((4, 4, 16, width), BF16) for width in widths]
        + [pltpu.VMEM((15, 16, width), BF16) for width in widths]
        + [dma((3, 15)), dma((3, 15)), dma((3, 4, 3)), dma((3, 4, 3)), dma((3, 4, 3)), dma((3, 4, 3)), dma((3, 15)), dma((3, 15))]
    )


def layer(lengths, latent, hidden, ids, gain1, gain2, w_router, queries, cache, w_values, w_out, dense, expert):
    any_space = pl.BlockSpec(memory_space=pl.ANY)
    vmem = pl.BlockSpec(memory_space=pltpu.VMEM)
    dma = pltpu.SemaphoreType.DMA
    n1, n2 = dense[2].shape[0], expert[2].shape[0]
    return pl.pallas_call(
        layer_kernel,
        out_shape=jax.ShapeDtypeStruct((2, D), BF16),
        in_specs=[pl.BlockSpec(memory_space=pltpu.SMEM)] + [vmem] * 6 + [any_space] * 10,
        out_specs=vmem,
        scratch_shapes=[
            pltpu.VMEM((4 * n1, D), BF16),
            pltpu.VMEM((2 * n1, D), BF16),
            pltpu.VMEM((4, D, n2), BF16),
            pltpu.VMEM((2 * n2, D), BF16),
            pltpu.VMEM((16, BLK), F32),
            pltpu.VMEM((256, 128), BF16),
            pltpu.VMEM((16, BLK), F32),
            pltpu.VMEM((128, 16), F32),
            pltpu.VMEM((16, BLK), BF16),
            pltpu.VMEM((4, 2, 16, 128), BF16),
            pltpu.VMEM((4, 2, 16, 128), BF16),
            dma((6,)), dma((6,)), dma((6,)), dma((7,)), dma((7,)),
        ]
        + attention_scratch()
        + layer_scratch((4 * n1, 128))
        + layer_scratch((128, 4 * n2)),
        compiler_params=pltpu.CompilerParams(collective_id=0, has_side_effects=True, vmem_limit_bytes=VMEM_LIMIT),
        name="decode_layer",
    )(
        lengths, latent, hidden, ids, gain1, gain2, w_router, queries, cache, w_values, w_out, *dense, *expert
    )


def body(
    hidden,
    queries,
    cache,
    new_latent,
    lengths,
    w_values,
    w_out,
    gain_attn,
    w_dense_gate,
    w_dense_up,
    w_dense_down,
    gain_moe,
    w_router,
    expert_ids,
    w_expert_gate,
    w_expert_up,
    w_expert_down,
):
    out = layer(
        lengths,
        new_latent,
        hidden,
        expert_ids,
        gain_attn.reshape(1, D),
        gain_moe.reshape(1, D),
        w_router.T,
        jnp.swapaxes(queries, 1, 2),
        jnp.swapaxes(cache, 1, 2),
        w_values,
        jnp.swapaxes(w_out, 1, 2),
        (w_dense_gate.T, w_dense_up.T, w_dense_down),
        (w_expert_gate[0], w_expert_up[0], w_expert_down[0]),
    )
    return out


def solution(mesh):
    in_specs = (
        P(("tp", "ep"), None),
        P(("tp", "ep"), None, None),
        P(("tp", "ep"), None, None),
        P(("tp", "ep"), None),
        P(("tp", "ep")),
        P("tp", None, None),
        P("tp", None, "ep"),
        P(),
        P(None, ("tp", "ep")),
        P(None, ("tp", "ep")),
        P(("tp", "ep"), None),
        P(),
        P(),
        P(("tp", "ep"), None),
        P("ep", None, "tp"),
        P("ep", None, "tp"),
        P("ep", "tp", None),
    )
    out_specs = P(("tp", "ep"), None)
    return jax.shard_map(body, mesh=mesh, in_specs=in_specs, out_specs=out_specs, check_vma=False)
```

```python
import jax
import jax.numpy as jnp
from jax import lax
from jax.experimental import pallas as pl
from jax.experimental.pallas import tpu as pltpu
from jax.sharding import PartitionSpec as P

ROPE = 64
VD = 128
D = 7168
BLK = 896
EPSILON = 1e-06
ROUTE_SCALE = 2.5
MESH = pl.DeviceIdType.MESH
F32 = jnp.float32
BF16 = jnp.bfloat16
VMEM_LIMIT = 60 * 2**20


PORTIONS = ((0, 384, ("x", "y", "z")), (384, 256, ("y", "z", "x")), (640, 256, ("z", "x", "y")))
DIMS = ("z", "y", "x")
PLANE = sorted(((i, j) for i in range(4) for j in range(4) if i or j), key=lambda d: -sum(min(k, 4 - k) for k in d))

ROWS = (2, 1, 3, 0)

LAUNCH = [(k, p) for k in sorted(range(15), key=lambda k: (PLANE[k][0] != 0, k)) for p in range(3)]


def coords():
    tp, ep = lax.axis_index("tp"), lax.axis_index("ep")
    return dict(x=tp // 2, c=tp % 2, z=ep // 4, y=ep % 4)


def device(at):
    return (at["x"] * 2 + at["c"], at["z"] * 4 + at["y"])


def moved(at, **steps):
    new = dict(at)
    for name, step in steps.items():
        new[name] = lax.rem(at[name] + step, 2 if name == "c" else 4)
    return new


def greet(partners):
    barrier = pltpu.get_barrier_semaphore()
    for partner in partners:
        pl.semaphore_signal(barrier, inc=1, device_id=device(partner), device_id_type=MESH)


def gathered(partners):
    pl.semaphore_wait(pltpu.get_barrier_semaphore(), len(partners))


def remote(src, dst, send, recv, partner):
    return pltpu.make_async_remote_copy(
        src_ref=src, dst_ref=dst, send_sem=send, recv_sem=recv, device_id=device(partner), device_id_type=MESH
    )


def dot_nt(a, b):
    return lax.dot_general(a, b, (((1,), (1,)), ((), ())), preferred_element_type=F32)


def dot(a, b):
    return jnp.dot(a, b, preferred_element_type=F32)


def attend(t, q, cache, latent, length):
    scale = (VD + ROPE) ** (-0.5)
    scores = lax.dot_general(q[t], cache[t], (((0,), (0,)), ((), ())), preferred_element_type=F32) * scale
    own = lax.dot_general(q[t], latent, (((0,), (1,)), ((), ())), preferred_element_type=F32) * scale
    own = own[:, t : t + 1]
    place = lax.broadcasted_iota(jnp.int32, scores.shape, 1)
    scores = jnp.where(place < length, scores, -jnp.inf)
    peak = jnp.maximum(jnp.max(scores, axis=1, keepdims=True), own)
    weights = jnp.exp(scores - peak)
    own_weight = jnp.exp(own - peak)
    total = jnp.sum(weights, axis=1, keepdims=True) + own_weight
    probability = (weights / total).astype(BF16)
    own_probability = (own_weight / total).astype(BF16).astype(F32)
    context = dot_nt(probability, cache[t, 0:512, :])
    return (context + own_probability * latent[t : t + 1, 0:512].astype(F32)).astype(BF16)


def attention_part(me, len_ref, nl_ref, hid_ref, ids_ref, wv_hbm, wo_hbm, q_hbm, cache_hbm, shard, chosen_all, refs, meeting, early):
    (
        q, cache, latent, ctx, wv, wo, ctx_in, heads, part, part_in, hid_out, hid_in, mask_out, mask_in, load_sem,
        hid_s, hid_r, ctx_s, ctx_r, mask_s, mask_r, hv_s, hv_r, hw_s, hw_r, part_s, part_r,
    ) = refs
    x, c, z, y = me["x"], me["c"], me["z"], me["y"]
    yh, yl = y // 2, y % 2
    tp = x * 2 + c
    pad = pl.multiple_of(yl * 64, 64)
    requests = []
    for t in range(2):
        pairs = ((q_hbm.at[t], q.at[t]), (cache_hbm.at[t], cache.at[t]))
        requests.append([pltpu.make_async_copy(src, dst, load_sem.at[t * 2 + k]) for k, (src, dst) in enumerate(pairs)])
    load_wv = pltpu.make_async_copy(wv_hbm, wv, load_sem.at[4])
    load_wo = pltpu.make_async_copy(wo_hbm, wo.at[:, pl.ds(pad, 448), :], load_sem.at[5])
    for load in requests[0] + requests[1] + [load_wv, load_wo]:
        load.start()

    def at_tp(step):
        other = lax.rem(tp + step, 8)
        return dict(me, x=other // 2, c=other % 2)

    tp_steps = [(dt, dy) for dy in (1, 0) for dt in (4, 5, 3, 2, 6, 7, 1, 0) if dt or dy]
    part_to = [dict(at_tp(dt), y=yh * 2 + (yl + dy) % 2) for dt, dy in tp_steps]
    hid_steps = [(dz, dy) for dy in (0, 2) for dz in range(4) if dz or dy]
    hid_to = [moved(me, z=dz, y=dy) for dz, dy in hid_steps]
    greet(meeting)
    wo[:, pl.ds(pl.multiple_of((1 - yl) * 448, 64), 64), :] = jnp.zeros((16, 64, 128), BF16)
    latent[...] = jnp.zeros_like(latent)
    latent[0:2, :] = nl_ref[...].astype(F32)
    latents = latent[...].astype(BF16)
    ctx_copies = []
    for t in range(2):
        for load in requests[t]:
            load.wait()
        ctx[t] = attend(t, q, cache, latents, len_ref[t]).reshape(8, 16, 512)
        if t == 0:
            gathered(meeting)
        for step in (4, 3, 5, 2, 6, 1, 7):
            to = at_tp(step)
            source, into = ctx.at[t, to["x"] * 2 + to["c"]], ctx_in.at[tp, t]
            copy = remote(source, into, ctx_s.at[t, step - 1], ctx_r.at[t, step - 1], to)
            copy.start()
            ctx_copies.append(copy)

    first = (z * 2 + yh) * 2
    row = lax.broadcasted_iota(jnp.int32, (16, BLK), 0)
    for f in range(8):
        both = hid_ref[:, f * BLK : (f + 1) * BLK].astype(F32)
        placed = jnp.where(row == first, both[0:1, :], jnp.where(row == first + 1, both[1:2, :], 0.0))
        hid_out[f // 2, f % 2] = placed.astype(BF16)
    lane = lax.broadcasted_iota(jnp.int32, (2, 128), 1)
    chosen = jnp.zeros((2, 128), F32)
    for k in range(ids_ref.shape[1]):
        chosen = chosen + jnp.where(ids_ref[:, k : k + 1] == lane, 1.0, 0.0)
    row = lax.broadcasted_iota(jnp.int32, (16, 128), 0)
    placed = jnp.where(row == tp * 2, chosen[0:1, :], jnp.where(row == tp * 2 + 1, chosen[1:2, :], 0.0))
    mask_out[...] = placed.astype(BF16)
    for step in range(1, 8):
        copy = remote(mask_out, mask_in.at[tp], mask_s.at[step - 1], mask_r.at[step - 1], at_tp(step))
        copy.start()
        ctx_copies.append(copy)
    hid_copies = []
    for i, to in enumerate(hid_to):
        copy = remote(hid_out.at[to["z"], to["y"] // 2], hid_in.at[z, yh], hid_s.at[i], hid_r.at[i], to)
        copy.start()
        hid_copies.append(copy)
    ctx_in[tp] = ctx[:, tp]
    mask_in[tp] = mask_out[...]
    hid_in[z, yh] = hid_out[z, yh]
    for copy in ctx_copies:
        copy.wait_recv()
    load_wv.wait()
    early()

    i = lax.broadcasted_iota(jnp.int32, (256, 256), 0)
    j = lax.broadcasted_iota(jnp.int32, (256, 256), 1)
    turn = ((i & 15) * 16 + (i >> 4) == j).astype(BF16)
    by_head = dot(turn, ctx_in[...].reshape(256, 512)).astype(BF16)
    halves = ((0, "z", "y"), (1, "y", "z"))
    sends = []

    def lanes_of(half):
        return pl.ds(half * 1024, 1024 + half * 128)

    for half, one, two in halves:
        for h in range(half * 8, half * 8 + 8):
            heads[z, y, :, h * 128 : (h + 1) * 128] = dot(by_head[h * 16 : (h + 1) * 16, :], wv[h]).astype(BF16)
        if half:
            heads[z, y, :, 2048:2176] = jnp.sum(mask_in[...].astype(F32), axis=0).astype(BF16)
        mine = heads.at[z, y, :, lanes_of(half)]
        for k in (2, 1, 3):
            to = moved(me, **{one: k})
            sends.append(remote(mine, mine, hv_s.at[half, k - 1], hv_r.at[half, k - 1], to))
            sends[-1].start()
        for k in (2, 1, 3):
            to = moved(me, **{two: k})
            sends.append(remote(mine, mine, hw_s.at[half, 0, k - 1], hw_r.at[half, 0, k - 1], to))
            sends[-1].start()
    for k in (1, 3, 2):
        for half, one, two in halves:
            there = moved(me, **{one: 4 - k})
            piece = heads.at[there["z"], there["y"], :, lanes_of(half)]
            remote(piece, piece, hv_s.at[half, k - 1], hv_r.at[half, k - 1], me).wait_recv()
            for hop in (2, 1, 3):
                to = moved(me, **{two: hop})
                sends.append(remote(piece, piece, hw_s.at[half, k, hop - 1], hw_r.at[half, k, hop - 1], to))
                sends[-1].start()
    load_wo.wait()

    total = jnp.zeros((256, 512), F32)
    for half, one, two in halves:
        for k in range(4):
            for hop in (1, 3, 2):
                there = moved(me, **{one: (4 - k) % 4, two: 4 - hop})
                piece = heads.at[there["z"], there["y"], :, lanes_of(half)]
                remote(piece, piece, hw_s.at[half, k, hop - 1], hw_r.at[half, k, hop - 1], me).wait_recv()
        for pair in range(half * 4, half * 4 + 4):
            rows = heads[:, :, :, pair * 256 : (pair + 1) * 256].reshape(256, 256)
            weights = jnp.concatenate([wo[2 * pair], wo[2 * pair + 1]], axis=1)
            total = total + dot_nt(rows, weights)
    t, from_yh, from_z = i & 1, (i >> 1) & 1, (i >> 2) & 3
    source = from_z * 64 + (from_yh * 2 + (i >> 7)) * 16 + ((i >> 4) & 7) * 2 + t
    order = (source == j).astype(BF16)
    part[...] = dot(order, total.astype(BF16)).astype(BF16).reshape(2, 8, 16, 512)
    part_copies = []
    for i_to, to in enumerate(part_to):
        copy = remote(
            part.at[to["y"] % 2, to["x"] * 2 + to["c"]], part_in.at[yl, tp], part_s.at[i_to], part_r.at[i_to], to
        )
        copy.start()
        part_copies.append(copy)
    part_in[yl, tp] = part[yl, tp]
    plane = i >> 7
    to_yl = ((i >> 6) & 1) * (1 - plane) + ((i >> 4) & 1) * plane
    to_x = ((i >> 4) & 3) * (1 - plane) + ((i >> 5) & 3) * plane
    source = from_z * 64 + (from_yh * 2 + to_yl) * 16 + to_x * 4 + plane * 2 + t
    chosen_all[...] = dot((source == j).astype(BF16), heads[:, :, :, 2048:2176].reshape(256, 128)).astype(BF16)
    for copy in hid_copies:
        copy.wait_recv()
    shard[...] = jnp.sum(hid_in[...].astype(F32), axis=(0, 1))
    for copy in part_copies:
        copy.wait_recv()
    sums = jnp.sum(part_in[...].astype(F32), axis=1)
    shard[:, 0:512] += sums[0]
    shard[:, 384:896] += sums[1]
    return ctx_copies + hid_copies + sends + part_copies


def attention_scratch():
    dma = pltpu.SemaphoreType.DMA
    return [
        pltpu.VMEM((2, 576, 128), BF16),
        pltpu.VMEM((2, 576, 1024), BF16),
        pltpu.VMEM((16, 576), F32),
        pltpu.VMEM((2, 8, 16, 512), BF16),
        pltpu.VMEM((16, 512, 128), BF16),
        pltpu.VMEM((16, 512, 128), BF16),
        pltpu.VMEM((8, 2, 16, 512), BF16),
        pltpu.VMEM((4, 4, 16, 2176), BF16),
        pltpu.VMEM((2, 8, 16, 512), BF16),
        pltpu.VMEM((2, 8, 16, 512), BF16),
        pltpu.VMEM((4, 2, 16, BLK), BF16),
        pltpu.VMEM((4, 2, 16, BLK), BF16),
        pltpu.VMEM((16, 128), BF16),
        pltpu.VMEM((8, 16, 128), BF16),
        dma((6,)),
        dma((7,)), dma((7,)), dma((2, 7)), dma((2, 7)), dma((7,)), dma((7,)),
        dma((2, 3)), dma((2, 3)), dma((2, 4, 3)), dma((2, 4, 3)), dma((15,)), dma((15,)),
    ]


def turned(at):
    c = at["c"]
    return dict(
        z=at["z"] * (1 - c) + at["x"] * c, y=at["y"] * (1 - c) + at["z"] * c, x=at["x"] * (1 - c) + at["y"] * c, c=c
    )


def straight(at):
    c = at["c"]
    return dict(
        z=at["z"] * (1 - c) + at["y"] * c, y=at["y"] * (1 - c) + at["x"] * c, x=at["x"] * (1 - c) + at["z"] * c, c=c
    )


def region_of(at, portion, phase):
    start, width, order = PORTIONS[portion]
    done = order[::-1][:phase]
    index = tuple(pl.ds(0, 4) if name in done else at[name] for name in DIMS)
    return index + (slice(None), pl.ds(start, width))


def portion_cut(plane, part, ys, p):
    start, width, order = PORTIONS[p]
    place = (part, ys, slice(None)) if plane == 0 else (slice(None), part, ys)
    return place + (slice(None), pl.ds(start, width))


def plane_cut(plane, part, ys):
    return (part, ys) if plane == 0 else (slice(None), part, ys)


class Layer:
    def __init__(self, me, x_ref, gain_ref, refs):
        self.me, self.x, self.gain = me, x_ref, gain_ref
        self.full, self.partial, self.acc, self.square, *lists = refs
        (
            self.plane_s, self.plane_r, self.slab_s, self.slab_r, self.sum_s, self.sum_r, self.last_s, self.last_r
        ) = lists[9:]
        self.in1, self.held2, self.in2 = [lists[i * 3 : i * 3 + 3] for i in range(3)]
        self.ring = {name: [moved(me, **{name: step}) for step in (1, 2, 3)] for name in DIMS}
        self.back = {name: [moved(me, **{name: 4 - step}) for step in (1, 2, 3)] for name in DIMS}
        self.sends = []

    def begin(self, p, f_me):
        start, width, order = PORTIONS[p]
        me = self.me
        lanes = pl.ds(start, width)
        scaled = self.x[:, lanes] * self.gain[:, pl.ds(pl.multiple_of(f_me * BLK + start, 128), width)]
        self.full[me["z"], me["y"], me["x"], :, lanes] = scaled.astype(BF16)

    def launch(self):
        for k, p in LAUNCH:
            order = PORTIONS[p][2]
            region = self.full.at[region_of(self.me, p, 0)]
            to = straight(moved(self.me, **dict(zip(order[1:], PLANE[k]))))
            copy = remote(region, region, self.plane_s.at[p, k], self.plane_r.at[p, k], to)
            copy.start()
            self.sends.append(copy)

    def gather(self):
        me = self.me
        self.launch()
        for row in (0, 1, 3, 2):
            for p in range(3):
                start, width, order = PORTIONS[p]
                for k, step in enumerate(PLANE):
                    if step[0] == row:
                        there = moved(me, **{name: 4 - by for name, by in zip(order[1:], step)})
                        region = self.full.at[region_of(there, p, 0)]
                        remote(region, region, self.plane_s.at[p, k], self.plane_r.at[p, k], straight(me)).wait_recv()
                region = self.full.at[region_of(moved(me, **{order[1]: 4 - row}), p, 1)]
                for k in (1, 0, 2):
                    to = straight(self.ring[order[0]][k])
                    copy = remote(region, region, self.slab_s.at[p, row, k], self.slab_r.at[p, row, k], to)
                    copy.start()
                    self.sends.append(copy)

    def take(self, p):
        order = PORTIONS[p][2]
        for row in (0, 1, 3, 2):
            for k in (0, 2, 1):
                there = moved(self.back[order[0]][k], **{order[1]: 4 - row})
                region = self.full.at[region_of(there, p, 1)]
                remote(region, region, self.slab_s.at[p, row, k], self.slab_r.at[p, row, k], straight(self.me)).wait_recv()

    def first_sums(self, p, row):
        begin, width, order = PORTIONS[p]
        left = [name for name in DIMS if name != order[0]]
        there = moved(self.me, **{left[0]: row})
        copies = []
        for k in (1, 0, 2):
            to = self.ring[order[0]][k]
            index = dict(there, **{order[0]: to[order[0]], left[1]: slice(None)})
            source = self.partial.at[tuple(index[name] for name in DIMS) + (slice(None), pl.ds(begin, width))]
            into = self.in1[p].at[k, there[left[0]]]
            copies.append(remote(source, into, self.sum_s.at[p, row, k], self.sum_r.at[p, row, k], straight(to)))
        return copies

    def sums(self, finish):
        me = self.me
        second = []
        for row in ROWS:
            for p in range(3):
                begin, width, order = PORTIONS[p]
                for copy in self.first_sums(p, row):
                    copy.wait_recv()
                left = [name for name in DIMS if name != order[0]]
                there = moved(me, **{left[0]: row})
                index = dict(there, **{left[1]: slice(None)})
                value = self.partial[tuple(index[name] for name in DIMS) + (slice(None), pl.ds(begin, width))].astype(F32)
                for k in range(3):
                    value = value + self.in1[p][k, there[left[0]]].astype(F32)
                self.held2[p][there[left[0]]] = value.astype(BF16)
                for k, step in enumerate(PLANE):
                    if step[0] == row:
                        to = moved(me, **dict(zip(left, step)))
                        source = self.held2[p].at[to[left[0]], to[left[1]]]
                        into = self.in2[p].at[k]
                        copy = remote(source, into, self.last_s.at[p, k], self.last_r.at[p, k], straight(to))
                        copy.start()
                        second.append((p, copy))
        for p in range(3):
            begin, width, order = PORTIONS[p]
            for at, copy in second:
                if at == p:
                    copy.wait_recv()
            left = [name for name in DIMS if name != order[0]]
            value = self.held2[p][me[left[0]], me[left[1]]].astype(F32)
            value = value + jnp.sum(self.in2[p][...].astype(F32), axis=0)
            finish(p, begin, width, value + self.x[:, begin : begin + width])
        self.sends += [copy for at, copy in second]

    def run(self, multiply, activate, down, weights):
        self.gather()
        for wait in weights:
            wait()
        for portions, start, width in (((1, 2), 384, 512), ((0,), 0, 384)):
            for p in portions:
                self.take(p)
            for plane in (0, 1):

                @pl.when(self.me["c"] == plane)
                def _(plane=plane, start=start, width=width):
                    for f in range(8):
                        place = plane_cut(plane, f // 2, slice(f % 2 * 2, f % 2 * 2 + 2))
                        place += (slice(None),) * (4 - len(place)) + (slice(start, start + width),)
                        rows = self.full[place].reshape(128, width)
                        at = slice(f * BLK + start, f * BLK + start + width)
                        first = f == 0 and start > 0
                        multiply(rows, at, first)
                        plain = rows.astype(F32) * (1.0 / self.gain[:, at])
                        plain = plain * plain
                        piece = plain[:, 0:128]
                        for k in range(1, width // 128):
                            piece = piece + plain[:, k * 128 : (k + 1) * 128]
                        put(self.square, piece, first)

        for plane in (0, 1):

            @pl.when(self.me["c"] == plane)
            def _(plane=plane):
                scale = lax.rsqrt(jnp.sum(self.square[...], axis=1, keepdims=True) * (1.0 / D) + EPSILON)
                act = activate(plane, scale)
                for p in range(3):
                    start, width, order = PORTIONS[p]
                    for f in range(8):
                        block = down(act, slice(f * BLK + start, f * BLK + start + width)).astype(BF16)
                        shape = (2, 4, 16, width) if plane == 0 else (4, 2, 16, width)
                        ys = slice(f % 2 * 2, f % 2 * 2 + 2)
                        self.partial[portion_cut(plane, f // 2, ys, p)] = block.reshape(shape)
                    for row in ROWS:
                        for copy in self.first_sums(p, row):
                            copy.start()

    def end(self):
        for copy in self.sends:
            copy.wait_send()
        for p in range(3):
            for row in ROWS:
                for copy in self.first_sums(p, row):
                    copy.wait_send()


def put(ref, value, first):
    if first:
        ref[...] = value
    else:
        ref[...] += value


def silu(value):
    return value / (1.0 + jnp.exp(-value))


def layer_kernel(
    len_ref, nl_ref, hid_ref, ids_ref, gain1_ref, gain2_ref, wr_ref, q_hbm, cache_hbm, wv_hbm, wo_hbm,
    wg1_hbm, wu1_hbm, wd1_hbm, wg2_hbm, wu2_hbm, wd2_hbm, out_ref,
    up1, down1, up2, down2, x_ref, chosen_ref, mid, router_acc, own, packed, final_in, load_sem, give_s, give_r, final_s, final_r,
    *refs,
):
    here = coords()
    f_me = here["z"] * 2 + here["y"] // 2
    yh = here["y"] // 2
    me = turned(here)
    sibling = moved(here, c=1)
    n1, n2 = wd1_hbm.shape[0], wd2_hbm.shape[0]
    sources = (wg1_hbm, wu1_hbm, wd1_hbm, wg2_hbm, wu2_hbm, wd2_hbm)

    def places(k):
        return (
            up1.at[pl.ds(k * n1, n1), :], up1.at[pl.ds((2 + k) * n1, n1), :], down1.at[pl.ds(k * n1, n1), :],
            up2.at[k], up2.at[2 + k], down2.at[pl.ds(k * n2, n2), :],
        )

    loads = [pltpu.make_async_copy(src, dst, load_sem.at[i]) for i, (src, dst) in enumerate(zip(sources, places(0)))]
    gives = [
        remote(src, dst, give_s.at[i], give_r.at[i], sibling) for i, (src, dst) in enumerate(zip(sources, places(1)))
    ]
    count = len(attention_scratch())
    attention_refs, refs = refs[:count], refs[count:]
    half = len(refs) // 2
    dense = Layer(me, x_ref, gain1_ref, refs[:half])
    routed = Layer(me, mid, gain2_ref, refs[half:])
    final_steps = [(dz, dy) for dz in (2, 1, 3, 0) for dy in (2, 0) if dz or dy]
    final_to = [moved(here, z=dz, y=dy) for dz, dy in final_steps]
    partners = [moved(here, **{name: step}) for name in DIMS for step in (1, 2, 3)] + [sibling]
    for one, two in (("x", "y"), ("y", "z"), ("z", "x")):
        partners += [moved(here, **{one: i, two: j}) for i in (1, 2, 3) for j in (1, 2, 3)]
    partners += [moved(here, x=i, c=1) for i in (1, 2, 3)]
    across = dict(here, y=yh * 2 + (1 - here["y"] % 2), c=1 - here["c"])
    partners += [moved(across, x=i) for i in range(4)]

    def early():
        for load in loads:
            load.start()
        for give in gives[:3]:
            give.start()

    sent = attention_part(
        here, len_ref, nl_ref, hid_ref, ids_ref, wv_hbm, wo_hbm, q_hbm, cache_hbm, x_ref, chosen_ref, attention_refs,
        partners, early,
    )
    for p in range(3):
        dense.begin(p, f_me)
    for give in gives[3:]:
        give.start()
    def multiply_dense(rows, at, first):
        put(dense.acc, dot_nt(up1[:, at], rows), first)

    def activate_dense(plane, scale):
        gate, up = dense.acc[0 : 2 * n1, :].T, dense.acc[2 * n1 :, :].T
        return (silu(gate * scale) * (up * scale)).astype(BF16)

    def down_dense(act, at):
        return dot(act, down1[:, at])

    dense.run(multiply_dense, activate_dense, down_dense, [q.wait for q in loads[:3]] + [q.wait_recv for q in gives[:3]])

    def between(p, begin, width, value):
        mid[:, begin : begin + width] = value
        routed.begin(p, f_me)

    dense.sums(between)
    def multiply_routed(rows, at, first):
        for k in range(4):
            put(routed.acc.at[:, k * n2 : (k + 1) * n2], dot(rows, up2[k, at, :]), first)
        put(router_acc, dot_nt(rows, wr_ref[:, at]), first)

    def activate_routed(plane, scale):
        affinity = 1.0 / (1.0 + jnp.exp(-(router_acc[...] * scale)))
        chosen = chosen_ref[plane * 128 : plane * 128 + 128, 0:16].astype(F32)
        picked = jnp.where(chosen > 0.5, affinity, 0.0)
        below = jnp.sum(picked, axis=1, keepdims=True)
        mine = lax.broadcasted_iota(jnp.int32, (128, 16), 1) == here["z"] * 4 + here["y"]
        weight = ROUTE_SCALE * jnp.sum(jnp.where(mine, picked, 0.0), axis=1, keepdims=True) / below
        wanted = jnp.sum(jnp.where(mine, chosen, 0.0), axis=1, keepdims=True) > 0.5
        act = silu(routed.acc[:, : 2 * n2] * scale) * (routed.acc[:, 2 * n2 :] * scale)
        return jnp.where(wanted, act * weight, 0.0).astype(BF16)

    def down_routed(act, at):
        return dot(act, down2[:, at])

    routed.run(multiply_routed, activate_routed, down_routed, [q.wait for q in loads[3:]] + [q.wait_recv for q in gives[3:]])

    def last(p, begin, width, value):
        own[:, begin : begin + width] = value.astype(BF16)

    routed.sums(last)

    tiles = [own[:, k * 128 : (k + 1) * 128] for k in range(7)] + [jnp.zeros((16, 128), BF16)]
    i = lax.broadcasted_iota(jnp.int32, (128, 128), 0)
    j = lax.broadcasted_iota(jnp.int32, (128, 128), 1)
    spot = i & 15
    token = (spot >= 7).astype(jnp.int32)
    source = (spot - 7 * token) * 16 + (i >> 4) * 2 + token
    pick = jnp.where(spot < 14, source, -1) == j
    packed[...] = dot(pick.astype(BF16), jnp.concatenate(tiles, axis=0)).astype(BF16).reshape(4, 2, 16, 128)
    final_copies = []
    for i, to in enumerate(final_to):
        copy = remote(packed.at[to["z"], to["y"] // 2], final_in.at[here["z"], yh], final_s.at[i], final_r.at[i], to)
        copy.start()
        final_copies.append(copy)
    final_in[here["z"], yh] = packed[here["z"], yh]
    for copy in final_copies:
        copy.wait_recv()
    for f in range(8):
        block = final_in[f // 2, f % 2].astype(F32)
        both = [jnp.concatenate([block[t * 7 + k : t * 7 + k + 1, :] for k in range(7)], axis=1) for t in range(2)]
        out_ref[:, f * BLK : (f + 1) * BLK] = jnp.concatenate(both, axis=0).astype(BF16)
    for copy in final_copies:
        copy.wait_send()
    for give in gives:
        give.wait_send()
    for copy in sent:
        copy.wait_send()
    dense.end()
    routed.end()


def layer_scratch(products):
    dma = pltpu.SemaphoreType.DMA
    widths = [width for _, width, _ in PORTIONS]
    return (
        [
            pltpu.VMEM((4, 4, 4, 16, BLK), BF16),
            pltpu.VMEM((4, 4, 4, 16, BLK), BF16),
            pltpu.VMEM(products, F32),
            pltpu.VMEM((128, 128), F32),
        ]
        + [pltpu.VMEM((3, 4, 4, 16, width), BF16) for width in widths]
        + [pltpu.VMEM((4, 4, 16, width), BF16) for width in widths]
        + [pltpu.VMEM((15, 16, width), BF16) for width in widths]
        + [dma((3, 15)), dma((3, 15)), dma((3, 4, 3)), dma((3, 4, 3)), dma((3, 4, 3)), dma((3, 4, 3)), dma((3, 15)), dma((3, 15))]
    )


def layer(lengths, latent, hidden, ids, gain1, gain2, w_router, queries, cache, w_values, w_out, dense, expert):
    any_space = pl.BlockSpec(memory_space=pl.ANY)
    vmem = pl.BlockSpec(memory_space=pltpu.VMEM)
    dma = pltpu.SemaphoreType.DMA
    n1, n2 = dense[2].shape[0], expert[2].shape[0]
    return pl.pallas_call(
        layer_kernel,
        out_shape=jax.ShapeDtypeStruct((2, D), BF16),
        in_specs=[pl.BlockSpec(memory_space=pltpu.SMEM)] + [vmem] * 6 + [any_space] * 10,
        out_specs=vmem,
        scratch_shapes=[
            pltpu.VMEM((4 * n1, D), BF16),
            pltpu.VMEM((2 * n1, D), BF16),
            pltpu.VMEM((4, D, n2), BF16),
            pltpu.VMEM((2 * n2, D), BF16),
            pltpu.VMEM((16, BLK), F32),
            pltpu.VMEM((256, 128), BF16),
            pltpu.VMEM((16, BLK), F32),
            pltpu.VMEM((128, 16), F32),
            pltpu.VMEM((16, BLK), BF16),
            pltpu.VMEM((4, 2, 16, 128), BF16),
            pltpu.VMEM((4, 2, 16, 128), BF16),
            dma((6,)), dma((6,)), dma((6,)), dma((7,)), dma((7,)),
        ]
        + attention_scratch()
        + layer_scratch((4 * n1, 128))
        + layer_scratch((128, 4 * n2)),
        compiler_params=pltpu.CompilerParams(collective_id=0, has_side_effects=True, vmem_limit_bytes=VMEM_LIMIT),
        name="decode_layer",
    )(
        lengths, latent, hidden, ids, gain1, gain2, w_router, queries, cache, w_values, w_out, *dense, *expert
    )


def body(
    hidden,
    queries,
    cache,
    new_latent,
    lengths,
    w_values,
    w_out,
    gain_attn,
    w_dense_gate,
    w_dense_up,
    w_dense_down,
    gain_moe,
    w_router,
    expert_ids,
    w_expert_gate,
    w_expert_up,
    w_expert_down,
):
    out = layer(
        lengths,
        new_latent,
        hidden,
        expert_ids,
        gain_attn.reshape(1, D),
        gain_moe.reshape(1, D),
        w_router.T,
        jnp.swapaxes(queries, 1, 2),
        jnp.swapaxes(cache, 1, 2),
        w_values,
        jnp.swapaxes(w_out, 1, 2),
        (w_dense_gate.T, w_dense_up.T, w_dense_down),
        (w_expert_gate[0], w_expert_up[0], w_expert_down[0]),
    )
    return out


def solution(mesh):
    in_specs = (
        P(("tp", "ep"), None),
        P(("tp", "ep"), None, None),
        P(("tp", "ep"), None, None),
        P(("tp", "ep"), None),
        P(("tp", "ep")),
        P("tp", None, None),
        P("tp", None, "ep"),
        P(),
        P(None, ("tp", "ep")),
        P(None, ("tp", "ep")),
        P(("tp", "ep"), None),
        P(),
        P(),
        P(("tp", "ep"), None),
        P("ep", None, "tp"),
        P("ep", None, "tp"),
        P("ep", "tp", None),
    )
    out_specs = P(("tp", "ep"), None)
    return jax.shard_map(body, mesh=mesh, in_specs=in_specs, out_specs=out_specs, check_vma=False)
```
